128 devices in a mesh: dp: 16 (over y_hi, z, core), mp: 8 (over y_lo, x).
Axes of the slice: x: 4, y: 4 (y_hi: 2, y_lo: 2; y = y_hi * 2 + y_lo), z: 4, core: 2. Of those that a mesh axis runs over, the one named last changes fastest.
Arguments:
- tokens: bfloat16 [17408, 2048], P(('dp', 'mp')), may hold values from -6 to 6
- lengths: int32 [16, 3], P('dp'), may hold values from 1 to 512, 832 in all within a row
- place: int32 [32], replicated, may hold values from 0 to 31, each once
- attn_gain: float32 [2048], replicated, may hold values from 0.5 to 1.5
- w_query: bfloat16 [2048, 2048], P(None, 'mp'), may hold values from -0.125 to 0.125
- w_key: bfloat16 [2048, 512], P(None, 'mp'), may hold values from -0.125 to 0.125
- w_value: bfloat16 [2048, 512], P(None, 'mp'), may hold values from -0.125 to 0.125
- w_out: bfloat16 [2048, 2048], P('mp'), may hold values from -1.5 to 1.5
- mlp_gain: float32 [2048], replicated, may hold values from 0.5 to 1.5
- w_gate: bfloat16 [2048, 8192], P(None, 'mp'), may hold values from -0.125 to 0.125
- w_up: bfloat16 [2048, 8192], P(None, 'mp'), may hold values from -0.125 to 0.125
- w_down: bfloat16 [8192, 2048], P('mp'), may hold values from -0.0625 to 0.0625
- out_grad: bfloat16 [17408, 2048], P(('dp', 'mp')), may hold values from -6 to 6
Outputs:
- output: bfloat16 [17408, 2048], P(('dp', 'mp'))
- tokens_grad: bfloat16 [17408, 2048], P(('dp', 'mp'))
- attn_gain_grad: float32 [2048], replicated
- w_query_grad: float32 [2048, 2048], P('dp', 'mp')
- w_key_grad: float32 [2048, 512], P('dp', 'mp')
- w_value_grad: float32 [2048, 512], P('dp', 'mp')
- w_out_grad: float32 [2048, 2048], P('mp', 'dp')
- mlp_gain_grad: float32 [2048], replicated
- w_gate_grad: float32 [2048, 8192], P('dp', 'mp')
- w_up_grad: float32 [2048, 8192], P('dp', 'mp')
- w_down_grad: float32 [8192, 2048], P('mp', 'dp')
The draws below stay inside these ranges and needn't reach their ends.
Inputs may be any that keep to these rules, and one draw needn't show every extreme that they name: Row g holds, in order, the lengths of the short sequences packed in dp group g after its long-sequence rows; each row sums to 832 and its largest entry is 512. A permutation; dp group g holds half-blocks place[2 * g] and place[2 * g + 1] of the long sequence, in that order.
All inputs are finite; a program needn't handle non-finite values.
Results may differ from the reference program's by a relative error of at most 0.025.
Values may be sent and summed in bfloat16 or wider, within the bound.
No kernel may reach another device: no remote copies, remote signals or barrier semaphores. Data moves between devices by JAX's collectives and lax.ppermute only.
A program may use at most 256 MiB of HBM per device.

```python
import math
import jax
import jax.numpy as jnp
import numpy as np
from jax import lax

D = 2048
HEADS = 32
KV_HEADS = 8
HEAD_DIM = 64
FF = 8192
HALF = 128
PACK = 832
SHORT_MOST = 512
SEQS = 3
GROUP = 1088
LONG = 4096
TOKENS = 17408
N_DP = 16


def block_levels(key, extent, split, least, largest):
    level, own = 1.0, jax.random.fold_in(key, 6)
    for axis_at, parts in split:
        heights = jnp.exp(jax.random.uniform(jax.random.fold_in(own, axis_at), (parts,), jnp.float32, least / len(split), largest / len(split)))
        level = level * jnp.repeat(heights, extent[axis_at] // parts).reshape([-1 if axis == axis_at else 1 for axis in range(len(extent))])
    return level


def profile(number_of, total, limit, slope):
    portions = [(1 << 20) // math.isqrt(standing ** slope) + 1 for standing in range(2, number_of + 1)]
    rest, holding = total - limit - (number_of - 1), [1] * (number_of - 1)
    while rest > 0:
        free = [i for i in range(number_of - 1) if holding[i] < limit]
        whole, left = sum([portions[i] for i in free]), rest
        for i in free:
            more = min(limit - holding[i], max(1, left * portions[i] // whole), rest)
            holding[i] = holding[i] + more
            rest = rest - more
    return np.array([limit] + holding)


def ragged(key, count, total, limit, skew):
    if count == 2:
        one = jax.random.randint(key, (), max(1, total - limit), min(limit, total - 1) + 1)
        return jnp.stack([one, total - one])
    sizes = jnp.asarray(profile(count, total, limit, skew), jnp.int32)
    twos = (count - 1) // 2
    giver, taker = sizes[1:1 + 2 * twos:2], sizes[2:2 + 2 * twos:2]
    room = jnp.minimum(giver - 1, limit - taker)
    moved = jax.random.randint(jax.random.fold_in(key, 1), (twos,), 0, 1 << 20) % (room + 1)
    sizes = sizes.at[1:1 + 2 * twos:2].set(giver - moved).at[2:2 + 2 * twos:2].set(taker + moved)
    return sizes[jax.random.permutation(jax.random.fold_in(key, 2), count)]


def centred(rng, extent, scale, most, shards=(), kind=jnp.bfloat16):
    factor_of = block_levels(rng, extent, shards, -0.22, 0.18) if shards else 1.0
    array = jax.random.normal(rng, extent, jnp.float32) * scale * factor_of
    return jnp.minimum(jnp.maximum(array, -most), most).astype(kind)


def setup_inputs(seed: int = 0) -> dict:
    key_list = jax.random.split(jax.random.key(seed), 14)
    return {
        "tokens": centred(key_list[0], (TOKENS, D), 1.0, 6.0, ((0, 128),)),
        "lengths": jax.vmap(lambda own: ragged(own, SEQS, PACK, SHORT_MOST, 2))(jax.random.split(key_list[1], N_DP)).reshape((N_DP, SEQS)).astype(jnp.int32),
        "place": jax.random.permutation(key_list[2], 2 * N_DP).astype(jnp.int32),
        "attn_gain": jnp.clip(1.0 + 0.1 * jax.random.normal(key_list[3], (D,), jnp.float32), 0.5, 1.5),
        "w_query": centred(key_list[4], (D, HEADS * HEAD_DIM), D ** -0.5, 0.125, ((1, 8),)),
        "w_key": centred(key_list[5], (D, KV_HEADS * HEAD_DIM), D ** -0.5, 0.125, ((1, 8),)),
        "w_value": centred(key_list[6], (D, KV_HEADS * HEAD_DIM), D ** -0.5, 0.125, ((1, 8),)),
        "w_out": centred(key_list[7], (HEADS * HEAD_DIM, D), 16 ** -0.5, 1.5, ((0, 8),)),
        "mlp_gain": jnp.clip(1.0 + 0.1 * jax.random.normal(key_list[8], (D,), jnp.float32), 0.5, 1.5),
        "w_gate": centred(key_list[9], (D, FF), D ** -0.5, 0.125, ((1, 8),)),
        "w_up": centred(key_list[10], (D, FF), D ** -0.5, 0.125, ((1, 8),)),
        "w_down": centred(key_list[11], (FF, D), FF ** -0.5, 0.0625, ((0, 8),)),
        "out_grad": centred(key_list[12], (TOKENS, D), 1.0, 6.0, ((0, 128),)),
    }


EPS = 1e-05
THETA = 500000.0
MASKED = -1e+30
HIGHEST = lax.Precision.HIGHEST

@jax.custom_vjp
def low(v):
    return lax.optimization_barrier(v.astype(jnp.bfloat16)).astype(jnp.float32)

@jax.custom_vjp
def low_back(v):
    return v

def low_keep(v):
    return (low(v), None)

def low_pass(kept, grad):
    return (grad,)

def back_keep(v):
    return (v, None)

def back_low(kept, grad):
    return (low(grad),)
low.defvjp(low_keep, low_pass)
low_back.defvjp(back_keep, back_low)

def inverse_freq(head_width):
    indices = jnp.arange(head_width // 2, dtype=jnp.float32)
    base_freq = jnp.exp(-jnp.log(THETA) * 2.0 * indices / head_width)
    wavelength = 2.0 * jnp.pi / base_freq
    smooth = (8192.0 / wavelength - 1.0) / 3.0
    blended = (1.0 - smooth) * base_freq / 32.0 + smooth * base_freq
    return jnp.where(wavelength < 2048.0, base_freq, jnp.where(wavelength > 8192.0, base_freq / 32.0, blended))

def tables(positions, head_width):
    angles = positions.astype(jnp.float32)[:, None] * inverse_freq(head_width)[None, :]
    return (jnp.cos(angles)[:, None, :], jnp.sin(angles)[:, None, :])

def rotate(values, cos_table, sin_table):
    half_dim = values.shape[-1] // 2
    first_half = values[..., :half_dim]
    second_half = values[..., half_dim:]
    return jnp.concatenate([first_half * cos_table - second_half * sin_table, second_half * cos_table + first_half * sin_table], axis=-1)

def pack_layout(seq_lengths, pack_rows):
    pack_index = jnp.arange(pack_rows, dtype=jnp.int32)
    seq_ends = jnp.cumsum(seq_lengths).astype(jnp.int32)
    seq_starts = (seq_ends - seq_lengths).astype(jnp.int32)
    member = (pack_index[:, None] >= seq_starts[None, :]) & (pack_index[:, None] < seq_ends[None, :])
    seq_ids = jnp.arange(seq_lengths.shape[0], dtype=jnp.int32)
    segment = lax.optimization_barrier(jnp.sum(jnp.where(member, seq_ids[None, :], 0), axis=1)).astype(jnp.int32)
    offset = lax.optimization_barrier(jnp.sum(jnp.where(member, seq_starts[None, :], 0), axis=1)).astype(jnp.int32)
    return ((pack_index - offset).astype(jnp.int32), segment)

def matmul(left, right):
    return jnp.dot(left, right, precision=HIGHEST)

def rms_norm(values, gain):
    inv_rms = lax.rsqrt(lax.optimization_barrier(jnp.mean(values * values, axis=-1, keepdims=True)) + EPS)
    return values * inv_rms * gain

def attend(queries, key_rows, value_rows, visible):
    score_scale = queries.shape[-1] ** (-0.5)
    scores = jnp.einsum('rkgd,ckd->kgrc', queries, key_rows, precision=HIGHEST) * score_scale
    scores = low_back(scores)
    scores = jnp.where(visible[None, None], scores, MASKED)
    row_max = lax.optimization_barrier(jnp.max(scores, axis=-1, keepdims=True))
    exp_scores = jnp.exp(scores - row_max)
    attn_probs = low(exp_scores / lax.optimization_barrier(jnp.sum(exp_scores, axis=-1, keepdims=True)))
    return jnp.einsum('kgrc,ckd->rkgd', attn_probs, value_rows, precision=HIGHEST)

def reference(tokens, lengths, place, attn_gain, w_query, w_key, w_value, w_out, mlp_gain, w_gate, w_up, w_down, out_grad):
    kv_group = HEADS // KV_HEADS
    attn_width = HEADS * HEAD_DIM
    long_local = jnp.arange(2 * HALF, dtype=jnp.int32)
    place_pairs = place.reshape(N_DP, 2)
    long_pos = jnp.where(long_local[None, :] < HALF, place_pairs[:, :1], place_pairs[:, 1:]) * HALF + long_local[None, :] % HALF
    short_pos, segments = jax.vmap(lambda seq_lengths: pack_layout(seq_lengths, PACK))(lengths)
    positions = jnp.concatenate([long_pos.astype(jnp.int32), short_pos], axis=1).reshape(TOKENS)
    cos_table, sin_table = tables(positions, HEAD_DIM)
    half_ids = jnp.arange(2 * N_DP, dtype=jnp.int32)
    half_owner = jnp.zeros((2 * N_DP,), jnp.int32).at[place].set(half_ids)
    half_start = half_owner // 2 * GROUP + half_owner % 2 * HALF
    long_order = jnp.arange(LONG, dtype=jnp.int32)
    long_index = (half_start[long_order // HALF] + long_order % HALF).astype(jnp.int32)
    pack_index = jnp.arange(PACK, dtype=jnp.int32)
    short_index = (jnp.arange(N_DP, dtype=jnp.int32)[:, None] * GROUP + 2 * HALF + pack_index[None, :]).astype(jnp.int32)
    causal_pack = pack_index[:, None] >= pack_index[None, :]
    short_visible = (segments[:, :, None] == segments[:, None, :]) & causal_pack[None]
    block_rows = min(512, LONG)
    block_count = LONG // block_rows
    key_positions = jnp.arange(LONG, dtype=jnp.int32)

    def forward(residual, gain_one, query_weight, key_weight, value_weight, out_weight, gain_two, gate_weight, up_weight, down_weight):
        hidden_in = low(rms_norm(residual, gain_one))
        query_raw = low_back(matmul(hidden_in, query_weight)).reshape(TOKENS, HEADS, HEAD_DIM)
        key_raw = low_back(matmul(hidden_in, key_weight)).reshape(TOKENS, KV_HEADS, HEAD_DIM)
        value_all = low(low_back(matmul(hidden_in, value_weight))).reshape(TOKENS, KV_HEADS, HEAD_DIM)
        query_all = low(rotate(query_raw, cos_table, sin_table)).reshape(TOKENS, KV_HEADS, kv_group, HEAD_DIM)
        key_all = low(rotate(key_raw, cos_table, sin_table))
        long_keys = key_all[long_index]
        long_values = value_all[long_index]
        long_queries = query_all[long_index].reshape(block_count, block_rows, KV_HEADS, kv_group, HEAD_DIM)

        def long_block(operands):
            query_block, first_row = operands
            query_positions = first_row + jnp.arange(block_rows, dtype=jnp.int32)
            visible = query_positions[:, None] >= key_positions[None, :]
            return attend(query_block, long_keys, long_values, visible)

        def short_group(operands):
            return attend(operands[0], operands[1], operands[2], operands[3])
        block_starts = jnp.arange(block_count, dtype=jnp.int32) * block_rows
        long_out = lax.map(jax.checkpoint(long_block), (long_queries, block_starts))
        short_out = lax.map(jax.checkpoint(short_group), (query_all[short_index], key_all[short_index], value_all[short_index], short_visible))
        attn_out = jnp.zeros((TOKENS, attn_width), jnp.float32)
        attn_out = attn_out.at[long_index].set(long_out.reshape(LONG, attn_width))
        attn_out = attn_out.at[short_index.reshape(-1)].set(short_out.reshape(N_DP * PACK, attn_width))
        attn_cast = low(low_back(attn_out))
        mixed = residual + low_back(matmul(attn_cast, out_weight))
        hidden_two = low(rms_norm(mixed, gain_two))

        def mlp_group(row_block):
            gate_proj = low_back(matmul(row_block, gate_weight))
            up_proj = low_back(matmul(row_block, up_weight))
            return low_back(matmul(low(jax.nn.silu(gate_proj) * up_proj), down_weight))
        mlp_out = lax.map(jax.checkpoint(mlp_group), hidden_two.reshape(N_DP, GROUP, D))
        return mixed + mlp_out.reshape(TOKENS, D)
    floats = (tokens.astype(jnp.float32), attn_gain.astype(jnp.float32), w_query.astype(jnp.float32), w_key.astype(jnp.float32), w_value.astype(jnp.float32), w_out.astype(jnp.float32), mlp_gain.astype(jnp.float32), w_gate.astype(jnp.float32), w_up.astype(jnp.float32), w_down.astype(jnp.float32))
    result, pullback = jax.vjp(forward, *floats)
    gradients = pullback(out_grad.astype(jnp.float32))
    return (result.astype(jnp.bfloat16), gradients[0].astype(jnp.bfloat16), gradients[1], gradients[2], gradients[3], gradients[4], gradients[5], gradients[6], gradients[7], gradients[8], gradients[9])
```

```python
import jax
import jax.numpy as jnp
from jax import lax
from jax.sharding import PartitionSpec as P

HEAD_DIM = 64
HALF = 128


EPS = 1e-05
THETA = 500000.0
MASKED = -1e30

BOTH = ("dp", "mp")


def place_of(yh, z, c, yl, x):
    return ((yh * 4 + z) * 2 + c) * 8 + yl * 4 + x


def pairs_of(target, sender=lambda yh, z, c, yl, x: True):
    return [
        (place_of(yh, z, c, yl, x), place_of(*target(yh, z, c, yl, x)))
        for yh in range(2)
        for z in range(4)
        for c in range(2)
        for yl in range(2)
        for x in range(4)
        if sender(yh, z, c, yl, x)
    ]


X_UP = pairs_of(lambda yh, z, c, yl, x: (yh, z, c, yl, (x + 1) % 4))
X_DOWN = pairs_of(lambda yh, z, c, yl, x: (yh, z, c, yl, (x + 3) % 4))
X_FAR = pairs_of(lambda yh, z, c, yl, x: (yh, z, c, yl, (x + 2) % 4))
Z_UP = pairs_of(lambda yh, z, c, yl, x: (yh, (z + 1) % 4, c, yl, x))
Z_DOWN = pairs_of(lambda yh, z, c, yl, x: (yh, (z + 3) % 4, c, yl, x))
Z_FAR = pairs_of(lambda yh, z, c, yl, x: (yh, (z + 2) % 4, c, yl, x))
CORE = pairs_of(lambda yh, z, c, yl, x: (yh, z, 1 - c, yl, x))
Y_LOW = pairs_of(lambda yh, z, c, yl, x: (yh, z, c, 1 - yl, x))
Y_HIGH = pairs_of(lambda yh, z, c, yl, x: (1 - yh, z, c, 1 - yl, x))
Y_FAR = pairs_of(lambda yh, z, c, yl, x: (1 - yh, z, c, yl, x))
TURN = pairs_of(lambda yh, z, c, yl, x: (yh, z, yl, c, x))
NATIVE = lambda yh, z, c, yl, x: c == yl
FOREIGN = lambda yh, z, c, yl, x: c != yl
FOREIGN_LOW = pairs_of(lambda yh, z, c, yl, x: (yh, z, c, 1 - yl, x), FOREIGN)
FOREIGN_HIGH = pairs_of(lambda yh, z, c, yl, x: (1 - yh, z, c, 1 - yl, x), FOREIGN)
NATIVE_FAR = pairs_of(lambda yh, z, c, yl, x: (1 - yh, z, c, yl, x), NATIVE)
NATIVE_CORE = pairs_of(lambda yh, z, c, yl, x: (yh, z, 1 - c, yl, x), NATIVE)
WEIGHT_LOW = pairs_of(
    lambda yh, z, c, yl, x: (yh, z, c, 1 - yl, x) if c == yl else (yh, z, 1 - c, yl, x)
)
WEIGHT_HIGH = pairs_of(
    lambda yh, z, c, yl, x: (1 - yh, z, c, 1 - yl, x) if c == yl else (yh, z, 1 - c, yl, x)
)
Z_GROUPS = [
    [place_of(yh, z, c, yl, x) for z in range(4)]
    for yh in range(2)
    for c in range(2)
    for yl in range(2)
    for x in range(4)
]


def send(values, pairs):
    return lax.ppermute(values, BOTH, pairs)


def gather(rows):
    own = jnp.concatenate([rows, send(rows, X_DOWN), send(rows, X_FAR), send(rows, X_UP)])
    return (own, send(own, CORE))


def scatter(own, other):
    total = (own.astype(jnp.float32) + send(other, CORE).astype(jnp.float32)).astype(jnp.bfloat16)
    rows = total.shape[0] // 4
    part = [total[k * rows : (k + 1) * rows] for k in range(4)]
    one, two, three = send(part[1], X_UP), send(part[2], X_FAR), send(part[3], X_DOWN)
    return (part[0].astype(jnp.float32) + one.astype(jnp.float32)) + (
        two.astype(jnp.float32) + three.astype(jnp.float32)
    )


def in_order(values, core, x):
    half = values.shape[0] // 2
    rows = half // 4
    first = lax.dynamic_slice_in_dim(
        jnp.concatenate([values[:half], values[:half]]), (4 - x) % 4 * rows, half
    )
    second = lax.dynamic_slice_in_dim(
        jnp.concatenate([values[half:], values[half:]]), (4 - x) % 4 * rows, half
    )
    return jnp.concatenate(
        [jnp.where(core == 0, first, second), jnp.where(core == 0, second, first)]
    )


def from_order(values, core, x):
    half = values.shape[0] // 2
    rows = half // 4
    own = jnp.where(core == 0, values[:half], values[half:])
    other = jnp.where(core == 0, values[half:], values[:half])
    return (
        lax.dynamic_slice_in_dim(jnp.concatenate([own, own]), x * rows, half),
        lax.dynamic_slice_in_dim(jnp.concatenate([other, other]), x * rows, half),
    )


def sum_groups(grad, yh, core, native):
    width = grad.shape[1]
    ordered = grad.reshape(2, 4, 2, -1, width).transpose(1, 0, 2, 3, 4).reshape(-1, width)
    kept = lax.psum_scatter(
        ordered, BOTH, scatter_dimension=0, tiled=True, axis_index_groups=Z_GROUPS
    ).reshape(2, -1, width)
    near = jnp.where(yh == 0, kept[0], kept[1])
    far = jnp.where(yh == 0, kept[1], kept[0])
    low = send(near, FOREIGN_LOW)
    high = send(far, FOREIGN_HIGH)
    across = send(far, NATIVE_FAR)
    total = (near.astype(jnp.float32) + low.astype(jnp.float32)) + (
        high.astype(jnp.float32) + across.astype(jnp.float32)
    )
    rows = total.shape[0] // 2
    mine = jnp.where(core == 0, total[:rows], total[rows:])
    theirs = jnp.where(core == 0, total[rows:], total[:rows])
    passed = send(theirs.astype(jnp.bfloat16), NATIVE_CORE).astype(jnp.float32)
    return jnp.where(native, mine, passed)


def inverse_freq(head_width):
    indices = jnp.arange(head_width // 2, dtype=jnp.float32)
    base_freq = jnp.exp(-jnp.log(THETA) * 2.0 * indices / head_width)
    wavelength = 2.0 * jnp.pi / base_freq
    smooth = (8192.0 / wavelength - 1.0) / 3.0
    blended = (1.0 - smooth) * base_freq / 32.0 + smooth * base_freq
    return jnp.where(
        wavelength < 2048.0, base_freq, jnp.where(wavelength > 8192.0, base_freq / 32.0, blended)
    )


def tables(positions, head_width):
    angles = positions.astype(jnp.float32)[:, None] * inverse_freq(head_width)[None, :]
    return (jnp.cos(angles)[:, None, :], jnp.sin(angles)[:, None, :])


def rotate(values, cos_table, sin_table):
    half_dim = values.shape[-1] // 2
    first_half = values[..., :half_dim]
    second_half = values[..., half_dim:]
    return jnp.concatenate(
        [
            first_half * cos_table - second_half * sin_table,
            second_half * cos_table + first_half * sin_table,
        ],
        axis=-1,
    )


def pack_layout(seq_lengths, pack_rows):
    pack_index = jnp.arange(pack_rows, dtype=jnp.int32)
    seq_ends = jnp.cumsum(seq_lengths)
    seq_starts = seq_ends - seq_lengths
    member = (pack_index[:, None] >= seq_starts[None, :]) & (
        pack_index[:, None] < seq_ends[None, :]
    )
    seq_ids = jnp.arange(seq_lengths.shape[0], dtype=jnp.int32)
    segment = jnp.sum(jnp.where(member, seq_ids[None, :], 0), axis=1)
    offset = jnp.sum(jnp.where(member, seq_starts[None, :], 0), axis=1)
    return (pack_index - offset, segment)


def contract(left, right, left_dim, right_dim):
    return lax.dot_general(
        left, right, (((left_dim,), (right_dim,)), ((), ())), preferred_element_type=jnp.float32
    )


def attend_forward(queries, key_rows, value_rows, visible):
    score_scale = queries.shape[-1] ** (-0.5)
    scores = (
        jnp.einsum("rkgd,ckd->kgrc", queries, key_rows, preferred_element_type=jnp.float32)
        * score_scale
    )
    scores = jnp.where(visible[None, None], scores, MASKED)
    row_max = jnp.max(scores, axis=-1, keepdims=True)
    exp_scores = jnp.exp(scores - row_max)
    attn_probs = exp_scores / jnp.sum(exp_scores, axis=-1, keepdims=True)
    probs_low = attn_probs.astype(jnp.bfloat16)
    attn_rows = jnp.einsum(
        "kgrc,ckd->rkgd", probs_low, value_rows, preferred_element_type=jnp.float32
    )
    return (attn_rows, attn_probs, probs_low)


def attend_backward(queries, key_rows, value_rows, attn_probs, probs_low, grad_rows):
    score_scale = queries.shape[-1] ** (-0.5)
    grad_probs = jnp.einsum(
        "rkgd,ckd->kgrc", grad_rows, value_rows, preferred_element_type=jnp.float32
    )
    grad_values = jnp.einsum(
        "kgrc,rkgd->ckd", probs_low, grad_rows, preferred_element_type=jnp.float32
    )
    grad_scores = attn_probs * (
        grad_probs - jnp.sum(attn_probs * grad_probs, axis=-1, keepdims=True)
    )
    scores_low = grad_scores.astype(jnp.bfloat16)
    grad_queries = (
        jnp.einsum("kgrc,ckd->rkgd", scores_low, key_rows, preferred_element_type=jnp.float32)
        * score_scale
    )
    grad_keys = (
        jnp.einsum("kgrc,rkgd->ckd", scores_low, queries, preferred_element_type=jnp.float32)
        * score_scale
    )
    return (grad_queries, grad_keys, grad_values)


def norm_back(grad_in, unit_rows, inv_rms, gain):
    scaled = grad_in * gain
    return inv_rms * (scaled - unit_rows * jnp.mean(scaled * unit_rows, axis=-1, keepdims=True))


def all_sum(values):
    for group in ((CORE,), (X_UP, X_DOWN, X_FAR), (Z_UP, Z_DOWN, Z_FAR), (Y_LOW, Y_HIGH, Y_FAR)):
        values = sum([send(values, pairs) for pairs in group], values)
    return values


def local(
    tokens,
    lengths,
    place,
    attn_gain,
    w_query,
    w_key,
    w_value,
    w_out,
    mlp_gain,
    w_gate,
    w_up,
    w_down,
    out_grad,
):
    head_width = HEAD_DIM
    kv_local = w_key.shape[1] // head_width
    query_heads = w_query.shape[1] // head_width
    kv_group = query_heads // kv_local
    kv_width = kv_local * head_width
    attn_width = query_heads * head_width
    local_rows = tokens.shape[0]
    group_rows = local_rows * 8
    long_rows = 2 * HALF
    pack_rows = group_rows - long_rows
    dp_index, mp_index = lax.axis_index("dp"), lax.axis_index("mp")
    yh, z, core = dp_index // 8, dp_index // 2 % 4, dp_index % 2
    yl, x = mp_index // 4, mp_index % 4
    native = core == yl

    tokens = send(tokens, TURN)
    lengths = send(lengths, TURN)
    w_key, w_value = send(w_key, WEIGHT_HIGH), send(w_value, WEIGHT_HIGH)
    w_query = send(w_query, WEIGHT_LOW)
    w_out = send(w_out, WEIGHT_HIGH)
    w_gate = send(w_gate, WEIGHT_LOW)
    w_up = send(w_up, WEIGHT_HIGH)
    w_down = send(w_down, WEIGHT_LOW)
    out_grad = send(out_grad, TURN)

    long_local = jnp.arange(long_rows, dtype=jnp.int32)

    def place_at(index):
        return jnp.sum(jnp.where(jnp.arange(place.shape[0]) == index, place, 0))

    def long_positions(group):
        pair = (place_at(2 * group), place_at(2 * group + 1))
        return jnp.where(long_local < HALF, pair[0], pair[1]) * HALF + long_local % HALF

    long_pos = long_positions((yh * 4 + z) * 2 + yl)
    far_pos = jnp.concatenate(
        [
            long_positions((gy * 4 + (z + step) % 4) * 2 + gl)
            for gy, gl in ((yh, yl), (yh, 1 - yl), (1 - yh, 1 - yl), (1 - yh, yl))
            for step in range(4)
        ]
    )
    short_pos, segment = pack_layout(lengths[0], pack_rows)
    positions = jnp.concatenate([long_pos, short_pos])
    cos_table, sin_table = tables(positions, head_width)
    long_visible = long_pos[:, None] >= far_pos[None, :]
    pack_index = jnp.arange(pack_rows, dtype=jnp.int32)
    short_visible = (segment[:, None] == segment[None, :]) & (
        pack_index[:, None] >= pack_index[None, :]
    )
    residual = tokens.astype(jnp.float32)
    inv_one = lax.rsqrt(jnp.mean(residual * residual, axis=-1, keepdims=True) + EPS)
    unit_one = residual * inv_one
    local_one = (unit_one * attn_gain).astype(jnp.bfloat16)
    hidden_own, hidden_other = gather(local_one)
    w_qkv = jnp.concatenate([w_query, w_key, w_value], axis=1)
    qkv = in_order(
        jnp.concatenate(
            [
                jnp.dot(hidden_own, w_qkv, preferred_element_type=jnp.float32),
                jnp.dot(hidden_other, w_qkv, preferred_element_type=jnp.float32),
            ]
        ),
        core,
        x,
    )
    query_raw = qkv[:, :attn_width].reshape(group_rows, query_heads, head_width)
    key_raw = qkv[:, attn_width : attn_width + kv_width].reshape(group_rows, kv_local, head_width)
    value_all = qkv[:, attn_width + kv_width :].astype(jnp.bfloat16)
    key_all = (
        rotate(key_raw, cos_table, sin_table).astype(jnp.bfloat16).reshape(group_rows, kv_width)
    )
    near_rows = jnp.concatenate([key_all[:long_rows], value_all[:long_rows]], axis=1)
    ring_rows = jnp.concatenate(
        [near_rows, send(near_rows, Z_DOWN), send(near_rows, Z_FAR), send(near_rows, Z_UP)]
    )
    far_rows = jnp.concatenate(
        [ring_rows, send(ring_rows, Y_LOW), send(ring_rows, Y_HIGH), send(ring_rows, Y_FAR)]
    )
    query_all = (
        rotate(query_raw, cos_table, sin_table)
        .astype(jnp.bfloat16)
        .reshape(group_rows, kv_local, kv_group, head_width)
    )
    far_keys = far_rows[:, :kv_width].reshape(-1, kv_local, head_width)
    far_values = far_rows[:, kv_width:].reshape(-1, kv_local, head_width)
    key_local = key_all.reshape(group_rows, kv_local, head_width)
    value_local = value_all.reshape(group_rows, kv_local, head_width)
    short_attn, short_probs, short_low = attend_forward(
        query_all[long_rows:], key_local[long_rows:], value_local[long_rows:], short_visible
    )
    long_attn, long_probs, long_low = attend_forward(
        query_all[:long_rows], far_keys, far_values, long_visible
    )
    attn_own, attn_other = from_order(
        jnp.concatenate([long_attn, short_attn])
        .reshape(group_rows, attn_width)
        .astype(jnp.bfloat16),
        core,
        x,
    )

    def project(left, right):
        return jnp.dot(left, right, preferred_element_type=jnp.float32).astype(jnp.bfloat16)

    mixed = residual + scatter(project(attn_own, w_out), project(attn_other, w_out))
    inv_two = lax.rsqrt(jnp.mean(mixed * mixed, axis=-1, keepdims=True) + EPS)
    unit_two = mixed * inv_two
    local_two = (unit_two * mlp_gain).astype(jnp.bfloat16)
    grad_rows = jnp.concatenate(gather(out_grad))
    grad_act = contract(grad_rows, w_down, 1, 1)
    hidden_two = jnp.concatenate(gather(local_two))
    gate_proj = jnp.dot(hidden_two, w_gate, preferred_element_type=jnp.float32)
    up_proj = jnp.dot(hidden_two, w_up, preferred_element_type=jnp.float32)
    gate_sig = jax.nn.sigmoid(gate_proj)
    gate_act = gate_proj * gate_sig
    act_low = (gate_act * up_proj).astype(jnp.bfloat16)
    grad_gate = (grad_act * up_proj * gate_sig * (1.0 + gate_proj * (1.0 - gate_sig))).astype(
        jnp.bfloat16
    )
    grad_up = (grad_act * gate_act).astype(jnp.bfloat16)
    half_rows = group_rows // 2
    grad_hidden = (contract(grad_gate, w_gate, 1, 1) + contract(grad_up, w_up, 1, 1)).astype(
        jnp.bfloat16
    )
    grad_two = scatter(grad_hidden[:half_rows], grad_hidden[half_rows:])
    down_part = contract(grad_rows, act_low, 0, 0).astype(jnp.bfloat16)
    gate_part = contract(hidden_two, grad_gate, 0, 0).astype(jnp.bfloat16)
    up_part = contract(hidden_two, grad_up, 0, 0).astype(jnp.bfloat16)
    down_sum = sum_groups(down_part, yh, core, native).T
    gate_sum = sum_groups(gate_part, yh, core, native)
    up_sum = sum_groups(up_part, yh, core, native)
    down_rows = project(act_low, w_down)
    output = mixed + scatter(down_rows[:half_rows], down_rows[half_rows:])
    output = send(output.astype(jnp.bfloat16), TURN)
    grad_mixed = out_grad.astype(jnp.float32) + norm_back(grad_two, unit_two, inv_two, mlp_gain)
    mixed_grad_rows = jnp.concatenate(gather(grad_mixed.astype(jnp.bfloat16)))
    mlp_gain_part = jnp.sum(grad_two * unit_two, axis=0)
    attn_rel = jnp.concatenate([attn_own, attn_other])
    out_part = contract(mixed_grad_rows, attn_rel, 0, 0).astype(jnp.bfloat16)
    out_sum = sum_groups(out_part, yh, core, native).T
    grad_attn = in_order(
        contract(mixed_grad_rows, w_out, 1, 1).astype(jnp.bfloat16), core, x
    ).reshape(group_rows, kv_local, kv_group, head_width)
    long_dq, long_dk, long_dv = attend_backward(
        query_all[:long_rows], far_keys, far_values, long_probs, long_low, grad_attn[:long_rows]
    )
    far_terms = jnp.concatenate(
        [long_dk.reshape(-1, kv_width), long_dv.reshape(-1, kv_width)], axis=1
    ).astype(jnp.bfloat16)
    ring = far_terms.reshape(4, 4 * long_rows, 2 * kv_width)
    ring_terms = (
        (ring[0].astype(jnp.float32) + send(ring[1], Y_LOW).astype(jnp.float32))
        + (send(ring[2], Y_HIGH).astype(jnp.float32) + send(ring[3], Y_FAR).astype(jnp.float32))
    ).astype(jnp.bfloat16)
    near = ring_terms.reshape(4, long_rows, 2 * kv_width)
    far_grads = (near[0].astype(jnp.float32) + send(near[1], Z_UP).astype(jnp.float32)) + (
        send(near[2], Z_FAR).astype(jnp.float32) + send(near[3], Z_DOWN).astype(jnp.float32)
    )
    short_dq, short_dk, short_dv = attend_backward(
        query_all[long_rows:],
        key_local[long_rows:],
        value_local[long_rows:],
        short_probs,
        short_low,
        grad_attn[long_rows:],
    )
    key_grad_all = jnp.concatenate(
        [far_grads[:, :kv_width], short_dk.reshape(pack_rows, kv_width)]
    ).reshape(group_rows, kv_local, head_width)
    value_low = jnp.concatenate(
        [far_grads[:, kv_width:], short_dv.reshape(pack_rows, kv_width)]
    ).astype(jnp.bfloat16)
    query_grad_all = jnp.concatenate([long_dq, short_dq]).reshape(
        group_rows, query_heads, head_width
    )
    query_low = (
        rotate(query_grad_all, cos_table, -sin_table)
        .reshape(group_rows, attn_width)
        .astype(jnp.bfloat16)
    )
    key_low = (
        rotate(key_grad_all, cos_table, -sin_table)
        .reshape(group_rows, kv_width)
        .astype(jnp.bfloat16)
    )
    low_own, low_other = from_order(
        jnp.concatenate([query_low, key_low, value_low], axis=1), core, x
    )
    grad_one = scatter(
        contract(low_own, w_qkv, 1, 1).astype(jnp.bfloat16),
        contract(low_other, w_qkv, 1, 1).astype(jnp.bfloat16),
    )
    qkv_part = (
        contract(hidden_own, low_own, 0, 0) + contract(hidden_other, low_other, 0, 0)
    ).astype(jnp.bfloat16)
    qkv_sum = sum_groups(qkv_part, yh, core, native)
    attn_gain_part = jnp.sum(grad_one * unit_one, axis=0)
    grad_tokens = grad_mixed + norm_back(grad_one, unit_one, inv_one, attn_gain)
    grad_tokens = send(grad_tokens.astype(jnp.bfloat16), TURN)
    gains = all_sum(jnp.stack([attn_gain_part, mlp_gain_part]))
    return (
        output,
        grad_tokens,
        gains[0],
        qkv_sum[:, :attn_width],
        qkv_sum[:, attn_width : attn_width + kv_width],
        qkv_sum[:, attn_width + kv_width :],
        out_sum,
        gains[1],
        gate_sum,
        up_sum,
        down_sum,
    )


def solution(mesh):
    placed = (
        P(("dp", "mp"), None),
        P("dp", None),
        P(),
        P(),
        P(None, "mp"),
        P(None, "mp"),
        P(None, "mp"),
        P("mp", None),
        P(),
        P(None, "mp"),
        P(None, "mp"),
        P("mp", None),
        P(("dp", "mp"), None),
    )
    return jax.shard_map(
        local,
        mesh=mesh,
        in_specs=placed,
        out_specs=(
            P(("dp", "mp"), None),
            P(("dp", "mp"), None),
            P(),
            P("dp", "mp"),
            P("dp", "mp"),
            P("dp", "mp"),
            P("mp", "dp"),
            P(),
            P("dp", "mp"),
            P("dp", "mp"),
            P("mp", "dp"),
        ),
        check_vma=False,
    )
```

```python
import jax
import jax.numpy as jnp
from jax import lax
from jax.experimental import pallas as pl
from jax.experimental.pallas import tpu as pltpu
from jax.sharding import PartitionSpec as P

HEAD_DIM = 64
HALF = 128
MASKED = -1e30


EPS = 1e-05
THETA = 500000.0

BOTH = ("dp", "mp")


def place_of(yh, z, c, yl, x):
    return ((yh * 4 + z) * 2 + c) * 8 + yl * 4 + x


def pairs_of(target, sender=lambda yh, z, c, yl, x: True):
    return [
        (place_of(yh, z, c, yl, x), place_of(*target(yh, z, c, yl, x)))
        for yh in range(2)
        for z in range(4)
        for c in range(2)
        for yl in range(2)
        for x in range(4)
        if sender(yh, z, c, yl, x)
    ]


X_UP = pairs_of(lambda yh, z, c, yl, x: (yh, z, c, yl, (x + 1) % 4))
X_DOWN = pairs_of(lambda yh, z, c, yl, x: (yh, z, c, yl, (x + 3) % 4))
X_FAR = pairs_of(lambda yh, z, c, yl, x: (yh, z, c, yl, (x + 2) % 4))
Z_UP = pairs_of(lambda yh, z, c, yl, x: (yh, (z + 1) % 4, c, yl, x))
Z_DOWN = pairs_of(lambda yh, z, c, yl, x: (yh, (z + 3) % 4, c, yl, x))
Z_FAR = pairs_of(lambda yh, z, c, yl, x: (yh, (z + 2) % 4, c, yl, x))
CORE = pairs_of(lambda yh, z, c, yl, x: (yh, z, 1 - c, yl, x))
Y_LOW = pairs_of(lambda yh, z, c, yl, x: (yh, z, c, 1 - yl, x))
Y_HIGH = pairs_of(lambda yh, z, c, yl, x: (1 - yh, z, c, 1 - yl, x))
Y_FAR = pairs_of(lambda yh, z, c, yl, x: (1 - yh, z, c, yl, x))
TURN = pairs_of(lambda yh, z, c, yl, x: (yh, z, yl, c, x))
NATIVE = lambda yh, z, c, yl, x: c == yl
FOREIGN = lambda yh, z, c, yl, x: c != yl
FOREIGN_LOW = pairs_of(lambda yh, z, c, yl, x: (yh, z, c, 1 - yl, x), FOREIGN)
FOREIGN_HIGH = pairs_of(lambda yh, z, c, yl, x: (1 - yh, z, c, 1 - yl, x), FOREIGN)
NATIVE_FAR = pairs_of(lambda yh, z, c, yl, x: (1 - yh, z, c, yl, x), NATIVE)
NATIVE_CORE = pairs_of(lambda yh, z, c, yl, x: (yh, z, 1 - c, yl, x), NATIVE)
WEIGHT_LOW = pairs_of(
    lambda yh, z, c, yl, x: (yh, z, c, 1 - yl, x) if c == yl else (yh, z, 1 - c, yl, x)
)
WEIGHT_HIGH = pairs_of(
    lambda yh, z, c, yl, x: (1 - yh, z, c, 1 - yl, x) if c == yl else (yh, z, 1 - c, yl, x)
)
Z_GROUPS = [
    [place_of(yh, z, c, yl, x) for z in range(4)]
    for yh in range(2)
    for c in range(2)
    for yl in range(2)
    for x in range(4)
]


def send(values, pairs):
    return lax.ppermute(values, BOTH, pairs)


def gather(rows):
    own = jnp.concatenate([rows, send(rows, X_DOWN), send(rows, X_FAR), send(rows, X_UP)])
    return (own, send(own, CORE))


def scatter(own, other):
    total = (own.astype(jnp.float32) + send(other, CORE).astype(jnp.float32)).astype(jnp.bfloat16)
    rows = total.shape[0] // 4
    part = [total[k * rows : (k + 1) * rows] for k in range(4)]
    one, two, three = send(part[1], X_UP), send(part[2], X_FAR), send(part[3], X_DOWN)
    return (part[0].astype(jnp.float32) + one.astype(jnp.float32)) + (
        two.astype(jnp.float32) + three.astype(jnp.float32)
    )


def in_order(values, core, x):
    half = values.shape[0] // 2
    start = (4 - x) % 4 * (half // 4)
    pair = jnp.stack([values[:half], values[half:]])
    pair = lax.dynamic_slice_in_dim(jnp.concatenate([pair, pair], axis=1), start, half, axis=1)
    return jnp.where(core == 0, pair, pair[::-1]).reshape(values.shape)


def from_order(values, core, x):
    half = values.shape[0] // 2
    pair = values.reshape(2, half, -1)
    pair = jnp.where(core == 0, pair, pair[::-1])
    pair = lax.dynamic_slice_in_dim(
        jnp.concatenate([pair, pair], axis=1), x * (half // 4), half, axis=1
    )
    return pair.reshape(values.shape)


def sum_groups(grad, yh, core, native):
    width = grad.shape[-1]
    kept = lax.psum_scatter(
        grad.reshape(-1, width),
        BOTH,
        scatter_dimension=0,
        tiled=True,
        axis_index_groups=Z_GROUPS,
    ).reshape(2, -1, width)
    near = jnp.where(yh == 0, kept[0], kept[1])
    far = jnp.where(yh == 0, kept[1], kept[0])
    low = send(near, FOREIGN_LOW)
    high = send(far, FOREIGN_HIGH)
    across = send(far, NATIVE_FAR)
    total = (near.astype(jnp.float32) + low.astype(jnp.float32)) + (
        high.astype(jnp.float32) + across.astype(jnp.float32)
    )
    rows = total.shape[0] // 2
    mine = jnp.where(core == 0, total[:rows], total[rows:])
    theirs = jnp.where(core == 0, total[rows:], total[:rows])
    passed = send(theirs.astype(jnp.bfloat16), NATIVE_CORE).astype(jnp.float32)
    return jnp.where(native, mine, passed)


def inverse_freq(head_width):
    indices = jnp.arange(head_width // 2, dtype=jnp.float32)
    base_freq = jnp.exp(-jnp.log(THETA) * 2.0 * indices / head_width)
    wavelength = 2.0 * jnp.pi / base_freq
    smooth = (8192.0 / wavelength - 1.0) / 3.0
    blended = (1.0 - smooth) * base_freq / 32.0 + smooth * base_freq
    return jnp.where(
        wavelength < 2048.0, base_freq, jnp.where(wavelength > 8192.0, base_freq / 32.0, blended)
    )


VMEM = pl.BlockSpec(memory_space=pltpu.VMEM)


def params(mib):
    return pltpu.CompilerParams(vmem_limit_bytes=mib * 1024 * 1024)


def dot(left, right, left_dim=1, right_dim=0):
    return lax.dot_general(
        left, right, (((left_dim,), (right_dim,)), ((), ())), preferred_element_type=jnp.float32
    )


def stacked(block):
    return jnp.concatenate(
        [block[:, h * HEAD_DIM : (h + 1) * HEAD_DIM] for h in range(4)], axis=0
    )


def unstacked(block):
    rows = block.shape[0] // 4
    return jnp.concatenate([block[h * rows : (h + 1) * rows] for h in range(4)], axis=1)


def as_row(column):
    return jnp.transpose(jnp.broadcast_to(column, (column.shape[0], 128)))[:8]


def turned(values, cos_rows, sin_rows):
    half = HEAD_DIM // 2
    swapped = jnp.concatenate([values[:, half:], values[:, :half]], axis=1)
    return values * cos_rows + swapped * sin_rows


def short_forward_kernel(qkv_ref, start_ref, attn_ref, lse_ref):
    blocks = attn_ref.shape[0] // HALF
    for i in range(blocks):
        rows = pl.ds((i + 2) * HALF, HALF)
        keys = (i + 1) * HALF
        q = stacked(qkv_ref[rows, :256]) * jnp.bfloat16(HEAD_DIM**-0.5)
        k = qkv_ref[pl.ds(2 * HALF, keys), 256:320]
        v = qkv_ref[pl.ds(2 * HALF, keys), 320:384]
        scores = dot(q, k, 1, 1)
        column = lax.broadcasted_iota(jnp.int32, (HALF, keys), 1)
        row = lax.broadcasted_iota(jnp.int32, (HALF, keys), 0) + i * HALF
        seen = (column <= row) & (column >= start_ref[pl.ds(i * HALF, HALF), :1])
        scores = jnp.where(jnp.concatenate([seen] * 4, axis=0), scores, MASKED)
        top = jnp.max(scores, axis=1, keepdims=True)
        weights = jnp.exp(scores - top)
        total = jnp.sum(weights, axis=1, keepdims=True)
        out = dot(weights.astype(jnp.bfloat16), v) / total
        attn_ref[pl.ds(i * HALF, HALF), :] = unstacked(out).astype(jnp.bfloat16)
        lse_ref[i] = as_row(top + jnp.log(total))


def short_forward(qkv, start):
    rows = qkv.shape[0] - 2 * HALF
    blocks = rows // HALF
    return pl.pallas_call(
        short_forward_kernel,
        out_shape=(
            jax.ShapeDtypeStruct((rows, 256), jnp.bfloat16),
            jax.ShapeDtypeStruct((blocks, 8, 4 * HALF), jnp.float32),
        ),
        in_specs=[VMEM] * 2,
        out_specs=(VMEM,) * 2,
        compiler_params=params(40),
        name="short_forward",
    )(qkv, start)


CHUNK = 1024


def long_forward_kernel(q_ref, far_ref, far_pos_ref, pos_ref, attn_ref, lse_ref):
    for half in range(2):
        rows = pl.ds(half * HALF, HALF)
        q = stacked(q_ref[rows, :256]) * jnp.bfloat16(HEAD_DIM**-0.5)
        position = jnp.concatenate([pos_ref[rows, :1]] * 4, axis=0)

        def step(i, carry):
            top, total, out = carry
            keys = pl.ds(pl.multiple_of(i * CHUNK, CHUNK), CHUNK)
            block = far_ref[keys, :]
            scores = dot(q, block[:, :HEAD_DIM], 1, 1)
            seen = far_pos_ref[i, :1] <= position
            scores = jnp.where(seen, scores, MASKED)
            now = jnp.maximum(top, jnp.max(scores, axis=1, keepdims=True))
            weights = jnp.where(seen, jnp.exp(scores - now), 0.0)
            scale = jnp.exp(top - now)
            total = total * scale + jnp.sum(weights, axis=1, keepdims=True)
            out = out * scale + dot(weights.astype(jnp.bfloat16), block[:, HEAD_DIM:])
            return now, total, out

        first = (
            jnp.full((4 * HALF, 1), MASKED, jnp.float32),
            jnp.zeros((4 * HALF, 1), jnp.float32),
            jnp.zeros((4 * HALF, HEAD_DIM), jnp.float32),
        )
        top, total, out = lax.fori_loop(0, far_ref.shape[0] // CHUNK, step, first)
        attn_ref[rows, :] = unstacked(out / total).astype(jnp.bfloat16)
        lse_ref[half] = as_row(top + jnp.log(total))


def long_forward(q, far, far_pos, pos):
    return pl.pallas_call(
        long_forward_kernel,
        out_shape=(
            jax.ShapeDtypeStruct((2 * HALF, 256), jnp.bfloat16),
            jax.ShapeDtypeStruct((2, 8, 4 * HALF), jnp.float32),
        ),
        in_specs=[VMEM] * 4,
        out_specs=(VMEM,) * 2,
        compiler_params=params(40),
        name="long_forward",
    )(q, far, far_pos, pos)


def grad_terms(q, grad, k, v, seen, lse, delta):
    weights = jnp.where(seen, jnp.exp(dot(k, q, 1, 1) - lse), 0.0)
    grad_scores = (weights * (dot(v, grad, 1, 1) - delta)).astype(jnp.bfloat16)
    return (
        dot(grad_scores, k, 0, 0),
        dot(grad_scores, q),
        dot(weights.astype(jnp.bfloat16), grad),
    )


def row_product(left, right):
    return as_row(
        jnp.sum(left.astype(jnp.float32) * right.astype(jnp.float32), axis=1, keepdims=True)
    )[:1]


def short_backward_kernel(
    qkv_ref, start_ref, attn_ref, grad_ref, lse_ref, cos_ref, sin_ref, out_ref, dk_ref, dv_ref
):
    blocks = attn_ref.shape[0] // HALF
    scale = HEAD_DIM**-0.5
    dk_ref[...] = jnp.zeros_like(dk_ref)
    dv_ref[...] = jnp.zeros_like(dv_ref)
    for i in range(blocks):
        rows = pl.ds((i + 2) * HALF, HALF)
        keys = (i + 1) * HALF
        q = stacked(qkv_ref[rows, :256]) * jnp.bfloat16(scale)
        k = qkv_ref[pl.ds(2 * HALF, keys), 256:320]
        v = qkv_ref[pl.ds(2 * HALF, keys), 320:384]
        grad = stacked(grad_ref[rows, :])
        delta = row_product(grad, stacked(attn_ref[pl.ds(i * HALF, HALF), :]))
        key = lax.broadcasted_iota(jnp.int32, (keys, HALF), 0)
        query = lax.broadcasted_iota(jnp.int32, (keys, HALF), 1) + i * HALF
        seen = (key <= query) & (key >= start_ref[:1, pl.ds(i * HALF, HALF)])
        dq, dk, dv = grad_terms(
            q, grad, k, v, jnp.concatenate([seen] * 4, axis=1), lse_ref[i, :1], delta
        )
        cos_rows = cos_ref[rows, :]
        sin_rows = sin_ref[rows, :]
        dq = turned(
            dq * scale,
            jnp.concatenate([cos_rows] * 4, axis=0),
            jnp.concatenate([-sin_rows] * 4, axis=0),
        )
        out_ref[pl.ds(i * HALF, HALF), :256] = unstacked(dq).astype(jnp.bfloat16)
        dk_ref[pl.ds(0, keys), :] += dk
        dv_ref[pl.ds(0, keys), :] += dv
    rows = pl.ds(2 * HALF, blocks * HALF)
    dk = turned(dk_ref[...], cos_ref[rows, :], -sin_ref[rows, :])
    out_ref[:, 256:] = jnp.concatenate([dk, dv_ref[...]], axis=1).astype(jnp.bfloat16)


def short_backward(qkv, start, attn, grad, lse, cos_rows, sin_rows):
    rows = attn.shape[0]
    return pl.pallas_call(
        short_backward_kernel,
        out_shape=jax.ShapeDtypeStruct((rows, 384), jnp.bfloat16),
        in_specs=[VMEM] * 7,
        out_specs=VMEM,
        scratch_shapes=[pltpu.VMEM((rows, HEAD_DIM), jnp.float32)] * 2,
        compiler_params=params(48),
        name="short_backward",
    )(qkv, start, attn, grad, lse, cos_rows, sin_rows)


BACK_CHUNK = 1024


def long_backward_kernel(
    q_ref, far_ref, far_pos_ref, pos_ref, attn_ref, grad_ref, lse_ref, cos_ref, sin_ref,
    dq_ref, far_grad_ref, acc_ref,
):
    scale = HEAD_DIM**-0.5
    acc_ref[...] = jnp.zeros_like(acc_ref)
    queries = []
    for half in range(2):
        rows = pl.ds(half * HALF, HALF)
        grad = stacked(grad_ref[rows, :])
        queries.append(
            (
                stacked(q_ref[rows, :256]) * jnp.bfloat16(scale),
                grad,
                lse_ref[half, :1],
                row_product(grad, stacked(attn_ref[rows, :])),
                jnp.concatenate([pos_ref[:1, rows]] * 4, axis=1),
            )
        )

    def step(i, carry):
        keys = pl.ds(pl.multiple_of(i * BACK_CHUNK, BACK_CHUNK), BACK_CHUNK)
        block = far_ref[keys, :]
        k, v = block[:, :HEAD_DIM], block[:, HEAD_DIM:]
        sums = []
        for half, (q, grad, lse, delta, position) in enumerate(queries):
            seen = far_pos_ref[keys, :1] <= position
            dq, dk, dv = grad_terms(q, grad, k, v, seen, lse, delta)
            acc_ref[half] += dq
            sums.append((dk, dv))
        far_grad_ref[keys, :] = jnp.concatenate(
            [sums[0][0] + sums[1][0], sums[0][1] + sums[1][1]], axis=1
        ).astype(jnp.bfloat16)
        return carry

    lax.fori_loop(0, far_ref.shape[0] // BACK_CHUNK, step, 0)
    for half in range(2):
        rows = pl.ds(half * HALF, HALF)
        dq = turned(
            acc_ref[half] * scale,
            jnp.concatenate([cos_ref[rows, :]] * 4, axis=0),
            jnp.concatenate([-sin_ref[rows, :]] * 4, axis=0),
        )
        dq_ref[rows, :] = unstacked(dq).astype(jnp.bfloat16)


def long_backward(q, far, far_pos, pos, attn, grad, lse, cos_rows, sin_rows):
    return pl.pallas_call(
        long_backward_kernel,
        out_shape=(
            jax.ShapeDtypeStruct((2 * HALF, 256), jnp.bfloat16),
            jax.ShapeDtypeStruct(far.shape, jnp.bfloat16),
        ),
        in_specs=[VMEM] * 9,
        out_specs=(VMEM,) * 2,
        scratch_shapes=[pltpu.VMEM((2, 4 * HALF, HEAD_DIM), jnp.float32)],
        compiler_params=params(48),
        name="long_backward",
    )(q, far, far_pos, pos, attn, grad, lse, cos_rows, sin_rows)


def weight_grad_kernel(left_ref, right_ref, out_ref):
    out_ref[0, 0] = dot(left_ref[...], right_ref[...], 0, 0).astype(jnp.bfloat16)


def weight_grad(left, right):
    tokens, width = right.shape
    return pl.pallas_call(
        weight_grad_kernel,
        grid=(8,),
        out_shape=jax.ShapeDtypeStruct((4, 2, 256, width), jnp.bfloat16),
        in_specs=[
            pl.BlockSpec((tokens, 256), lambda i: (0, i)),
            pl.BlockSpec((tokens, width), lambda i: (0, 0), pipeline_mode=pl.Buffered(1)),
        ],
        out_specs=pl.BlockSpec((1, 1, 256, width), lambda i: (i % 4, i // 4, 0, 0)),
        compiler_params=params(40),
        name="weight_grad",
    )(left, right)


def mlp_kernel(hidden_ref, grad_act_ref, gate_ref, up_ref, act_ref, both_ref, back_ref):
    hidden = hidden_ref[...]
    gate = dot(hidden, gate_ref[...])
    up = dot(hidden, up_ref[...])
    grad_act = grad_act_ref[...].astype(jnp.float32)
    sig = jax.nn.sigmoid(gate)
    silu = gate * sig
    act_ref[...] = (silu * up).astype(jnp.bfloat16)
    grad_gate = (grad_act * up * sig * (1.0 + gate * (1.0 - sig))).astype(jnp.bfloat16)
    grad_up = (grad_act * silu).astype(jnp.bfloat16)
    width = gate.shape[1]
    both_ref[:, :width] = grad_gate
    both_ref[:, width:] = grad_up
    back_ref[...] = (dot(grad_gate, gate_ref[...], 1, 1) + dot(grad_up, up_ref[...], 1, 1)).astype(
        jnp.bfloat16
    )


def mlp(hidden, grad_act, w_gate, w_up, block=272):
    rows, d = hidden.shape
    width = w_gate.shape[1]
    return pl.pallas_call(
        mlp_kernel,
        grid=(rows // block,),
        out_shape=(
            jax.ShapeDtypeStruct((rows, width), jnp.bfloat16),
            jax.ShapeDtypeStruct((rows, 2 * width), jnp.bfloat16),
            jax.ShapeDtypeStruct((rows, d), jnp.bfloat16),
        ),
        in_specs=[
            pl.BlockSpec((block, d), lambda i: (i, 0)),
            pl.BlockSpec((block, width), lambda i: (i, 0)),
            pl.BlockSpec((d, width), lambda i: (0, 0), pipeline_mode=pl.Buffered(1)),
            pl.BlockSpec((d, width), lambda i: (0, 0), pipeline_mode=pl.Buffered(1)),
        ],
        out_specs=(
            pl.BlockSpec((block, width), lambda i: (i, 0)),
            pl.BlockSpec((block, 2 * width), lambda i: (i, 0)),
            pl.BlockSpec((block, d), lambda i: (i, 0)),
        ),
        compiler_params=params(56),
        name="mlp",
    )(hidden, grad_act, w_gate, w_up)


def qkv_kernel(hidden_ref, query_ref, kv_ref, cos_ref, sin_ref, out_ref):
    hidden = hidden_ref[...]
    query = dot(hidden, query_ref[...])
    kv = dot(hidden, kv_ref[...])
    cos_rows, sin_rows = cos_ref[...], sin_ref[...]
    heads = [
        turned(query[:, h * HEAD_DIM : (h + 1) * HEAD_DIM], cos_rows, sin_rows) for h in range(4)
    ]
    heads += [turned(kv[:, :HEAD_DIM], cos_rows, sin_rows), kv[:, HEAD_DIM:]]
    out_ref[...] = jnp.concatenate(heads, axis=1).astype(jnp.bfloat16)


def project_qkv(hidden, w_query, w_key_value, cos_rows, sin_rows, block=272):
    rows, d = hidden.shape
    return pl.pallas_call(
        qkv_kernel,
        grid=(rows // block,),
        out_shape=jax.ShapeDtypeStruct((rows, 384), jnp.bfloat16),
        in_specs=[
            pl.BlockSpec((block, d), lambda i: (i, 0)),
            pl.BlockSpec((d, 256), lambda i: (0, 0), pipeline_mode=pl.Buffered(1)),
            pl.BlockSpec((d, 128), lambda i: (0, 0), pipeline_mode=pl.Buffered(1)),
            pl.BlockSpec((block, HEAD_DIM), lambda i: (i, 0)),
            pl.BlockSpec((block, HEAD_DIM), lambda i: (i, 0)),
        ],
        out_specs=pl.BlockSpec((block, 384), lambda i: (i, 0)),
        compiler_params=params(32),
        name="project_qkv",
    )(hidden, w_query, w_key_value, cos_rows, sin_rows)


def norm_back(grad_in, unit_rows, inv_rms, gain):
    scaled = grad_in * gain
    return inv_rms * (scaled - unit_rows * jnp.mean(scaled * unit_rows, axis=-1, keepdims=True))


def all_sum(values):
    for group in ((CORE,), (X_UP, X_DOWN, X_FAR), (Z_UP, Z_DOWN, Z_FAR), (Y_LOW, Y_HIGH, Y_FAR)):
        values = sum([send(values, pairs) for pairs in group], values)
    return values


def local(
    tokens,
    lengths,
    place,
    attn_gain,
    w_query,
    w_key,
    w_value,
    w_out,
    mlp_gain,
    w_gate,
    w_up,
    w_down,
    out_grad,
):
    rows = tokens.shape[0]
    group_rows = rows * 8
    half_rows = rows * 4
    long_rows = 2 * HALF
    padded_rows = -(-group_rows // HALF) * HALF
    dp_index, mp_index = lax.axis_index("dp"), lax.axis_index("mp")
    yh, z, core = dp_index // 8, dp_index // 2 % 4, dp_index % 2
    yl, x = mp_index // 4, mp_index % 4
    native = core == yl

    tokens = send(tokens, TURN)
    lengths = send(lengths, TURN)[0]
    w_key_value = send(jnp.concatenate([w_key, w_value], axis=1), WEIGHT_HIGH)
    w_query = send(w_query, WEIGHT_LOW)
    w_out = send(w_out, WEIGHT_HIGH)
    w_gate = send(w_gate, WEIGHT_LOW)
    w_up = send(w_up, WEIGHT_HIGH)
    w_down = send(w_down, WEIGHT_LOW)
    out_grad = send(out_grad, TURN)

    group = (yh * 4 + z) * 2 + yl
    half_ids = jnp.arange(place.shape[0], dtype=jnp.int32)

    def place_at(index):
        return jnp.sum(jnp.where(half_ids == index[..., None], place, 0), axis=-1)

    def position_of(row):
        packed = row - long_rows
        first, second = lengths[0], lengths[0] + lengths[1]
        start = jnp.where(packed >= second, second, jnp.where(packed >= first, first, 0))
        start = jnp.where(row >= group_rows, packed, start)
        own = jnp.where(row < HALF, place_at(2 * group), place_at(2 * group + 1))
        return jnp.where(row < long_rows, own * HALF + row % HALF, packed - start), start

    def tables(position):
        angles = position.astype(jnp.float32)[:, None] * inverse_freq(HEAD_DIM)[None, :]
        cos_rows, sin_rows = jnp.cos(angles), jnp.sin(angles)
        return (
            jnp.concatenate([cos_rows, cos_rows], axis=1),
            jnp.concatenate([-sin_rows, sin_rows], axis=1),
        )

    ordered_rows = jnp.arange(padded_rows, dtype=jnp.int32)
    ordered_pos, ordered_start = position_of(ordered_rows)
    cos_ordered, sin_ordered = tables(ordered_pos)
    index = jnp.arange(group_rows, dtype=jnp.int32)
    shard = jnp.where(index < half_rows, core, 1 - core) * 4 + (x + index % half_rows // rows) % 4
    cos_gathered, sin_gathered = tables(position_of(shard * rows + index % rows)[0])
    starts = ordered_start[long_rows:]
    start_column = jnp.broadcast_to(starts[:, None], (starts.shape[0], 128))
    start_row = jnp.broadcast_to(starts[None, :], (8, starts.shape[0]))
    long_pos = ordered_pos[:long_rows]
    pos_column = jnp.broadcast_to(long_pos[:, None], (long_rows, 128))
    pos_row = jnp.broadcast_to(long_pos[None, :], (8, long_rows))
    step = jnp.arange(16, dtype=jnp.int32)
    far_yh = jnp.where(step // 4 >= 2, 1 - yh, yh)
    far_yl = jnp.where((step // 4 == 1) | (step // 4 == 2), 1 - yl, yl)
    far_group = (far_yh * 4 + (z + step) % 4) * 2 + far_yl
    far_half = place_at(2 * far_group[:, None] + jnp.arange(2, dtype=jnp.int32)[None, :])
    far_pos = (
        far_half.reshape(-1, 1) * HALF + jnp.arange(HALF, dtype=jnp.int32)[None, :]
    ).reshape(-1)
    far_row = jnp.broadcast_to(far_pos.reshape(-1, 1, CHUNK), (far_pos.shape[0] // CHUNK, 8, CHUNK))
    far_column = jnp.broadcast_to(far_pos[:, None], (far_pos.shape[0], 128))

    residual = tokens.astype(jnp.float32)
    inv_one = lax.rsqrt(jnp.mean(residual * residual, axis=-1, keepdims=True) + EPS)
    unit_one = residual * inv_one
    hidden_one = jnp.concatenate(gather((unit_one * attn_gain).astype(jnp.bfloat16)))
    qkv = project_qkv(hidden_one, w_query, w_key_value, cos_gathered, sin_gathered)
    qkv = jnp.pad(in_order(qkv, core, x), ((0, padded_rows - group_rows), (0, 0)))
    near_rows = qkv[:long_rows, 256:]
    ring_rows = jnp.concatenate(
        [near_rows, send(near_rows, Z_DOWN), send(near_rows, Z_FAR), send(near_rows, Z_UP)]
    )
    far_rows = jnp.concatenate(
        [ring_rows, send(ring_rows, Y_LOW), send(ring_rows, Y_HIGH), send(ring_rows, Y_FAR)]
    )
    long_q = qkv[:long_rows]
    short_attn, short_lse = short_forward(qkv, start_column)
    long_attn, long_lse = long_forward(long_q, far_rows, far_row, pos_column)
    attn_rows = from_order(
        jnp.concatenate([long_attn, short_attn[: group_rows - long_rows]]), core, x
    )

    def project(left, right):
        return jnp.dot(left, right, preferred_element_type=jnp.float32).astype(jnp.bfloat16)

    mixed = residual + scatter(
        project(attn_rows[:half_rows], w_out), project(attn_rows[half_rows:], w_out)
    )
    inv_two = lax.rsqrt(jnp.mean(mixed * mixed, axis=-1, keepdims=True) + EPS)
    unit_two = mixed * inv_two
    grad_rows = jnp.concatenate(gather(out_grad))
    grad_act = dot(grad_rows, w_down, 1, 1).astype(jnp.bfloat16)
    hidden_two = jnp.concatenate(gather((unit_two * mlp_gain).astype(jnp.bfloat16)))

    act, grad_both, grad_hidden = mlp(hidden_two, grad_act, w_gate, w_up)
    grad_two = scatter(grad_hidden[:half_rows], grad_hidden[half_rows:])
    down_sum = sum_groups(weight_grad(grad_rows, act), yh, core, native).T
    both_sum = sum_groups(weight_grad(hidden_two, grad_both), yh, core, native)
    ff = act.shape[1]
    down_rows = project(act, w_down)
    output = mixed + scatter(down_rows[:half_rows], down_rows[half_rows:])
    output = send(output.astype(jnp.bfloat16), TURN)

    grad_mixed = out_grad.astype(jnp.float32) + norm_back(grad_two, unit_two, inv_two, mlp_gain)
    mixed_grad_rows = jnp.concatenate(gather(grad_mixed.astype(jnp.bfloat16)))
    mlp_gain_part = jnp.sum(grad_two * unit_two, axis=0)
    grad_attn = in_order(dot(mixed_grad_rows, w_out, 1, 1).astype(jnp.bfloat16), core, x)
    grad_attn = jnp.pad(grad_attn, ((0, padded_rows - group_rows), (0, 0)))
    long_dq, far_terms = long_backward(
        long_q,
        far_rows,
        far_column,
        pos_row,
        long_attn,
        grad_attn[:long_rows],
        long_lse,
        cos_ordered[:long_rows],
        sin_ordered[:long_rows],
    )
    ring = far_terms.reshape(4, 4 * long_rows, -1)
    ring_terms = (
        (ring[0].astype(jnp.float32) + send(ring[1], Y_LOW).astype(jnp.float32))
        + (send(ring[2], Y_HIGH).astype(jnp.float32) + send(ring[3], Y_FAR).astype(jnp.float32))
    ).astype(jnp.bfloat16)
    near = ring_terms.reshape(4, long_rows, -1)
    far_grads = (near[0].astype(jnp.float32) + send(near[1], Z_UP).astype(jnp.float32)) + (
        send(near[2], Z_FAR).astype(jnp.float32) + send(near[3], Z_DOWN).astype(jnp.float32)
    )
    short_low = short_backward(
        qkv, start_row, short_attn, grad_attn, short_lse, cos_ordered, sin_ordered
    )
    long_dk = turned(far_grads[:, :HEAD_DIM], cos_ordered[:long_rows], -sin_ordered[:long_rows])
    long_low = jnp.concatenate(
        [
            long_dq,
            long_dk.astype(jnp.bfloat16),
            far_grads[:, HEAD_DIM:].astype(jnp.bfloat16),
        ],
        axis=1,
    )
    low_rows = from_order(
        jnp.concatenate([long_low, short_low[: group_rows - long_rows]]), core, x
    )
    grad_hidden = (
        dot(low_rows[:, :256], w_query, 1, 1) + dot(low_rows[:, 256:], w_key_value, 1, 1)
    ).astype(jnp.bfloat16)
    grad_one = scatter(grad_hidden[:half_rows], grad_hidden[half_rows:])
    out_sum = sum_groups(weight_grad(mixed_grad_rows, attn_rows), yh, core, native).T
    qkv_sum = sum_groups(weight_grad(hidden_one, low_rows), yh, core, native)
    attn_gain_part = jnp.sum(grad_one * unit_one, axis=0)
    grad_tokens = grad_mixed + norm_back(grad_one, unit_one, inv_one, attn_gain)
    grad_tokens = send(grad_tokens.astype(jnp.bfloat16), TURN)
    gains = all_sum(jnp.stack([attn_gain_part, mlp_gain_part]))
    return (
        output,
        grad_tokens,
        gains[0],
        qkv_sum[:, :256],
        qkv_sum[:, 256:320],
        qkv_sum[:, 320:],
        out_sum,
        gains[1],
        both_sum[:, :ff],
        both_sum[:, ff:],
        down_sum,
    )


def solution(mesh):
    placed = (
        P(("dp", "mp"), None),
        P("dp", None),
        P(),
        P(),
        P(None, "mp"),
        P(None, "mp"),
        P(None, "mp"),
        P("mp", None),
        P(),
        P(None, "mp"),
        P(None, "mp"),
        P("mp", None),
        P(("dp", "mp"), None),
    )
    return jax.shard_map(
        local,
        mesh=mesh,
        in_specs=placed,
        out_specs=(
            P(("dp", "mp"), None),
            P(("dp", "mp"), None),
            P(),
            P("dp", "mp"),
            P("dp", "mp"),
            P("dp", "mp"),
            P("mp", "dp"),
            P(),
            P("dp", "mp"),
            P("dp", "mp"),
            P("mp", "dp"),
        ),
        check_vma=False,
    )
```

```python
import jax
import jax.numpy as jnp
from jax import lax
from jax.experimental import pallas as pl
from jax.experimental.pallas import tpu as pltpu
from jax.sharding import PartitionSpec as P

HEAD_DIM = 64
HALF = 128
MASKED = -1e30


EPS = 1e-05
THETA = 500000.0

BOTH = ("dp", "mp")


def place_of(yh, z, c, yl, x):
    return ((yh * 4 + z) * 2 + c) * 8 + yl * 4 + x


def pairs_of(target, sender=lambda yh, z, c, yl, x: True):
    return [
        (place_of(yh, z, c, yl, x), place_of(*target(yh, z, c, yl, x)))
        for yh in range(2)
        for z in range(4)
        for c in range(2)
        for yl in range(2)
        for x in range(4)
        if sender(yh, z, c, yl, x)
    ]


X_UP = pairs_of(lambda yh, z, c, yl, x: (yh, z, c, yl, (x + 1) % 4))
X_DOWN = pairs_of(lambda yh, z, c, yl, x: (yh, z, c, yl, (x + 3) % 4))
X_FAR = pairs_of(lambda yh, z, c, yl, x: (yh, z, c, yl, (x + 2) % 4))
Z_UP = pairs_of(lambda yh, z, c, yl, x: (yh, (z + 1) % 4, c, yl, x))
Z_DOWN = pairs_of(lambda yh, z, c, yl, x: (yh, (z + 3) % 4, c, yl, x))
Z_FAR = pairs_of(lambda yh, z, c, yl, x: (yh, (z + 2) % 4, c, yl, x))
CORE = pairs_of(lambda yh, z, c, yl, x: (yh, z, 1 - c, yl, x))
Y_LOW = pairs_of(lambda yh, z, c, yl, x: (yh, z, c, 1 - yl, x))
Y_HIGH = pairs_of(lambda yh, z, c, yl, x: (1 - yh, z, c, 1 - yl, x))
Y_FAR = pairs_of(lambda yh, z, c, yl, x: (1 - yh, z, c, yl, x))
TURN = pairs_of(lambda yh, z, c, yl, x: (yh, z, yl, c, x))
NATIVE = lambda yh, z, c, yl, x: c == yl
FOREIGN = lambda yh, z, c, yl, x: c != yl
FOREIGN_LOW = pairs_of(lambda yh, z, c, yl, x: (yh, z, c, 1 - yl, x), FOREIGN)
FOREIGN_HIGH = pairs_of(lambda yh, z, c, yl, x: (1 - yh, z, c, 1 - yl, x), FOREIGN)
NATIVE_FAR = pairs_of(lambda yh, z, c, yl, x: (1 - yh, z, c, yl, x), NATIVE)
NATIVE_CORE = pairs_of(lambda yh, z, c, yl, x: (yh, z, 1 - c, yl, x), NATIVE)
WEIGHT_LOW = pairs_of(
    lambda yh, z, c, yl, x: (yh, z, c, 1 - yl, x) if c == yl else (yh, z, 1 - c, yl, x)
)
WEIGHT_HIGH = pairs_of(
    lambda yh, z, c, yl, x: (1 - yh, z, c, 1 - yl, x) if c == yl else (yh, z, 1 - c, yl, x)
)
Z_GROUPS = [
    [place_of(yh, z, c, yl, x) for z in range(4)]
    for yh in range(2)
    for c in range(2)
    for yl in range(2)
    for x in range(4)
]


def send(values, pairs):
    return lax.ppermute(values, BOTH, pairs)


def gather(rows):
    own = jnp.concatenate([rows, send(rows, X_DOWN), send(rows, X_FAR), send(rows, X_UP)])
    return (own, send(own, CORE))


def scatter(own, other, after=()):
    part = add_parts(own, send(other, CORE), after)
    one, two, three = send(part[1], X_UP), send(part[2], X_FAR), send(part[3], X_DOWN)
    return (part[0].astype(jnp.float32) + one.astype(jnp.float32)) + (
        two.astype(jnp.float32) + three.astype(jnp.float32)
    )


def in_order(values, core, x):
    half = values.shape[0] // 2
    start = (4 - x) % 4 * (half // 4)
    pair = jnp.stack([values[:half], values[half:]])
    pair = lax.dynamic_slice_in_dim(jnp.concatenate([pair, pair], axis=1), start, half, axis=1)
    return jnp.where(core == 0, pair, pair[::-1]).reshape(values.shape)


def from_order(values, core, x):
    half = values.shape[0] // 2
    pair = values.reshape(2, half, -1)
    pair = jnp.where(core == 0, pair, pair[::-1])
    pair = lax.dynamic_slice_in_dim(
        jnp.concatenate([pair, pair], axis=1), x * (half // 4), half, axis=1
    )
    return pair.reshape(values.shape)


def sum_groups(grad, yh, core, native):
    width = grad.shape[-1]
    kept = lax.psum_scatter(
        grad.reshape(-1, width),
        BOTH,
        scatter_dimension=0,
        tiled=True,
        axis_index_groups=Z_GROUPS,
    ).reshape(2, -1, width)
    near = jnp.where(yh == 0, kept[0], kept[1])
    far = jnp.where(yh == 0, kept[1], kept[0])
    low = send(near, FOREIGN_LOW)
    high = send(far, FOREIGN_HIGH)
    across = send(far, NATIVE_FAR)
    total = (near.astype(jnp.float32) + low.astype(jnp.float32)) + (
        high.astype(jnp.float32) + across.astype(jnp.float32)
    )
    rows = total.shape[0] // 2
    mine = jnp.where(core == 0, total[:rows], total[rows:])
    theirs = jnp.where(core == 0, total[rows:], total[:rows])
    passed = send(theirs.astype(jnp.bfloat16), NATIVE_CORE).astype(jnp.float32)
    return jnp.where(native, mine, passed)


def inverse_freq(head_width):
    indices = jnp.arange(head_width // 2, dtype=jnp.float32)
    base_freq = jnp.exp(-jnp.log(THETA) * 2.0 * indices / head_width)
    wavelength = 2.0 * jnp.pi / base_freq
    smooth = (8192.0 / wavelength - 1.0) / 3.0
    blended = (1.0 - smooth) * base_freq / 32.0 + smooth * base_freq
    return jnp.where(
        wavelength < 2048.0, base_freq, jnp.where(wavelength > 8192.0, base_freq / 32.0, blended)
    )


VMEM = pl.BlockSpec(memory_space=pltpu.VMEM)
ANY = pl.BlockSpec(memory_space=pl.ANY)
PARAMS = pltpu.CompilerParams(vmem_limit_bytes=60 * 1024 * 1024)


def cost(flops, nbytes):
    return pl.CostEstimate(flops=int(flops), bytes_accessed=int(nbytes), transcendentals=0)


def dot(left, right, left_dim=1, right_dim=0):
    return lax.dot_general(
        left, right, (((left_dim,), (right_dim,)), ((), ())), preferred_element_type=jnp.float32
    )


def stacked(block):
    return jnp.concatenate(
        [block[:, h * HEAD_DIM : (h + 1) * HEAD_DIM] for h in range(4)], axis=0
    )


def unstacked(block):
    rows = block.shape[0] // 4
    return jnp.concatenate([block[h * rows : (h + 1) * rows] for h in range(4)], axis=1)


def as_row(column):
    return jnp.transpose(jnp.broadcast_to(column, (column.shape[0], 128)))[:8]


def turned(values, cos_rows, sin_rows):
    half = HEAD_DIM // 2
    swapped = jnp.concatenate([values[:, half:], values[:, :half]], axis=1)
    return values * cos_rows + swapped * sin_rows


def short_forward_kernel(qkv_ref, start_ref, attn_ref, lse_ref):
    blocks = attn_ref.shape[0] // HALF
    for i in range(blocks):
        rows = pl.ds((i + 2) * HALF, HALF)
        keys = (i + 1) * HALF
        q = stacked(qkv_ref[rows, :256]) * jnp.bfloat16(HEAD_DIM**-0.5)
        k = qkv_ref[pl.ds(2 * HALF, keys), 256:320]
        v = qkv_ref[pl.ds(2 * HALF, keys), 320:384]
        scores = dot(q, k, 1, 1)
        column = lax.broadcasted_iota(jnp.int32, (HALF, keys), 1)
        row = lax.broadcasted_iota(jnp.int32, (HALF, keys), 0) + i * HALF
        seen = (column <= row) & (column >= start_ref[pl.ds(i * HALF, HALF), :1])
        scores = jnp.where(jnp.concatenate([seen] * 4, axis=0), scores, MASKED)
        top = jnp.max(scores, axis=1, keepdims=True)
        weights = jnp.exp(scores - top)
        total = jnp.sum(weights, axis=1, keepdims=True)
        out = dot(weights.astype(jnp.bfloat16), v) / total
        attn_ref[pl.ds(i * HALF, HALF), :] = unstacked(out).astype(jnp.bfloat16)
        lse_ref[i] = as_row(top + jnp.log(total))


def short_forward(qkv, start):
    rows = qkv.shape[0] - 2 * HALF
    blocks = rows // HALF
    return pl.pallas_call(
        short_forward_kernel,
        out_shape=(
            jax.ShapeDtypeStruct((rows, 256), jnp.bfloat16),
            jax.ShapeDtypeStruct((blocks, 8, 4 * HALF), jnp.float32),
        ),
        in_specs=[VMEM] * 2,
        out_specs=(VMEM,) * 2,
        compiler_params=PARAMS,
        cost_estimate=cost(4e9, 2e6),
        name="short_forward",
    )(qkv, start)


CHUNK = 1024


def long_forward_kernel(q_ref, far_ref, far_pos_ref, pos_ref, *refs):
    attn_ref, lse_ref = refs[-2:]
    for half in range(2):
        rows = pl.ds(half * HALF, HALF)
        q = stacked(q_ref[rows, :256]) * jnp.bfloat16(HEAD_DIM**-0.5)
        position = jnp.concatenate([pos_ref[rows, :1]] * 4, axis=0)

        def step(i, carry):
            top, total, out = carry
            keys = pl.ds(pl.multiple_of(i * CHUNK, CHUNK), CHUNK)
            block = far_ref[keys, :]
            scores = dot(q, block[:, :HEAD_DIM], 1, 1)
            seen = far_pos_ref[i, :1] <= position
            scores = jnp.where(seen, scores, MASKED)
            now = jnp.maximum(top, jnp.max(scores, axis=1, keepdims=True))
            weights = jnp.where(seen, jnp.exp(scores - now), 0.0)
            scale = jnp.exp(top - now)
            total = total * scale + jnp.sum(weights, axis=1, keepdims=True)
            out = out * scale + dot(weights.astype(jnp.bfloat16), block[:, HEAD_DIM:])
            return now, total, out

        first = (
            jnp.full((4 * HALF, 1), MASKED, jnp.float32),
            jnp.zeros((4 * HALF, 1), jnp.float32),
            jnp.zeros((4 * HALF, HEAD_DIM), jnp.float32),
        )
        top, total, out = lax.fori_loop(0, far_ref.shape[0] // CHUNK, step, first)
        attn_ref[rows, :] = unstacked(out / total).astype(jnp.bfloat16)
        lse_ref[half] = as_row(top + jnp.log(total))


def long_forward(q, far, far_pos, pos, after=()):
    return pl.pallas_call(
        long_forward_kernel,
        out_shape=(
            jax.ShapeDtypeStruct((2 * HALF, 256), jnp.bfloat16),
            jax.ShapeDtypeStruct((2, 8, 4 * HALF), jnp.float32),
        ),
        in_specs=[VMEM] * 4 + [ANY] * len(after),
        out_specs=(VMEM,) * 2,
        compiler_params=PARAMS,
        cost_estimate=cost(10e9, 2e6),
        name="long_forward",
    )(q, far, far_pos, pos, *after)


def grad_terms(q, grad, k, v, seen, lse, delta):
    weights = jnp.where(seen, jnp.exp(dot(k, q, 1, 1) - lse), 0.0)
    grad_scores = (weights * (dot(v, grad, 1, 1) - delta)).astype(jnp.bfloat16)
    return (
        dot(grad_scores, k, 0, 0),
        dot(grad_scores, q),
        dot(weights.astype(jnp.bfloat16), grad),
    )


def row_product(left, right):
    return as_row(
        jnp.sum(left.astype(jnp.float32) * right.astype(jnp.float32), axis=1, keepdims=True)
    )[:1]


def short_backward_kernel(
    qkv_ref, start_ref, attn_ref, grad_ref, lse_ref, cos_ref, sin_ref, out_ref, dk_ref, dv_ref
):
    blocks = attn_ref.shape[0] // HALF
    scale = HEAD_DIM**-0.5
    dk_ref[...] = jnp.zeros_like(dk_ref)
    dv_ref[...] = jnp.zeros_like(dv_ref)
    for i in range(blocks):
        rows = pl.ds((i + 2) * HALF, HALF)
        keys = (i + 1) * HALF
        q = stacked(qkv_ref[rows, :256]) * jnp.bfloat16(scale)
        k = qkv_ref[pl.ds(2 * HALF, keys), 256:320]
        v = qkv_ref[pl.ds(2 * HALF, keys), 320:384]
        grad = stacked(grad_ref[rows, :])
        delta = row_product(grad, stacked(attn_ref[pl.ds(i * HALF, HALF), :]))
        key = lax.broadcasted_iota(jnp.int32, (keys, HALF), 0)
        query = lax.broadcasted_iota(jnp.int32, (keys, HALF), 1) + i * HALF
        seen = (key <= query) & (key >= start_ref[:1, pl.ds(i * HALF, HALF)])
        dq, dk, dv = grad_terms(
            q, grad, k, v, jnp.concatenate([seen] * 4, axis=1), lse_ref[i, :1], delta
        )
        cos_rows = cos_ref[rows, :]
        sin_rows = sin_ref[rows, :]
        dq = turned(
            dq * scale,
            jnp.concatenate([cos_rows] * 4, axis=0),
            jnp.concatenate([-sin_rows] * 4, axis=0),
        )
        out_ref[pl.ds(i * HALF, HALF), :256] = unstacked(dq).astype(jnp.bfloat16)
        dk_ref[pl.ds(0, keys), :] += dk
        dv_ref[pl.ds(0, keys), :] += dv
    rows = pl.ds(2 * HALF, blocks * HALF)
    dk = turned(dk_ref[...], cos_ref[rows, :], -sin_ref[rows, :])
    out_ref[:, 256:] = jnp.concatenate([dk, dv_ref[...]], axis=1).astype(jnp.bfloat16)


def short_backward(qkv, start, attn, grad, lse, cos_rows, sin_rows):
    rows = attn.shape[0]
    return pl.pallas_call(
        short_backward_kernel,
        out_shape=jax.ShapeDtypeStruct((rows, 384), jnp.bfloat16),
        in_specs=[VMEM] * 7,
        out_specs=VMEM,
        scratch_shapes=[pltpu.VMEM((rows, HEAD_DIM), jnp.float32)] * 2,
        compiler_params=PARAMS,
        cost_estimate=cost(7e9, 2e6),
        name="short_backward",
    )(qkv, start, attn, grad, lse, cos_rows, sin_rows)


BACK_CHUNK = 1024


def long_backward_kernel(
    q_ref, far_ref, far_pos_ref, pos_ref, attn_ref, grad_ref, lse_ref, cos_ref, sin_ref,
    dq_ref, far_grad_ref, acc_ref,
):
    scale = HEAD_DIM**-0.5
    acc_ref[...] = jnp.zeros_like(acc_ref)
    queries = []
    for half in range(2):
        rows = pl.ds(half * HALF, HALF)
        grad = stacked(grad_ref[rows, :])
        queries.append(
            (
                stacked(q_ref[rows, :256]) * jnp.bfloat16(scale),
                grad,
                lse_ref[half, :1],
                row_product(grad, stacked(attn_ref[rows, :])),
                jnp.concatenate([pos_ref[:1, rows]] * 4, axis=1),
            )
        )

    def step(i, carry):
        keys = pl.ds(pl.multiple_of(i * BACK_CHUNK, BACK_CHUNK), BACK_CHUNK)
        block = far_ref[keys, :]
        k, v = block[:, :HEAD_DIM], block[:, HEAD_DIM:]
        sums = []
        for half, (q, grad, lse, delta, position) in enumerate(queries):
            seen = far_pos_ref[keys, :1] <= position
            dq, dk, dv = grad_terms(q, grad, k, v, seen, lse, delta)
            acc_ref[half] += dq
            sums.append((dk, dv))
        total = jnp.concatenate(
            [sums[0][0] + sums[1][0], sums[0][1] + sums[1][1]], axis=1
        ).astype(jnp.bfloat16)
        rows = BACK_CHUNK // 4
        for k in range(4):
            far_grad_ref[k, pl.ds(pl.multiple_of(i * rows, rows), rows), :] = total[
                k * rows : (k + 1) * rows
            ]
        return carry

    lax.fori_loop(0, far_ref.shape[0] // BACK_CHUNK, step, 0)
    for half in range(2):
        rows = pl.ds(half * HALF, HALF)
        dq = turned(
            acc_ref[half] * scale,
            jnp.concatenate([cos_ref[rows, :]] * 4, axis=0),
            jnp.concatenate([-sin_ref[rows, :]] * 4, axis=0),
        )
        dq_ref[rows, :] = unstacked(dq).astype(jnp.bfloat16)


def long_backward(q, far, far_pos, pos, attn, grad, lse, cos_rows, sin_rows):
    return pl.pallas_call(
        long_backward_kernel,
        out_shape=(
            jax.ShapeDtypeStruct((2 * HALF, 256), jnp.bfloat16),
            jax.ShapeDtypeStruct((4, far.shape[0] // 4, far.shape[1]), jnp.bfloat16),
        ),
        in_specs=[VMEM] * 9,
        out_specs=(VMEM,) * 2,
        scratch_shapes=[pltpu.VMEM((2, 4 * HALF, HEAD_DIM), jnp.float32)],
        compiler_params=PARAMS,
        cost_estimate=cost(13e9, 3e6),
        name="long_backward",
    )(q, far, far_pos, pos, attn, grad, lse, cos_rows, sin_rows)


def weight_grad_kernel(left_ref, right_ref, out_ref):
    out_ref[...] = dot(left_ref[...], right_ref[...], 0, 0).astype(jnp.bfloat16)


def weight_grad(left, right):
    tokens, width = right.shape
    columns = left.shape[1]
    return pl.pallas_call(
        weight_grad_kernel,
        grid=(8,),
        out_shape=jax.ShapeDtypeStruct((columns, width), jnp.bfloat16),
        in_specs=[
            pl.BlockSpec((tokens, columns // 8), lambda i: (0, i)),
            pl.BlockSpec((tokens, width), lambda i: (0, 0), pipeline_mode=pl.Buffered(1)),
        ],
        out_specs=pl.BlockSpec((columns // 8, width), lambda i: (i % 4 * 2 + i // 4, 0)),
        compiler_params=PARAMS,
        cost_estimate=cost(3e9 + 2 * tokens * columns * width, 4 * columns * (tokens + width)),
        name="weight_grad",
    )(left, right)


def add_kernel(left_ref, right_ref, *refs):
    for k, out_ref in enumerate(refs[-4:]):
        rows = pl.ds(k * out_ref.shape[0], out_ref.shape[0])
        out_ref[...] = (
            left_ref[rows, :].astype(jnp.float32) + right_ref[rows, :].astype(jnp.float32)
        ).astype(jnp.bfloat16)


def add_parts(left, right, after=()):
    rows, width = left.shape
    return pl.pallas_call(
        add_kernel,
        grid=(2,),
        out_shape=(jax.ShapeDtypeStruct((rows // 4, width), jnp.bfloat16),) * 4,
        in_specs=[pl.BlockSpec((rows, width // 2), lambda i: (0, i))] * 2 + [ANY] * len(after),
        out_specs=(pl.BlockSpec((rows // 4, width // 2), lambda i: (0, i)),) * 4,
        compiler_params=PARAMS,
        cost_estimate=cost(1e6, 6 * rows * width),
        name="add_parts",
    )(left, right, *after)


def hidden_grad_kernel(low_ref, query_ref, kv_ref, hidden_ref, own_ref, other_ref, gain_ref):
    i = pl.program_id(0)
    low = low_ref[...]
    grad = dot(low[:, :256], query_ref[...], 1, 1) + dot(low[:, 256:], kv_ref[...], 1, 1)
    part = jnp.sum(grad * hidden_ref[...].astype(jnp.float32), axis=0, keepdims=True)

    @pl.when(i == 0)
    def _():
        gain_ref[...] = jnp.broadcast_to(part, gain_ref.shape)

    @pl.when(i > 0)
    def _():
        gain_ref[...] += part

    @pl.when(i < 2)
    def _():
        own_ref[...] = grad.astype(jnp.bfloat16)

    @pl.when(i >= 2)
    def _():
        other_ref[...] = grad.astype(jnp.bfloat16)


def hidden_grad(low, w_query, w_key_value, hidden):
    rows, d = hidden.shape
    block = rows // 4
    return pl.pallas_call(
        hidden_grad_kernel,
        grid=(4,),
        out_shape=(
            jax.ShapeDtypeStruct((rows // 2, d), jnp.bfloat16),
            jax.ShapeDtypeStruct((rows // 2, d), jnp.bfloat16),
            jax.ShapeDtypeStruct((8, d), jnp.float32),
        ),
        in_specs=[
            pl.BlockSpec((block, 384), lambda i: (i, 0)),
            pl.BlockSpec((d, 256), lambda i: (0, 0), pipeline_mode=pl.Buffered(1)),
            pl.BlockSpec((d, 128), lambda i: (0, 0), pipeline_mode=pl.Buffered(1)),
            pl.BlockSpec((block, d), lambda i: (i, 0)),
        ],
        out_specs=(
            pl.BlockSpec((block, d), lambda i: (jnp.minimum(i, 1), 0)),
            pl.BlockSpec((block, d), lambda i: (jnp.maximum(i, 2) - 2, 0)),
            pl.BlockSpec((8, d), lambda i: (0, 0)),
        ),
        compiler_params=PARAMS,
        cost_estimate=cost(2 * rows * d * 384, 4 * rows * d),
        name="hidden_grad",
    )(low, w_query, w_key_value, hidden)


def mlp_kernel(hidden_ref, grad_act_ref, gate_ref, up_ref, act_ref, both_ref, own_ref, other_ref):
    i = pl.program_id(0)
    hidden = hidden_ref[...]
    gate = dot(hidden, gate_ref[...])
    up = dot(hidden, up_ref[...])
    grad_act = grad_act_ref[...].astype(jnp.float32)
    sig = jax.nn.sigmoid(gate)
    silu = gate * sig
    act_ref[...] = (silu * up).astype(jnp.bfloat16)
    grad_gate = (grad_act * up * sig * (1.0 + gate * (1.0 - sig))).astype(jnp.bfloat16)
    grad_up = (grad_act * silu).astype(jnp.bfloat16)
    width = gate.shape[1]
    both_ref[:, :width] = grad_gate
    both_ref[:, width:] = grad_up
    back = (dot(grad_gate, gate_ref[...], 1, 1) + dot(grad_up, up_ref[...], 1, 1)).astype(
        jnp.bfloat16
    )

    @pl.when(i < 2)
    def _():
        own_ref[...] = back

    @pl.when(i >= 2)
    def _():
        other_ref[...] = back


def mlp(hidden, grad_act, w_gate, w_up):
    rows, d = hidden.shape
    block = rows // 4
    width = w_gate.shape[1]
    return pl.pallas_call(
        mlp_kernel,
        grid=(rows // block,),
        out_shape=(
            jax.ShapeDtypeStruct((rows, width), jnp.bfloat16),
            jax.ShapeDtypeStruct((rows, 2 * width), jnp.bfloat16),
            jax.ShapeDtypeStruct((rows // 2, d), jnp.bfloat16),
            jax.ShapeDtypeStruct((rows // 2, d), jnp.bfloat16),
        ),
        in_specs=[
            pl.BlockSpec((block, d), lambda i: (i, 0)),
            pl.BlockSpec((block, width), lambda i: (i, 0)),
            pl.BlockSpec((d, width), lambda i: (0, 0), pipeline_mode=pl.Buffered(1)),
            pl.BlockSpec((d, width), lambda i: (0, 0), pipeline_mode=pl.Buffered(1)),
        ],
        out_specs=(
            pl.BlockSpec((block, width), lambda i: (i, 0)),
            pl.BlockSpec((block, 2 * width), lambda i: (i, 0)),
            pl.BlockSpec((block, d), lambda i: (jnp.minimum(i, 1), 0)),
            pl.BlockSpec((block, d), lambda i: (jnp.maximum(i, 2) - 2, 0)),
        ),
        compiler_params=PARAMS,
        cost_estimate=cost(10 * rows * width * d, 12 * rows * d),
        name="mlp",
    )(hidden, grad_act, w_gate, w_up)


def qkv_kernel(hidden_ref, query_ref, kv_ref, cos_ref, sin_ref, out_ref):
    hidden = hidden_ref[...]
    query = dot(hidden, query_ref[...])
    kv = dot(hidden, kv_ref[...])
    cos_rows, sin_rows = cos_ref[...], sin_ref[...]
    heads = [
        turned(query[:, h * HEAD_DIM : (h + 1) * HEAD_DIM], cos_rows, sin_rows) for h in range(4)
    ]
    heads += [turned(kv[:, :HEAD_DIM], cos_rows, sin_rows), kv[:, HEAD_DIM:]]
    out_ref[...] = jnp.concatenate(heads, axis=1).astype(jnp.bfloat16)


def project_qkv(hidden, w_query, w_key_value, cos_rows, sin_rows, block=272):
    rows, d = hidden.shape
    return pl.pallas_call(
        qkv_kernel,
        grid=(rows // block,),
        out_shape=jax.ShapeDtypeStruct((rows, 384), jnp.bfloat16),
        in_specs=[
            pl.BlockSpec((block, d), lambda i: (i, 0)),
            pl.BlockSpec((d, 256), lambda i: (0, 0), pipeline_mode=pl.Buffered(1)),
            pl.BlockSpec((d, 128), lambda i: (0, 0), pipeline_mode=pl.Buffered(1)),
            pl.BlockSpec((block, HEAD_DIM), lambda i: (i, 0)),
            pl.BlockSpec((block, HEAD_DIM), lambda i: (i, 0)),
        ],
        out_specs=pl.BlockSpec((block, 384), lambda i: (i, 0)),
        compiler_params=PARAMS,
        cost_estimate=cost(4 * rows * d * 384, 4 * rows * d),
        name="project_qkv",
    )(hidden, w_query, w_key_value, cos_rows, sin_rows)


def norm_back(grad_in, unit_rows, inv_rms, gain):
    scaled = grad_in * gain
    return inv_rms * (scaled - unit_rows * jnp.mean(scaled * unit_rows, axis=-1, keepdims=True))


def all_sum(values):
    for group in ((CORE,), (X_UP, X_DOWN, X_FAR), (Z_UP, Z_DOWN, Z_FAR), (Y_LOW, Y_HIGH, Y_FAR)):
        values = sum([send(values, pairs) for pairs in group], values)
    return values


def local(
    tokens,
    lengths,
    place,
    attn_gain,
    w_query,
    w_key,
    w_value,
    w_out,
    mlp_gain,
    w_gate,
    w_up,
    w_down,
    out_grad,
):
    rows = tokens.shape[0]
    group_rows = rows * 8
    half_rows = rows * 4
    long_rows = 2 * HALF
    padded_rows = -(-group_rows // HALF) * HALF
    dp_index, mp_index = lax.axis_index("dp"), lax.axis_index("mp")
    yh, z, core = dp_index // 8, dp_index // 2 % 4, dp_index % 2
    yl, x = mp_index // 4, mp_index % 4
    native = core == yl

    tokens = send(tokens, TURN)
    lengths = send(lengths, TURN)[0]
    w_key_value = send(jnp.concatenate([w_key, w_value], axis=1), WEIGHT_HIGH)
    w_query = send(w_query, WEIGHT_LOW)
    w_out = send(w_out, WEIGHT_HIGH)
    w_gate = send(w_gate, WEIGHT_LOW)
    w_up = send(w_up, WEIGHT_HIGH)
    w_down = send(w_down, WEIGHT_LOW)
    out_grad = send(out_grad, TURN)

    group = (yh * 4 + z) * 2 + yl
    half_ids = jnp.arange(place.shape[0], dtype=jnp.int32)

    def place_at(index):
        return jnp.sum(jnp.where(half_ids == index[..., None], place, 0), axis=-1)

    def position_of(row):
        packed = row - long_rows
        first, second = lengths[0], lengths[0] + lengths[1]
        start = jnp.where(packed >= second, second, jnp.where(packed >= first, first, 0))
        start = jnp.where(row >= group_rows, packed, start)
        own = jnp.where(row < HALF, place_at(2 * group), place_at(2 * group + 1))
        return jnp.where(row < long_rows, own * HALF + row % HALF, packed - start), start

    def tables(position):
        angles = position.astype(jnp.float32)[:, None] * inverse_freq(HEAD_DIM)[None, :]
        cos_rows, sin_rows = jnp.cos(angles), jnp.sin(angles)
        return (
            jnp.concatenate([cos_rows, cos_rows], axis=1),
            jnp.concatenate([-sin_rows, sin_rows], axis=1),
        )

    ordered_rows = jnp.arange(padded_rows, dtype=jnp.int32)
    ordered_pos, ordered_start = position_of(ordered_rows)
    cos_ordered, sin_ordered = tables(ordered_pos)
    index = jnp.arange(group_rows, dtype=jnp.int32)
    shard = jnp.where(index < half_rows, core, 1 - core) * 4 + (x + index % half_rows // rows) % 4
    cos_gathered, sin_gathered = tables(position_of(shard * rows + index % rows)[0])
    starts = ordered_start[long_rows:]
    start_column = jnp.broadcast_to(starts[:, None], (starts.shape[0], 128))
    start_row = jnp.broadcast_to(starts[None, :], (8, starts.shape[0]))
    long_pos = ordered_pos[:long_rows]
    pos_column = jnp.broadcast_to(long_pos[:, None], (long_rows, 128))
    pos_row = jnp.broadcast_to(long_pos[None, :], (8, long_rows))
    step = jnp.arange(16, dtype=jnp.int32)
    far_yh = jnp.where(step % 4 >= 2, 1 - yh, yh)
    far_yl = jnp.where((step % 4 == 1) | (step % 4 == 2), 1 - yl, yl)
    far_group = (far_yh * 4 + (z + step // 4) % 4) * 2 + far_yl
    far_half = place_at(2 * far_group[:, None] + jnp.arange(2, dtype=jnp.int32)[None, :])
    far_pos = (
        far_half.reshape(-1, 1) * HALF + jnp.arange(HALF, dtype=jnp.int32)[None, :]
    ).reshape(-1)
    far_row = jnp.broadcast_to(far_pos.reshape(-1, 1, CHUNK), (far_pos.shape[0] // CHUNK, 8, CHUNK))
    far_column = jnp.broadcast_to(far_pos[:, None], (far_pos.shape[0], 128))

    residual = tokens.astype(jnp.float32)
    inv_one = lax.rsqrt(jnp.mean(residual * residual, axis=-1, keepdims=True) + EPS)
    unit_one = residual * inv_one
    hidden_one = jnp.concatenate(gather((unit_one * attn_gain).astype(jnp.bfloat16)))
    qkv = project_qkv(hidden_one, w_query, w_key_value, cos_gathered, sin_gathered)
    qkv = jnp.pad(in_order(qkv, core, x), ((0, padded_rows - group_rows), (0, 0)))
    near_rows = qkv[:long_rows, 256:]
    ring_rows = jnp.concatenate(
        [near_rows, send(near_rows, Y_LOW), send(near_rows, Y_HIGH), send(near_rows, Y_FAR)]
    )
    far_rows = jnp.concatenate(
        [ring_rows, send(ring_rows, Z_DOWN), send(ring_rows, Z_FAR), send(ring_rows, Z_UP)]
    )
    grad_own, grad_other = gather(out_grad)
    long_q = qkv[:long_rows]
    short_attn, short_lse = short_forward(qkv, start_column)
    long_attn, long_lse = long_forward(
        long_q, far_rows, far_row, pos_column, (grad_own, w_gate, w_up)
    )
    attn_rows = from_order(
        jnp.concatenate([long_attn, short_attn[: group_rows - long_rows]]), core, x
    )

    def project(left, right):
        return jnp.dot(left, right, preferred_element_type=jnp.float32).astype(jnp.bfloat16)

    mixed = residual + scatter(
        project(attn_rows[:half_rows], w_out), project(attn_rows[half_rows:], w_out)
    )
    inv_two = lax.rsqrt(jnp.mean(mixed * mixed, axis=-1, keepdims=True) + EPS)
    unit_two = mixed * inv_two
    grad_rows = jnp.concatenate([grad_own, grad_other])
    grad_act = dot(grad_rows, w_down, 1, 1).astype(jnp.bfloat16)
    hidden_two = jnp.concatenate(gather((unit_two * mlp_gain).astype(jnp.bfloat16)))

    act, grad_both, back_own, back_other = mlp(hidden_two, grad_act, w_gate, w_up)
    grad_two = scatter(back_own, back_other)
    down_sum = sum_groups(weight_grad(grad_rows, act), yh, core, native).T
    both_sum = sum_groups(weight_grad(hidden_two, grad_both), yh, core, native)
    ff = act.shape[1]
    down_rows = project(act, w_down)
    grad_mixed = out_grad.astype(jnp.float32) + norm_back(grad_two, unit_two, inv_two, mlp_gain)
    mixed_grad_rows = jnp.concatenate(gather(grad_mixed.astype(jnp.bfloat16)))
    mlp_gain_part = jnp.sum(grad_two * unit_two, axis=0)
    output = mixed + scatter(down_rows[:half_rows], down_rows[half_rows:], (mixed_grad_rows,))
    output = send(output.astype(jnp.bfloat16), TURN)
    grad_attn = in_order(dot(mixed_grad_rows, w_out, 1, 1).astype(jnp.bfloat16), core, x)
    grad_attn = jnp.pad(grad_attn, ((0, padded_rows - group_rows), (0, 0)))
    long_dq, far_terms = long_backward(
        long_q,
        far_rows,
        far_column,
        pos_row,
        long_attn,
        grad_attn[:long_rows],
        long_lse,
        cos_ordered[:long_rows],
        sin_ordered[:long_rows],
    )
    ring = far_terms
    ring_terms = (
        (ring[0].astype(jnp.float32) + send(ring[1], Y_LOW).astype(jnp.float32))
        + (send(ring[2], Y_HIGH).astype(jnp.float32) + send(ring[3], Y_FAR).astype(jnp.float32))
    ).astype(jnp.bfloat16)
    near = ring_terms.reshape(4, long_rows, -1)
    far_grads = (near[0].astype(jnp.float32) + send(near[1], Z_UP).astype(jnp.float32)) + (
        send(near[2], Z_FAR).astype(jnp.float32) + send(near[3], Z_DOWN).astype(jnp.float32)
    )
    short_low = short_backward(
        qkv, start_row, short_attn, grad_attn, short_lse, cos_ordered, sin_ordered
    )
    long_dk = turned(far_grads[:, :HEAD_DIM], cos_ordered[:long_rows], -sin_ordered[:long_rows])
    long_low = jnp.concatenate(
        [
            long_dq,
            long_dk.astype(jnp.bfloat16),
            far_grads[:, HEAD_DIM:].astype(jnp.bfloat16),
        ],
        axis=1,
    )
    low_rows = from_order(
        jnp.concatenate([long_low, short_low[: group_rows - long_rows]]), core, x
    )
    back_own, back_other, attn_gain_part = hidden_grad(
        low_rows, w_query, w_key_value, hidden_one
    )
    grad_one = scatter(back_own, back_other)
    gains = all_sum(jnp.stack([attn_gain_part[0] / attn_gain, mlp_gain_part]))
    out_sum = sum_groups(weight_grad(mixed_grad_rows, attn_rows), yh, core, native).T
    qkv_sum = sum_groups(weight_grad(hidden_one, low_rows), yh, core, native)
    grad_tokens = grad_mixed + norm_back(grad_one, unit_one, inv_one, attn_gain)
    grad_tokens = send(grad_tokens.astype(jnp.bfloat16), TURN)
    return (
        output,
        grad_tokens,
        gains[0],
        qkv_sum[:, :256],
        qkv_sum[:, 256:320],
        qkv_sum[:, 320:],
        out_sum,
        gains[1],
        both_sum[:, :ff],
        both_sum[:, ff:],
        down_sum,
    )


def solution(mesh):
    placed = (
        P(("dp", "mp"), None),
        P("dp", None),
        P(),
        P(),
        P(None, "mp"),
        P(None, "mp"),
        P(None, "mp"),
        P("mp", None),
        P(),
        P(None, "mp"),
        P(None, "mp"),
        P("mp", None),
        P(("dp", "mp"), None),
    )
    return jax.shard_map(
        local,
        mesh=mesh,
        in_specs=placed,
        out_specs=(
            P(("dp", "mp"), None),
            P(("dp", "mp"), None),
            P(),
            P("dp", "mp"),
            P("dp", "mp"),
            P("dp", "mp"),
            P("mp", "dp"),
            P(),
            P("dp", "mp"),
            P("dp", "mp"),
            P("mp", "dp"),
        ),
        check_vma=False,
    )
```

```python
import functools

import jax
import jax.numpy as jnp
from jax import lax
from jax.experimental import pallas as pl
from jax.experimental.pallas import tpu as pltpu
from jax.sharding import PartitionSpec as P

HEAD_DIM = 64
HALF = 128
MASKED = -1e30


EPS = 1e-05
THETA = 500000.0

BOTH = ("dp", "mp")


def place_of(yh, z, c, yl, x):
    return ((yh * 4 + z) * 2 + c) * 8 + yl * 4 + x


def pairs_of(target, sender=lambda yh, z, c, yl, x: True):
    return [
        (place_of(yh, z, c, yl, x), place_of(*target(yh, z, c, yl, x)))
        for yh in range(2)
        for z in range(4)
        for c in range(2)
        for yl in range(2)
        for x in range(4)
        if sender(yh, z, c, yl, x)
    ]


X_UP = pairs_of(lambda yh, z, c, yl, x: (yh, z, c, yl, (x + 1) % 4))
X_DOWN = pairs_of(lambda yh, z, c, yl, x: (yh, z, c, yl, (x + 3) % 4))
X_FAR = pairs_of(lambda yh, z, c, yl, x: (yh, z, c, yl, (x + 2) % 4))
Z_UP = pairs_of(lambda yh, z, c, yl, x: (yh, (z + 1) % 4, c, yl, x))
Z_DOWN = pairs_of(lambda yh, z, c, yl, x: (yh, (z + 3) % 4, c, yl, x))
Z_FAR = pairs_of(lambda yh, z, c, yl, x: (yh, (z + 2) % 4, c, yl, x))
CORE = pairs_of(lambda yh, z, c, yl, x: (yh, z, 1 - c, yl, x))
Y_LOW = pairs_of(lambda yh, z, c, yl, x: (yh, z, c, 1 - yl, x))
Y_HIGH = pairs_of(lambda yh, z, c, yl, x: (1 - yh, z, c, 1 - yl, x))
Y_FAR = pairs_of(lambda yh, z, c, yl, x: (1 - yh, z, c, yl, x))
TURN = pairs_of(lambda yh, z, c, yl, x: (yh, z, yl, c, x))
NATIVE = lambda yh, z, c, yl, x: c == yl
FOREIGN = lambda yh, z, c, yl, x: c != yl
FOREIGN_LOW = pairs_of(lambda yh, z, c, yl, x: (yh, z, c, 1 - yl, x), FOREIGN)
FOREIGN_HIGH = pairs_of(lambda yh, z, c, yl, x: (1 - yh, z, c, 1 - yl, x), FOREIGN)
NATIVE_FAR = pairs_of(lambda yh, z, c, yl, x: (1 - yh, z, c, yl, x), NATIVE)
NATIVE_CORE = pairs_of(lambda yh, z, c, yl, x: (yh, z, 1 - c, yl, x), NATIVE)
WEIGHT_LOW = pairs_of(
    lambda yh, z, c, yl, x: (yh, z, c, 1 - yl, x) if c == yl else (yh, z, 1 - c, yl, x)
)
WEIGHT_HIGH = pairs_of(
    lambda yh, z, c, yl, x: (1 - yh, z, c, 1 - yl, x) if c == yl else (yh, z, 1 - c, yl, x)
)
Z_GROUPS = [
    [place_of(yh, z, c, yl, x) for z in range(4)]
    for yh in range(2)
    for c in range(2)
    for yl in range(2)
    for x in range(4)
]


CHIP_GROUPS = [
    [place_of(yh, z, c, yl, x) for c in range(2) for x in range(4)]
    for yh in range(2)
    for z in range(4)
    for yl in range(2)
]


def send(values, pairs):
    return lax.ppermute(values, BOTH, pairs)


def gather(rows, after=(), passed=()):
    pieces = (rows, send(rows, X_DOWN), send(rows, X_FAR), send(rows, X_UP))
    own, *passed = join(pieces, after, passed)
    return (own, send(own, CORE), *passed)


def scatter(parts):
    return (
        parts[0],
        send(parts[1], X_UP),
        send(parts[2], X_FAR),
        send(parts[3], X_DOWN),
    )


def total_of(parts):
    one, two, three, four = [part.astype(jnp.float32) for part in parts]
    return (one + two) + (three + four)


def in_order(own, other, core, x):
    half = own.shape[0]
    pair = jnp.stack([own, other])
    start = (4 - x) % 4 * (half // 4)
    pair = lax.dynamic_slice_in_dim(jnp.concatenate([pair, pair], axis=1), start, half, axis=1)
    return jnp.where(core == 0, pair, pair[::-1]).reshape(2 * half, -1)


def from_order(values, core, x):
    half = values.shape[0] // 2
    pair = values.reshape(2, half, -1)
    pair = jnp.where(core == 0, pair, pair[::-1])
    pair = lax.dynamic_slice_in_dim(
        jnp.concatenate([pair, pair], axis=1), x * (half // 4), half, axis=1
    )
    return pair[0], pair[1]


def sum_groups(grad, yh, core, native):
    width = grad.shape[-1]
    kept = lax.psum_scatter(
        grad.reshape(-1, width),
        BOTH,
        scatter_dimension=0,
        tiled=True,
        axis_index_groups=Z_GROUPS,
    ).reshape(2, -1, width)
    near = jnp.where(yh == 0, kept[0], kept[1])
    far = jnp.where(yh == 0, kept[1], kept[0])
    low = send(near, FOREIGN_LOW)
    high = send(far, FOREIGN_HIGH)
    across = send(far, NATIVE_FAR)
    total = (near.astype(jnp.float32) + low.astype(jnp.float32)) + (
        high.astype(jnp.float32) + across.astype(jnp.float32)
    )
    rows = total.shape[0] // 2
    mine = jnp.where(core == 0, total[:rows], total[rows:])
    theirs = jnp.where(core == 0, total[rows:], total[:rows])
    passed = send(theirs.astype(jnp.bfloat16), NATIVE_CORE).astype(jnp.float32)
    return jnp.where(native, mine, passed)


def inverse_freq(head_width):
    indices = jnp.arange(head_width // 2, dtype=jnp.float32)
    base_freq = jnp.exp(-jnp.log(THETA) * 2.0 * indices / head_width)
    wavelength = 2.0 * jnp.pi / base_freq
    smooth = (8192.0 / wavelength - 1.0) / 3.0
    blended = (1.0 - smooth) * base_freq / 32.0 + smooth * base_freq
    return jnp.where(
        wavelength < 2048.0, base_freq, jnp.where(wavelength > 8192.0, base_freq / 32.0, blended)
    )


VMEM = pl.BlockSpec(memory_space=pltpu.VMEM)
ANY = pl.BlockSpec(memory_space=pl.ANY)
PARAMS = pltpu.CompilerParams(vmem_limit_bytes=60 * 1024 * 1024)


def cost(flops, nbytes):
    return pl.CostEstimate(flops=int(flops), bytes_accessed=int(nbytes), transcendentals=0)


def dot(left, right, left_dim=1, right_dim=0):
    return lax.dot_general(
        left, right, (((left_dim,), (right_dim,)), ((), ())), preferred_element_type=jnp.float32
    )


def stacked(block):
    return jnp.concatenate(
        [block[:, h * HEAD_DIM : (h + 1) * HEAD_DIM] for h in range(4)], axis=0
    )


def unstacked(block):
    rows = block.shape[0] // 4
    return jnp.concatenate([block[h * rows : (h + 1) * rows] for h in range(4)], axis=1)


def as_row(column):
    return jnp.transpose(jnp.broadcast_to(column, (column.shape[0], 128)))[:8]


def turned(values, cos_rows, sin_rows):
    half = HEAD_DIM // 2
    swapped = jnp.concatenate([values[:, half:], values[:, :half]], axis=1)
    return values * cos_rows + swapped * sin_rows


def short_forward_kernel(qkv_ref, start_ref, attn_ref, lse_ref):
    blocks = attn_ref.shape[0] // HALF
    for i in range(blocks):
        rows = pl.ds((i + 2) * HALF, HALF)
        keys = (i + 1) * HALF
        q = stacked(qkv_ref[rows, :256]) * jnp.bfloat16(HEAD_DIM**-0.5)
        k = qkv_ref[pl.ds(2 * HALF, keys), 256:320]
        v = qkv_ref[pl.ds(2 * HALF, keys), 320:384]
        scores = dot(q, k, 1, 1)
        column = lax.broadcasted_iota(jnp.int32, (HALF, keys), 1)
        row = lax.broadcasted_iota(jnp.int32, (HALF, keys), 0) + i * HALF
        seen = (column <= row) & (column >= start_ref[pl.ds(i * HALF, HALF), :1])
        scores = jnp.where(jnp.concatenate([seen] * 4, axis=0), scores, MASKED)
        top = jnp.max(scores, axis=1, keepdims=True)
        weights = jnp.exp(scores - top)
        total = jnp.sum(weights, axis=1, keepdims=True)
        out = dot(weights.astype(jnp.bfloat16), v) / total
        attn_ref[pl.ds(i * HALF, HALF), :] = unstacked(out).astype(jnp.bfloat16)
        lse_ref[i] = as_row(top + jnp.log(total))


def short_forward(qkv, start):
    rows = qkv.shape[0] - 2 * HALF
    blocks = rows // HALF
    return pl.pallas_call(
        short_forward_kernel,
        out_shape=(
            jax.ShapeDtypeStruct((rows, 256), jnp.bfloat16),
            jax.ShapeDtypeStruct((blocks, 8, 4 * HALF), jnp.float32),
        ),
        in_specs=[VMEM] * 2,
        out_specs=(VMEM,) * 2,
        compiler_params=PARAMS,
        cost_estimate=cost(4e9, 2e6),
        name="short_forward",
    )(qkv, start)


CHUNK = 1024


def long_forward_kernel(q_ref, far_ref, far_pos_ref, pos_ref, *refs):
    attn_ref, lse_ref = refs[-2:]
    for half in range(2):
        rows = pl.ds(half * HALF, HALF)
        q = stacked(q_ref[rows, :256]) * jnp.bfloat16(HEAD_DIM**-0.5)
        position = jnp.concatenate([pos_ref[rows, :1]] * 4, axis=0)

        def step(i, carry):
            top, total, out = carry
            keys = pl.ds(pl.multiple_of(i * CHUNK, CHUNK), CHUNK)
            block = far_ref[keys, :]
            scores = dot(q, block[:, :HEAD_DIM], 1, 1)
            seen = far_pos_ref[i, :1] <= position
            scores = jnp.where(seen, scores, MASKED)
            now = jnp.maximum(top, jnp.max(scores, axis=1, keepdims=True))
            weights = jnp.where(seen, jnp.exp(scores - now), 0.0)
            scale = jnp.exp(top - now)
            total = total * scale + jnp.sum(weights, axis=1, keepdims=True)
            out = out * scale + dot(weights.astype(jnp.bfloat16), block[:, HEAD_DIM:])
            return now, total, out

        first = (
            jnp.full((4 * HALF, 1), MASKED, jnp.float32),
            jnp.zeros((4 * HALF, 1), jnp.float32),
            jnp.zeros((4 * HALF, HEAD_DIM), jnp.float32),
        )
        top, total, out = lax.fori_loop(0, far_ref.shape[0] // CHUNK, step, first)
        attn_ref[rows, :] = unstacked(out / total).astype(jnp.bfloat16)
        lse_ref[half] = as_row(top + jnp.log(total))


def long_forward(q, far, far_pos, pos, after=()):
    return pl.pallas_call(
        long_forward_kernel,
        out_shape=(
            jax.ShapeDtypeStruct((2 * HALF, 256), jnp.bfloat16),
            jax.ShapeDtypeStruct((2, 8, 4 * HALF), jnp.float32),
        ),
        in_specs=[VMEM] * 4 + [ANY] * len(after),
        out_specs=(VMEM,) * 2,
        compiler_params=PARAMS,
        cost_estimate=cost(10e9, 2e6),
        name="long_forward",
    )(q, far, far_pos, pos, *after)


def grad_terms(q, grad, k, v, seen, lse, delta):
    weights = jnp.where(seen, jnp.exp(dot(k, q, 1, 1) - lse), 0.0)
    grad_scores = (weights * (dot(v, grad, 1, 1) - delta)).astype(jnp.bfloat16)
    return (
        dot(grad_scores, k, 0, 0),
        dot(grad_scores, q),
        dot(weights.astype(jnp.bfloat16), grad),
    )


def row_product(left, right):
    return as_row(
        jnp.sum(left.astype(jnp.float32) * right.astype(jnp.float32), axis=1, keepdims=True)
    )[:1]


def short_backward_kernel(
    qkv_ref, start_ref, attn_ref, grad_ref, lse_ref, cos_ref, sin_ref, *refs
):
    out_ref, dk_ref, dv_ref = refs[-3:]
    blocks = attn_ref.shape[0] // HALF
    scale = HEAD_DIM**-0.5
    dk_ref[...] = jnp.zeros_like(dk_ref)
    dv_ref[...] = jnp.zeros_like(dv_ref)
    for i in range(blocks):
        rows = pl.ds((i + 2) * HALF, HALF)
        keys = (i + 1) * HALF
        q = stacked(qkv_ref[rows, :256]) * jnp.bfloat16(scale)
        k = qkv_ref[pl.ds(2 * HALF, keys), 256:320]
        v = qkv_ref[pl.ds(2 * HALF, keys), 320:384]
        grad = stacked(grad_ref[rows, :])
        delta = row_product(grad, stacked(attn_ref[pl.ds(i * HALF, HALF), :]))
        key = lax.broadcasted_iota(jnp.int32, (keys, HALF), 0)
        query = lax.broadcasted_iota(jnp.int32, (keys, HALF), 1) + i * HALF
        seen = (key <= query) & (key >= start_ref[:1, pl.ds(i * HALF, HALF)])
        dq, dk, dv = grad_terms(
            q, grad, k, v, jnp.concatenate([seen] * 4, axis=1), lse_ref[i, :1], delta
        )
        cos_rows = cos_ref[rows, :]
        sin_rows = sin_ref[rows, :]
        dq = turned(
            dq * scale,
            jnp.concatenate([cos_rows] * 4, axis=0),
            jnp.concatenate([-sin_rows] * 4, axis=0),
        )
        out_ref[pl.ds(i * HALF, HALF), :256] = unstacked(dq).astype(jnp.bfloat16)
        dk_ref[pl.ds(0, keys), :] += dk
        dv_ref[pl.ds(0, keys), :] += dv
    rows = pl.ds(2 * HALF, blocks * HALF)
    dk = turned(dk_ref[...], cos_ref[rows, :], -sin_ref[rows, :])
    out_ref[:, 256:] = jnp.concatenate([dk, dv_ref[...]], axis=1).astype(jnp.bfloat16)


def short_backward(qkv, start, attn, grad, lse, cos_rows, sin_rows, after=()):
    rows = attn.shape[0]
    return pl.pallas_call(
        short_backward_kernel,
        out_shape=jax.ShapeDtypeStruct((rows, 384), jnp.bfloat16),
        in_specs=[VMEM] * 7 + [ANY] * len(after),
        out_specs=VMEM,
        scratch_shapes=[pltpu.VMEM((rows, HEAD_DIM), jnp.float32)] * 2,
        compiler_params=PARAMS,
        cost_estimate=cost(7e9, 2e6),
        name="short_backward",
    )(qkv, start, attn, grad, lse, cos_rows, sin_rows, *after)


BACK_CHUNK = 1024


def long_backward_kernel(
    q_ref, far_ref, far_pos_ref, pos_ref, attn_ref, grad_ref, lse_ref, cos_ref, sin_ref, *refs
):
    dq_ref, far_grad_ref, acc_ref = refs[-3:]
    scale = HEAD_DIM**-0.5
    acc_ref[...] = jnp.zeros_like(acc_ref)
    queries = []
    for half in range(2):
        rows = pl.ds(half * HALF, HALF)
        grad = stacked(grad_ref[rows, :])
        queries.append(
            (
                stacked(q_ref[rows, :256]) * jnp.bfloat16(scale),
                grad,
                lse_ref[half, :1],
                row_product(grad, stacked(attn_ref[rows, :])),
                jnp.concatenate([pos_ref[:1, rows]] * 4, axis=1),
            )
        )

    def step(i, carry):
        keys = pl.ds(pl.multiple_of(i * BACK_CHUNK, BACK_CHUNK), BACK_CHUNK)
        block = far_ref[keys, :]
        k, v = block[:, :HEAD_DIM], block[:, HEAD_DIM:]
        sums = []
        for half, (q, grad, lse, delta, position) in enumerate(queries):
            seen = far_pos_ref[keys, :1] <= position
            dq, dk, dv = grad_terms(q, grad, k, v, seen, lse, delta)
            acc_ref[half] += dq
            sums.append((dk, dv))
        total = jnp.concatenate(
            [sums[0][0] + sums[1][0], sums[0][1] + sums[1][1]], axis=1
        ).astype(jnp.bfloat16)
        rows = BACK_CHUNK // 4
        for k in range(4):
            far_grad_ref[k, pl.ds(pl.multiple_of(i * rows, rows), rows), :] = total[
                k * rows : (k + 1) * rows
            ]
        return carry

    lax.fori_loop(0, far_ref.shape[0] // BACK_CHUNK, step, 0)
    for half in range(2):
        rows = pl.ds(half * HALF, HALF)
        dq = turned(
            acc_ref[half] * scale,
            jnp.concatenate([cos_ref[rows, :]] * 4, axis=0),
            jnp.concatenate([-sin_ref[rows, :]] * 4, axis=0),
        )
        dq_ref[rows, :] = unstacked(dq).astype(jnp.bfloat16)


def long_backward(q, far, far_pos, pos, attn, grad, lse, cos_rows, sin_rows, after=()):
    return pl.pallas_call(
        long_backward_kernel,
        out_shape=(
            jax.ShapeDtypeStruct((2 * HALF, 256), jnp.bfloat16),
            jax.ShapeDtypeStruct((4, far.shape[0] // 4, far.shape[1]), jnp.bfloat16),
        ),
        in_specs=[VMEM] * 9 + [ANY] * len(after),
        out_specs=(VMEM,) * 2,
        scratch_shapes=[pltpu.VMEM((2, 4 * HALF, HEAD_DIM), jnp.float32)],
        compiler_params=PARAMS,
        cost_estimate=cost(13e9, 3e6),
        name="long_backward",
    )(q, far, far_pos, pos, attn, grad, lse, cos_rows, sin_rows, *after)


def weight_grad_kernel(left_ref, other_left_ref, right_ref, other_right_ref, *refs):
    out_ref, width = refs[-1], right_ref.shape[1]
    out_ref[:, :width] = (
        dot(left_ref[...], right_ref[...], 0, 0)
        + dot(other_left_ref[...], other_right_ref[...], 0, 0)
    ).astype(jnp.bfloat16)
    if out_ref.shape[1] > width:
        out_ref[:, width:] = refs[0][...]


def weight_grad(left, right, after=(), beside=()):
    tokens, width = right[0].shape
    columns = left[0].shape[1]
    whole = width + sum(array.shape[1] for array in beside)
    once = pl.BlockSpec((tokens, width), lambda i: (0, 0), pipeline_mode=pl.Buffered(1))

    def out_block(n):
        return pl.BlockSpec((columns // 8, n), lambda i: (i % 4 * 2 + i // 4, 0))

    return pl.pallas_call(
        weight_grad_kernel,
        grid=(8,),
        out_shape=jax.ShapeDtypeStruct((columns, whole), jnp.bfloat16),
        in_specs=[pl.BlockSpec((tokens, columns // 8), lambda i: (0, i))] * 2
        + [once] * 2
        + [out_block(array.shape[1]) for array in beside]
        + [ANY] * len(after),
        out_specs=out_block(whole),
        compiler_params=PARAMS,
        cost_estimate=cost(3e9 + 4 * tokens * columns * width, 4 * columns * (tokens + width)),
        name="weight_grad",
    )(*left, *right, *beside, *after)


def join_kernel(count, after, passed, *refs):
    sources = refs[:count]
    inputs = refs[count + after : count + after + passed]
    outs = refs[count + after + passed :]
    for k, ref in enumerate(sources):
        outs[0][k] = ref[...]
    for ref, out in zip(inputs, outs[1:]):
        out[...] = ref[...]


def join(pieces, after=(), passed=()):
    rows, width = pieces[0].shape
    count = len(pieces)
    block = pl.BlockSpec((rows, width // 4), lambda i: (0, i))
    joined, *copied = pl.pallas_call(
        functools.partial(join_kernel, count, len(after), len(passed)),
        grid=(4,),
        out_shape=(
            jax.ShapeDtypeStruct((count, rows, width), pieces[0].dtype),
            *[jax.ShapeDtypeStruct(array.shape, array.dtype) for array in passed],
        ),
        in_specs=[block] * count + [ANY] * len(after) + [block] * len(passed),
        out_specs=(
            pl.BlockSpec((count, rows, width // 4), lambda i: (0, 0, i)),
            *[block for _ in passed],
        ),
        compiler_params=PARAMS,
        cost_estimate=cost(1e6, 4 * count * rows * width),
        name="join",
    )(*pieces, *after, *passed)
    return (joined.reshape(count * rows, width), *copied)


def add_kernel(left_ref, right_ref, *refs):
    for k, out_ref in enumerate(refs[-4:]):
        rows = pl.ds(k * out_ref.shape[0], out_ref.shape[0])
        out_ref[...] = (
            left_ref[rows, :].astype(jnp.float32) + right_ref[rows, :].astype(jnp.float32)
        ).astype(jnp.bfloat16)


def add_parts(left, right, after=()):
    rows, width = left.shape
    return pl.pallas_call(
        add_kernel,
        grid=(4,),
        out_shape=(jax.ShapeDtypeStruct((rows // 4, width), jnp.bfloat16),) * 4,
        in_specs=[pl.BlockSpec((rows, width // 4), lambda i: (0, i))] * 2 + [ANY] * len(after),
        out_specs=(pl.BlockSpec((rows // 4, width // 4), lambda i: (0, i)),) * 4,
        compiler_params=PARAMS,
        cost_estimate=cost(1e6, 6 * rows * width),
        name="add_parts",
    )(left, right, *after)


def product_kernel(turned_right, left_ref, right_ref, *refs):
    refs[-1][...] = dot(left_ref[...], right_ref[...], 1, 1 if turned_right else 0).astype(
        jnp.bfloat16
    )


def product(left, right, after=(), turned_right=False, block=272):
    rows, depth = left.shape
    width = right.shape[0] if turned_right else right.shape[1]
    return pl.pallas_call(
        functools.partial(product_kernel, turned_right),
        grid=(rows // block,),
        out_shape=jax.ShapeDtypeStruct((rows, width), jnp.bfloat16),
        in_specs=[
            pl.BlockSpec((block, depth), lambda i: (i, 0)),
            pl.BlockSpec(right.shape, lambda i: (0, 0), pipeline_mode=pl.Buffered(1)),
        ]
        + [ANY] * len(after),
        out_specs=pl.BlockSpec((block, width), lambda i: (i, 0)),
        compiler_params=PARAMS,
        cost_estimate=cost(2 * rows * depth * width, 2 * (depth + rows) * width),
        name="product",
    )(left, right, *after)


def parts_kernel(terms, turned_right, *refs):
    outs, sent_ref = refs[-4:], refs[2 * terms]
    total = sent_ref[...].astype(jnp.float32)
    for k in range(terms):
        total += dot(refs[2 * k][...], refs[2 * k + 1][...], 1, 1 if turned_right else 0)
    rows = outs[0].shape[0]
    for k, out_ref in enumerate(outs):
        out_ref[...] = total[k * rows : (k + 1) * rows].astype(jnp.bfloat16)


def product_parts(pairs, sent, turned_right=False, after=()):
    rows, width = sent.shape
    block = width // 4
    specs = []
    for left, right in pairs:
        specs.append(pl.BlockSpec(left.shape, lambda i: (0, 0), pipeline_mode=pl.Buffered(1)))
        if turned_right:
            specs.append(pl.BlockSpec((block, right.shape[1]), lambda i: (i, 0)))
        else:
            specs.append(pl.BlockSpec((right.shape[0], block), lambda i: (0, i)))
    return pl.pallas_call(
        functools.partial(parts_kernel, len(pairs), turned_right),
        grid=(4,),
        out_shape=(jax.ShapeDtypeStruct((rows // 4, width), jnp.bfloat16),) * 4,
        in_specs=specs + [pl.BlockSpec((rows, block), lambda i: (0, i))] + [ANY] * len(after),
        out_specs=(pl.BlockSpec((rows // 4, block), lambda i: (0, i)),) * 4,
        compiler_params=PARAMS,
        cost_estimate=cost(
            sum(2 * rows * width * left.shape[1] for left, _ in pairs), 6 * rows * width
        ),
        name="product_parts",
    )(*[array for pair in pairs for array in pair], sent, *after)


def mix_kernel(tokens_ref, gain_ref, *refs):
    parts, (mixed_ref, hidden_ref) = refs[:4], refs[-2:]
    mixed = tokens_ref[...].astype(jnp.float32) + total_of([ref[...] for ref in parts])
    inv = lax.rsqrt(jnp.mean(mixed * mixed, axis=-1, keepdims=True) + EPS)
    mixed_ref[...] = mixed
    hidden_ref[...] = (mixed * inv * gain_ref[...]).astype(jnp.bfloat16)


def mix(tokens, gain, parts, after):
    rows, d = tokens.shape
    return pl.pallas_call(
        mix_kernel,
        out_shape=(
            jax.ShapeDtypeStruct((rows, d), jnp.float32),
            jax.ShapeDtypeStruct((rows, d), jnp.bfloat16),
        ),
        in_specs=[VMEM] * 6 + [ANY] * len(after),
        out_specs=(VMEM,) * 2,
        compiler_params=PARAMS,
        cost_estimate=cost(1e6, 16 * rows * d),
        name="mix",
    )(tokens, gain.reshape(1, d), *parts, *after)


def norm_back(grad_in, values, gain):
    inv = lax.rsqrt(jnp.mean(values * values, axis=-1, keepdims=True) + EPS)
    unit = values * inv
    scaled = grad_in * gain
    return inv * (scaled - unit * jnp.mean(scaled * unit, axis=-1, keepdims=True)), unit


def mix_back_kernel(grad_ref, mixed_ref, gain_ref, *refs):
    parts, (total_ref, low_ref, part_ref) = refs[:4], refs[-3:]
    grad_in = total_of([ref[...] for ref in parts])
    back, unit = norm_back(grad_in, mixed_ref[...], gain_ref[...])
    total = grad_ref[...].astype(jnp.float32) + back
    total_ref[...] = total
    low_ref[...] = total.astype(jnp.bfloat16)
    part_ref[...] = jnp.sum(grad_in * unit, axis=0, keepdims=True)


def mix_back(grad, mixed, gain, parts, after):
    rows, d = grad.shape
    return pl.pallas_call(
        mix_back_kernel,
        out_shape=(
            jax.ShapeDtypeStruct((rows, d), jnp.float32),
            jax.ShapeDtypeStruct((rows, d), jnp.bfloat16),
            jax.ShapeDtypeStruct((1, d), jnp.float32),
        ),
        in_specs=[VMEM] * 7 + [ANY] * len(after),
        out_specs=(VMEM,) * 3,
        compiler_params=PARAMS,
        cost_estimate=cost(1e6, 20 * rows * d),
        name="mix_back",
    )(grad, mixed, gain.reshape(1, d), *parts, *after)


def hidden_grad_kernel(with_sent, low_ref, query_ref, kv_ref, hidden_ref, *refs):
    low = low_ref[...]
    grad = dot(low[:, :256], query_ref[...], 1, 1) + dot(low[:, 256:], kv_ref[...], 1, 1)
    refs[-1][...] = jnp.sum(grad * hidden_ref[...].astype(jnp.float32), axis=0, keepdims=True)
    if with_sent:
        grad += refs[0][...].astype(jnp.float32)
        rows = refs[1].shape[0]
        for k, out_ref in enumerate(refs[1:-1]):
            out_ref[...] = grad[k * rows : (k + 1) * rows].astype(jnp.bfloat16)
    else:
        refs[0][...] = grad.astype(jnp.bfloat16)


def hidden_grad(low, w_query, w_key_value, hidden, sent=None, after=()):
    rows, d = hidden.shape
    block = d // 4
    wide = pl.BlockSpec((rows, block), lambda i: (0, i))
    gain = jax.ShapeDtypeStruct((1, d), jnp.float32)
    if sent is None:
        shapes = (jax.ShapeDtypeStruct((rows, d), jnp.bfloat16), gain)
        outs, extra = (wide,), ()
    else:
        shapes = (jax.ShapeDtypeStruct((rows // 4, d), jnp.bfloat16),) * 4 + (gain,)
        outs, extra = (pl.BlockSpec((rows // 4, block), lambda i: (0, i)),) * 4, (sent,)

    def kernel(*refs):
        refs = refs[: 4 + len(extra)] + refs[4 + len(extra) + len(after) :]
        hidden_grad_kernel(sent is not None, *refs)

    return pl.pallas_call(
        kernel,
        grid=(4,),
        out_shape=shapes,
        in_specs=[
            pl.BlockSpec((rows, 384), lambda i: (0, 0), pipeline_mode=pl.Buffered(1)),
            pl.BlockSpec((block, 256), lambda i: (i, 0)),
            pl.BlockSpec((block, 128), lambda i: (i, 0)),
            wide,
        ]
        + [wide] * len(extra)
        + [ANY] * len(after),
        out_specs=outs + (pl.BlockSpec((1, block), lambda i: (0, i)),),
        compiler_params=PARAMS,
        cost_estimate=cost(2 * rows * d * 384, 4 * rows * d),
        name="hidden_grad",
    )(low, w_query, w_key_value, hidden, *extra, *after)


def mlp_kernel(hidden_ref, grad_act_ref, gate_ref, up_ref, act_ref, both_ref, *refs):
    hidden = hidden_ref[...]
    gate = dot(hidden, gate_ref[...])
    up = dot(hidden, up_ref[...])
    grad_act = grad_act_ref[...].astype(jnp.float32)
    sig = jax.nn.sigmoid(gate)
    silu = gate * sig
    act_ref[...] = (silu * up).astype(jnp.bfloat16)
    grad_gate = (grad_act * up * sig * (1.0 + gate * (1.0 - sig))).astype(jnp.bfloat16)
    grad_up = (grad_act * silu).astype(jnp.bfloat16)
    width = gate.shape[1]
    both_ref[:, :width] = grad_gate
    both_ref[:, width:] = grad_up
    if refs:
        refs[0][...] = (
            dot(grad_gate, gate_ref[...], 1, 1) + dot(grad_up, up_ref[...], 1, 1)
        ).astype(jnp.bfloat16)


def mlp(hidden, grad_act, w_gate, w_up, with_back):
    rows, d = hidden.shape
    block = rows // 2
    width = w_gate.shape[1]
    widths = (width, 2 * width) + ((d,) if with_back else ())
    return pl.pallas_call(
        mlp_kernel,
        grid=(rows // block,),
        out_shape=tuple(jax.ShapeDtypeStruct((rows, n), jnp.bfloat16) for n in widths),
        in_specs=[
            pl.BlockSpec((block, d), lambda i: (i, 0)),
            pl.BlockSpec((block, width), lambda i: (i, 0)),
            pl.BlockSpec((d, width), lambda i: (0, 0), pipeline_mode=pl.Buffered(1)),
            pl.BlockSpec((d, width), lambda i: (0, 0), pipeline_mode=pl.Buffered(1)),
        ],
        out_specs=tuple(pl.BlockSpec((block, n), lambda i: (i, 0)) for n in widths),
        compiler_params=PARAMS,
        cost_estimate=cost((8 if with_back else 4) * rows * width * d, 12 * rows * d),
        name="mlp",
    )(hidden, grad_act, w_gate, w_up)


def qkv_kernel(hidden_ref, query_ref, kv_ref, cos_ref, sin_ref, out_ref):
    hidden = hidden_ref[...]
    query = dot(hidden, query_ref[...])
    kv = dot(hidden, kv_ref[...])
    cos_rows, sin_rows = cos_ref[...], sin_ref[...]
    heads = [
        turned(query[:, h * HEAD_DIM : (h + 1) * HEAD_DIM], cos_rows, sin_rows) for h in range(4)
    ]
    heads += [turned(kv[:, :HEAD_DIM], cos_rows, sin_rows), kv[:, HEAD_DIM:]]
    out_ref[...] = jnp.concatenate(heads, axis=1).astype(jnp.bfloat16)


def project_qkv(hidden, w_query, w_key_value, cos_rows, sin_rows, block=272):
    rows, d = hidden.shape
    return pl.pallas_call(
        qkv_kernel,
        grid=(rows // block,),
        out_shape=jax.ShapeDtypeStruct((rows, 384), jnp.bfloat16),
        in_specs=[
            pl.BlockSpec((block, d), lambda i: (i, 0)),
            pl.BlockSpec((d, 256), lambda i: (0, 0), pipeline_mode=pl.Buffered(1)),
            pl.BlockSpec((d, 128), lambda i: (0, 0), pipeline_mode=pl.Buffered(1)),
            pl.BlockSpec((block, HEAD_DIM), lambda i: (i, 0)),
            pl.BlockSpec((block, HEAD_DIM), lambda i: (i, 0)),
        ],
        out_specs=pl.BlockSpec((block, 384), lambda i: (i, 0)),
        compiler_params=PARAMS,
        cost_estimate=cost(4 * rows * d * 384, 4 * rows * d),
        name="project_qkv",
    )(hidden, w_query, w_key_value, cos_rows, sin_rows)


def all_sum(values):
    for group in ((CORE,), (X_UP, X_DOWN, X_FAR), (Z_UP, Z_DOWN, Z_FAR), (Y_LOW, Y_HIGH, Y_FAR)):
        values = sum([send(values, pairs) for pairs in group], values)
    return values


def local(
    tokens,
    lengths,
    place,
    attn_gain,
    w_query,
    w_key,
    w_value,
    w_out,
    mlp_gain,
    w_gate,
    w_up,
    w_down,
    out_grad,
):
    rows = tokens.shape[0]
    group_rows = rows * 8
    half_rows = rows * 4
    long_rows = 2 * HALF
    padded_rows = -(-group_rows // HALF) * HALF
    dp_index, mp_index = lax.axis_index("dp"), lax.axis_index("mp")
    yh, z, core = dp_index // 8, dp_index // 2 % 4, dp_index % 2
    yl, x = mp_index // 4, mp_index % 4
    native = core == yl

    tokens = send(tokens, TURN)
    lengths = send(lengths, TURN)[0]
    w_key_value = send(jnp.concatenate([w_key, w_value], axis=1), WEIGHT_HIGH)
    w_query = send(w_query, WEIGHT_LOW)
    w_out = send(w_out, WEIGHT_HIGH)
    w_gate = send(w_gate, WEIGHT_LOW)
    w_up = send(w_up, WEIGHT_HIGH)
    w_down = send(w_down, WEIGHT_LOW)
    out_grad = send(out_grad, TURN)

    group = (yh * 4 + z) * 2 + yl
    half_ids = jnp.arange(place.shape[0], dtype=jnp.int32)

    def place_at(index):
        return jnp.sum(jnp.where(half_ids == index[..., None], place, 0), axis=-1)

    def position_of(row):
        packed = row - long_rows
        first, second = lengths[0], lengths[0] + lengths[1]
        start = jnp.where(packed >= second, second, jnp.where(packed >= first, first, 0))
        start = jnp.where(row >= group_rows, packed, start)
        own = jnp.where(row < HALF, place_at(2 * group), place_at(2 * group + 1))
        return jnp.where(row < long_rows, own * HALF + row % HALF, packed - start), start

    def tables(position):
        angles = position.astype(jnp.float32)[:, None] * inverse_freq(HEAD_DIM)[None, :]
        cos_rows, sin_rows = jnp.cos(angles), jnp.sin(angles)
        return (
            jnp.concatenate([cos_rows, cos_rows], axis=1),
            jnp.concatenate([-sin_rows, sin_rows], axis=1),
        )

    ordered_rows = jnp.arange(padded_rows, dtype=jnp.int32)
    ordered_pos, ordered_start = position_of(ordered_rows)
    cos_ordered, sin_ordered = tables(ordered_pos)
    index = jnp.arange(group_rows, dtype=jnp.int32)
    shard = jnp.where(index < half_rows, core, 1 - core) * 4 + (x + index % half_rows // rows) % 4
    cos_gathered, sin_gathered = tables(position_of(shard * rows + index % rows)[0])
    starts = ordered_start[long_rows:]
    start_column = jnp.broadcast_to(starts[:, None], (starts.shape[0], 128))
    start_row = jnp.broadcast_to(starts[None, :], (8, starts.shape[0]))
    long_pos = ordered_pos[:long_rows]
    pos_column = jnp.broadcast_to(long_pos[:, None], (long_rows, 128))
    pos_row = jnp.broadcast_to(long_pos[None, :], (8, long_rows))
    step = jnp.arange(16, dtype=jnp.int32)
    far_yh = jnp.where(step % 4 >= 2, 1 - yh, yh)
    far_yl = jnp.where((step % 4 == 1) | (step % 4 == 2), 1 - yl, yl)
    far_group = (far_yh * 4 + (z + step // 4) % 4) * 2 + far_yl
    far_half = place_at(2 * far_group[:, None] + jnp.arange(2, dtype=jnp.int32)[None, :])
    far_pos = (
        far_half.reshape(-1, 1) * HALF + jnp.arange(HALF, dtype=jnp.int32)[None, :]
    ).reshape(-1)
    far_row = jnp.broadcast_to(far_pos.reshape(-1, 1, CHUNK), (far_pos.shape[0] // CHUNK, 8, CHUNK))
    far_column = jnp.broadcast_to(far_pos[:, None], (far_pos.shape[0], 128))

    residual = tokens.astype(jnp.float32)
    inv_one = lax.rsqrt(jnp.mean(residual * residual, axis=-1, keepdims=True) + EPS)
    hidden_one = (residual * inv_one * attn_gain).astype(jnp.bfloat16)
    *hidden_one, grad_copy = gather(hidden_one, (w_query, w_key_value), (out_grad,))
    qkv = in_order(
        *[
            project_qkv(half, w_query, w_key_value, cos_rows, sin_rows)
            for half, cos_rows, sin_rows in zip(
                hidden_one,
                (cos_gathered[:half_rows], cos_gathered[half_rows:]),
                (sin_gathered[:half_rows], sin_gathered[half_rows:]),
            )
        ],
        core,
        x,
    )
    qkv = jnp.pad(qkv, ((0, padded_rows - group_rows), (0, 0)))
    near_rows = qkv[:long_rows, 256:]
    ring_rows = jnp.concatenate(
        [near_rows, send(near_rows, Y_LOW), send(near_rows, Y_HIGH), send(near_rows, Y_FAR)]
    )
    far_rows = jnp.concatenate(
        [ring_rows, send(ring_rows, Z_DOWN), send(ring_rows, Z_FAR), send(ring_rows, Z_UP)]
    )
    grad_rows = from_order(
        lax.all_gather(grad_copy, BOTH, axis=0, tiled=True, axis_index_groups=CHIP_GROUPS), core, x
    )
    long_q = qkv[:long_rows]
    short_attn, short_lse = short_forward(qkv, start_column)
    long_attn, long_lse = long_forward(
        long_q, far_rows, far_row, pos_column, (w_down, w_out)
    )
    attn_rows = from_order(
        jnp.concatenate([long_attn, short_attn[: group_rows - long_rows]]), core, x
    )
    sent = send(product(attn_rows[1], w_out), CORE)
    parts = product_parts([(attn_rows[0], w_out)], sent)
    mixed_parts = scatter(parts)
    grad_act = [product(half, w_down, parts[:1], True) for half in grad_rows]
    mixed, hidden_two = mix(tokens, mlp_gain, mixed_parts, (*grad_act, w_gate, w_up))
    hidden_two = gather(hidden_two)

    act_other, both_other, back = mlp(hidden_two[1], grad_act[1], w_gate, w_up, True)
    act_own, both_own = mlp(hidden_two[0], grad_act[0], w_gate, w_up, False)
    act, grad_both, ff = (act_own, act_other), (both_own, both_other), act_own.shape[1]
    parts = product_parts(
        [(both_own[:, :ff], w_gate), (both_own[:, ff:], w_up)], send(back, CORE), True
    )
    hidden_parts = scatter(parts)
    down_part = weight_grad(grad_rows, act, parts[:1])
    both_part = weight_grad(hidden_two, grad_both, (down_part,))
    down_sum = sum_groups(down_part, yh, core, native).T
    both_sum = sum_groups(both_part, yh, core, native)

    grad_mixed, grad_low, mlp_gain_part = mix_back(
        out_grad, mixed, mlp_gain, hidden_parts, (both_part,)
    )
    down_rows = [product(half, w_down, (grad_low,)) for half in act]
    mixed_grad_rows = gather(grad_low, down_rows)
    grad_attn = in_order(
        *[dot(half, w_out, 1, 1).astype(jnp.bfloat16) for half in mixed_grad_rows], core, x
    )
    out_parts = add_parts(down_rows[0], send(down_rows[1], CORE), mixed_grad_rows[1:])
    output = mixed + total_of(scatter(out_parts))
    output = send(output.astype(jnp.bfloat16), TURN)
    grad_attn = jnp.pad(grad_attn, ((0, padded_rows - group_rows), (0, 0)))
    long_dq, far_terms = long_backward(
        long_q,
        far_rows,
        far_column,
        pos_row,
        long_attn,
        grad_attn[:long_rows],
        long_lse,
        cos_ordered[:long_rows],
        sin_ordered[:long_rows],
        out_parts[:1],
    )
    ring_terms = total_of(
        (
            far_terms[0],
            send(far_terms[1], Y_LOW),
            send(far_terms[2], Y_HIGH),
            send(far_terms[3], Y_FAR),
        )
    ).astype(jnp.bfloat16)
    near = ring_terms.reshape(4, long_rows, -1)
    far_grads = total_of(
        (near[0], send(near[1], Z_UP), send(near[2], Z_FAR), send(near[3], Z_DOWN))
    )
    out_part = weight_grad(mixed_grad_rows, attn_rows, (long_dq,))
    short_low = short_backward(
        qkv, start_row, short_attn, grad_attn, short_lse, cos_ordered, sin_ordered, (out_part,)
    )
    long_dk = turned(far_grads[:, :HEAD_DIM], cos_ordered[:long_rows], -sin_ordered[:long_rows])
    long_low = jnp.concatenate(
        [
            long_dq,
            long_dk.astype(jnp.bfloat16),
            far_grads[:, HEAD_DIM:].astype(jnp.bfloat16),
        ],
        axis=1,
    )
    low_rows = from_order(
        jnp.concatenate([long_low, short_low[: group_rows - long_rows]]), core, x
    )
    back, gain_other = hidden_grad(low_rows[1], w_query, w_key_value, hidden_one[1])
    last_part = weight_grad(hidden_one, low_rows, (back,), (out_part,))
    *parts, gain_own = hidden_grad(
        low_rows[0], w_query, w_key_value, hidden_one[0], send(back, CORE), (last_part,)
    )
    grad_parts = scatter(parts)
    gains = all_sum(jnp.concatenate([(gain_own + gain_other) / attn_gain, mlp_gain_part]))
    last_sum = sum_groups(last_part, yh, core, native)
    qkv_sum, out_sum = last_sum[:, :384], last_sum[:, 384:].T
    grad_tokens = grad_mixed + norm_back(total_of(grad_parts), residual, attn_gain)[0]
    grad_tokens = send(grad_tokens.astype(jnp.bfloat16), TURN)
    return (
        output,
        grad_tokens,
        gains[0],
        qkv_sum[:, :256],
        qkv_sum[:, 256:320],
        qkv_sum[:, 320:],
        out_sum,
        gains[1],
        both_sum[:, :ff],
        both_sum[:, ff:],
        down_sum,
    )


def solution(mesh):
    placed = (
        P(("dp", "mp"), None),
        P("dp", None),
        P(),
        P(),
        P(None, "mp"),
        P(None, "mp"),
        P(None, "mp"),
        P("mp", None),
        P(),
        P(None, "mp"),
        P(None, "mp"),
        P("mp", None),
        P(("dp", "mp"), None),
    )
    return jax.shard_map(
        local,
        mesh=mesh,
        in_specs=placed,
        out_specs=(
            P(("dp", "mp"), None),
            P(("dp", "mp"), None),
            P(),
            P("dp", "mp"),
            P("dp", "mp"),
            P("dp", "mp"),
            P("mp", "dp"),
            P(),
            P("dp", "mp"),
            P("dp", "mp"),
            P("mp", "dp"),
        ),
        check_vma=False,
    )
```

```python
import functools

import jax
import jax.numpy as jnp
from jax import lax
from jax.experimental import pallas as pl
from jax.experimental.pallas import tpu as pltpu
from jax.sharding import PartitionSpec as P

HEAD_DIM = 64
HALF = 128
MASKED = -1e30


EPS = 1e-05
THETA = 500000.0

BOTH = ("dp", "mp")


def place_of(yh, z, c, yl, x):
    return ((yh * 4 + z) * 2 + c) * 8 + yl * 4 + x


def pairs_of(target, sender=lambda yh, z, c, yl, x: True):
    return [
        (place_of(yh, z, c, yl, x), place_of(*target(yh, z, c, yl, x)))
        for yh in range(2)
        for z in range(4)
        for c in range(2)
        for yl in range(2)
        for x in range(4)
        if sender(yh, z, c, yl, x)
    ]


X_UP = pairs_of(lambda yh, z, c, yl, x: (yh, z, c, yl, (x + 1) % 4))
X_DOWN = pairs_of(lambda yh, z, c, yl, x: (yh, z, c, yl, (x + 3) % 4))
X_FAR = pairs_of(lambda yh, z, c, yl, x: (yh, z, c, yl, (x + 2) % 4))
Z_UP = pairs_of(lambda yh, z, c, yl, x: (yh, (z + 1) % 4, c, yl, x))
Z_DOWN = pairs_of(lambda yh, z, c, yl, x: (yh, (z + 3) % 4, c, yl, x))
Z_FAR = pairs_of(lambda yh, z, c, yl, x: (yh, (z + 2) % 4, c, yl, x))
CORE = pairs_of(lambda yh, z, c, yl, x: (yh, z, 1 - c, yl, x))
Y_LOW = pairs_of(lambda yh, z, c, yl, x: (yh, z, c, 1 - yl, x))
Y_HIGH = pairs_of(lambda yh, z, c, yl, x: (1 - yh, z, c, 1 - yl, x))
Y_FAR = pairs_of(lambda yh, z, c, yl, x: (1 - yh, z, c, yl, x))
TURN = pairs_of(lambda yh, z, c, yl, x: (yh, z, yl, c, x))
NATIVE = lambda yh, z, c, yl, x: c == yl
FOREIGN = lambda yh, z, c, yl, x: c != yl
FOREIGN_LOW = pairs_of(lambda yh, z, c, yl, x: (yh, z, c, 1 - yl, x), FOREIGN)
FOREIGN_HIGH = pairs_of(lambda yh, z, c, yl, x: (1 - yh, z, c, 1 - yl, x), FOREIGN)
NATIVE_LOW = pairs_of(lambda yh, z, c, yl, x: (yh, z, c, 1 - yl, x), NATIVE)
NATIVE_HIGH = pairs_of(lambda yh, z, c, yl, x: (1 - yh, z, c, 1 - yl, x), NATIVE)
NATIVE_CORE = pairs_of(lambda yh, z, c, yl, x: (yh, z, 1 - c, yl, x), NATIVE)
WEIGHT_LOW = pairs_of(
    lambda yh, z, c, yl, x: (yh, z, c, 1 - yl, x) if c == yl else (yh, z, 1 - c, yl, x)
)
WEIGHT_HIGH = pairs_of(
    lambda yh, z, c, yl, x: (1 - yh, z, c, 1 - yl, x) if c == yl else (yh, z, 1 - c, yl, x)
)
Z_GROUPS = [
    [place_of(yh, z, c, yl, x) for z in range(4)]
    for yh in range(2)
    for c in range(2)
    for yl in range(2)
    for x in range(4)
]


Y_GROUPS = [
    [place_of(yh, z, c, yl, x) for yh in range(2) for yl in range(2)]
    for z in range(4)
    for c in range(2)
    for x in range(4)
]
CHIP_GROUPS = [
    [place_of(yh, z, c, yl, x) for c in range(2) for x in range(4)]
    for yh in range(2)
    for z in range(4)
    for yl in range(2)
]


def send(values, pairs):
    return lax.ppermute(values, BOTH, pairs)


CHUNKS = ((0, 136),)

VMEM = pl.BlockSpec(memory_space=pltpu.VMEM)
SMEM = pl.BlockSpec(memory_space=pltpu.SMEM)
ANY = pl.BlockSpec(memory_space=pl.ANY)
PARAMS = pltpu.CompilerParams(vmem_limit_bytes=64 * 1024 * 1024)
LASTS = {
    "tables": 6,
    "join": 4,
    "project_qkv": 4,
    "copied": 3,
    "short_forward": 6,
    "long_forward": 13,
    "product": 3,
    "product_parts": 5,
    "arrange": 5,
    "mix": 3,
    "mlp": 10,
    "weight_grad": 5,
    "mix_back": 4,
    "merged_product": 4,
    "merged_back": 3,
    "long_backward": 16,
    "short_backward": 10,
    "turn_far": 2,
    "hidden_grad": 5,
    "gains": 2,
    "gated": 1,
}


def cost(name):
    return pl.CostEstimate(
        flops=int(1.15e9 * LASTS[name]), bytes_accessed=1000, transcendentals=0
    )


def shaped(shape, dtype=jnp.bfloat16):
    return pltpu.HBM(tuple(shape), dtype)


def rows_of(block, width):
    return pl.BlockSpec((block, width), lambda i: (i, 0))


def columns_of(rows, block):
    return pl.BlockSpec((rows, block), lambda i: (0, i))


def once(shape):
    return pl.BlockSpec(tuple(shape), lambda i: (0,) * len(shape), pipeline_mode=pl.Buffered(1))


class Line:
    def __init__(self):
        self.last = ()

    def __call__(self, name, kernel, operands, in_specs, outs, out_specs, scratch=(), **grid):
        after = self.last
        count = len(operands)

        def ordered(*refs):
            kernel(*refs[:count], *refs[count + len(after) :])

        results = pl.pallas_call(
            ordered,
            out_shape=tuple(outs),
            in_specs=list(in_specs) + [ANY] * len(after),
            out_specs=tuple(out_specs),
            scratch_shapes=list(scratch),
            compiler_params=PARAMS,
            cost_estimate=cost(name),
            name=name,
            **grid,
        )(*operands, *after)
        self.last = (min(results, key=lambda array: array.size),)
        return results


def dot(left, right, left_dim=1, right_dim=0):
    return lax.dot_general(
        left, right, (((left_dim,), (right_dim,)), ((), ())), preferred_element_type=jnp.float32
    )


def total_of(parts):
    one, two, three, four = [part.astype(jnp.float32) for part in parts]
    return (one + two) + (three + four)


def scatter(parts):
    return (
        parts[0],
        send(parts[1], X_UP),
        send(parts[2], X_FAR),
        send(parts[3], X_DOWN),
    )


def collect(rows):
    return (rows, send(rows, X_DOWN), send(rows, X_FAR), send(rows, X_UP))


def in_order(pair, core, x):
    half = pair.shape[1]
    start = (4 - x) % 4 * (half // 4)
    pair = lax.dynamic_slice_in_dim(jnp.concatenate([pair, pair], axis=1), start, half, axis=1)
    return jnp.where(core == 0, pair, pair[::-1]).reshape(2 * half, -1)


def from_order(values, core, x):
    half = values.shape[0] // 2
    pair = values.reshape(2, half, -1)
    pair = jnp.where(core == 0, pair, pair[::-1])
    return lax.dynamic_slice_in_dim(
        jnp.concatenate([pair, pair], axis=1), x * (half // 4), half, axis=1
    )


def chunks_of(half):
    cut = half.reshape(4, half.shape[0] // 4, -1)
    return [cut[:, low:high].reshape(4 * (high - low), -1) for low, high in CHUNKS]


def plus(left, right):
    return (left.astype(jnp.float32) + right.astype(jnp.float32)).astype(jnp.bfloat16)


def reduce_near(grad):
    return lax.psum_scatter(
        grad, BOTH, scatter_dimension=0, tiled=True, axis_index_groups=Z_GROUPS
    )


def reduce_y(kept):
    kept = lax.psum_scatter(
        kept, BOTH, scatter_dimension=0, tiled=True, axis_index_groups=Y_GROUPS
    )
    return send(kept, TURN).astype(jnp.float32)


def reduce_ring(grad, z):
    grad = grad.reshape(4, -1, grad.shape[1])
    here, above, far, below = [
        lax.dynamic_index_in_dim(grad, (z + k) % 4, 0, False) for k in range(4)
    ]
    rows = far.shape[0] // 2
    from_below, from_above = send(far[:rows], Z_UP), send(far[rows:], Z_DOWN)
    above = send(jnp.concatenate([plus(above[:rows], from_below), above[rows:]]), Z_UP)
    below = send(jnp.concatenate([below[:rows], plus(below[rows:], from_above)]), Z_DOWN)
    return (
        here.astype(jnp.float32) + above.astype(jnp.float32) + below.astype(jnp.float32)
    ).astype(jnp.bfloat16)


def sum_groups(kept, yh, core, native):
    kept = kept.reshape(2, -1, kept.shape[1])
    near = jnp.where(yh == 0, kept[0], kept[1])
    far = jnp.where(yh == 0, kept[1], kept[0])
    rows = near.shape[0] // 2
    by_low = send(far[:rows], NATIVE_LOW)
    by_high = send(far[rows:], NATIVE_HIGH)
    low = send(jnp.concatenate([near[:rows], plus(near[rows:], by_high)]), FOREIGN_LOW)
    high = send(jnp.concatenate([plus(far[:rows], by_low), far[rows:]]), FOREIGN_HIGH)
    total = near.astype(jnp.float32) + low.astype(jnp.float32) + high.astype(jnp.float32)
    mine = jnp.where(core == 0, total[:rows], total[rows:])
    theirs = jnp.where(core == 0, total[rows:], total[:rows])
    passed = send(theirs.astype(jnp.bfloat16), NATIVE_CORE).astype(jnp.float32)
    return jnp.where(native, mine, passed), (low, high)


def all_sum(values):
    for group in ((CORE,), (X_UP, X_DOWN, X_FAR), (Z_UP, Z_DOWN, Z_FAR), (Y_LOW, Y_HIGH, Y_FAR)):
        values = sum([send(values, pairs) for pairs in group], values)
    return values


def inverse_freq(head_width):
    indices = jnp.arange(head_width // 2, dtype=jnp.float32)
    base_freq = jnp.exp(-jnp.log(THETA) * 2.0 * indices / head_width)
    wavelength = 2.0 * jnp.pi / base_freq
    smooth = (8192.0 / wavelength - 1.0) / 3.0
    blended = (1.0 - smooth) * base_freq / 32.0 + smooth * base_freq
    return jnp.where(
        wavelength < 2048.0, base_freq, jnp.where(wavelength > 8192.0, base_freq / 32.0, blended)
    )


FIRST_PLACE, SECOND_START, THIRD_START, CORE_AT, X_AT, FAR_PLACE = 0, 2, 3, 4, 5, 6


def tables_kernel(rows, facts_ref, freq_ref, *out_refs):
    sign = jnp.where(lax.broadcasted_iota(jnp.int32, (1, 128), 1) % 64 < 32, -1.0, 1.0)
    group_rows, half_rows = rows * 8, rows * 4
    for gathered, (cos_ref, sin_ref) in enumerate((out_refs[:2], out_refs[2:])):
        row = lax.broadcasted_iota(jnp.int32, cos_ref.shape, 0)
        if gathered == 0:
            other = (row >= half_rows).astype(jnp.int32)
            rest = row - other * half_rows
            step = sum([(rest >= k * rows).astype(jnp.int32) for k in (1, 2, 3)])
            core = jnp.where(other == 0, facts_ref[CORE_AT], 1 - facts_ref[CORE_AT])
            row = core * half_rows + ((facts_ref[X_AT] + step) & 3) * rows + rest - step * rows
        packed = row - 2 * HALF
        second, third = facts_ref[SECOND_START], facts_ref[THIRD_START]
        start = jnp.where(packed >= third, third, jnp.where(packed >= second, second, 0))
        own = jnp.where(row < HALF, facts_ref[FIRST_PLACE], facts_ref[FIRST_PLACE + 1])
        position = jnp.where(row < 2 * HALF, own * HALF + (row & (HALF - 1)), packed - start)
        angles = position.astype(jnp.float32) * freq_ref[...]
        cos_ref[...] = jnp.cos(angles)
        sin_ref[...] = jnp.sin(angles) * sign


def turned(values, cos_rows, sin_rows):
    first = lax.broadcasted_iota(jnp.int32, (1, 128), 1) % 64 < 32
    tiles = []
    for at in range(0, values.shape[1], 128):
        tile = values[:, at : at + 128]
        swapped = jnp.where(first, pltpu.roll(tile, 96, 1), pltpu.roll(tile, 32, 1))
        tiles.append(tile * cos_rows + swapped * sin_rows)
    return tiles[0] if len(tiles) == 1 else jnp.concatenate(tiles, axis=1)


def turned_key(values, cos_rows, sin_rows):
    key = lax.broadcasted_iota(jnp.int32, (1, 128), 1) < HEAD_DIM
    return jnp.where(key, turned(values, cos_rows, sin_rows), values)


def join_kernel(count, *refs):
    for k in range(count):
        refs[-1][k] = refs[k][...]


def join(line, pieces):
    count = len(pieces)
    rows, width = pieces[0].shape
    block = width // 4
    (joined,) = line(
        "join",
        functools.partial(join_kernel, count),
        pieces,
        [columns_of(rows, block)] * count,
        [shaped((count, rows, width))],
        [pl.BlockSpec((count, rows, block), lambda i: (0, 0, i))],
        grid=(4,),
    )
    return joined.reshape(count * rows, width)


def qkv_kernel(hidden_ref, query_ref, kv_ref, cos_ref, sin_ref, out_ref):
    hidden = hidden_ref[...]
    cos_rows, sin_rows = cos_ref[...], sin_ref[...]
    out_ref[:, :256] = turned(dot(hidden, query_ref[...]), cos_rows, sin_rows).astype(jnp.bfloat16)
    out_ref[:, 256:] = turned_key(dot(hidden, kv_ref[...]), cos_rows, sin_rows).astype(
        jnp.bfloat16
    )


def project_qkv(line, hidden, w_query, w_key_value, cos_rows, sin_rows, at):
    rows, d = hidden.shape
    block = rows // 2
    table = pl.BlockSpec((block, 128), lambda i: (i + 2 * at, 0))
    return line(
        "project_qkv",
        qkv_kernel,
        (hidden, w_query, w_key_value, cos_rows, sin_rows),
        [rows_of(block, d), once((d, 256)), once((d, 128)), table, table],
        [shaped((rows, 384))],
        [rows_of(block, 384)],
        grid=(2,),
    )[0]


def stacked(block):
    return jnp.concatenate(
        [block[:, h * HEAD_DIM : (h + 1) * HEAD_DIM] for h in range(4)], axis=0
    )


def unstacked(block):
    rows = block.shape[0] // 4
    return jnp.concatenate([block[h * rows : (h + 1) * rows] for h in range(4)], axis=1)


def as_row(column):
    return jnp.transpose(jnp.broadcast_to(column, (column.shape[0], 128)))[:8]


def start_of(row, facts_ref, pack_rows):
    second, third = facts_ref[SECOND_START], facts_ref[THIRD_START]
    start = jnp.where(row >= third, third, jnp.where(row >= second, second, 0))
    return jnp.where(row >= pack_rows, pack_rows, start)


def short_forward_kernel(pack_rows, qkv_ref, facts_ref, attn_ref, lse_ref):
    for i in range(attn_ref.shape[0] // HALF):
        rows = pl.ds((i + 2) * HALF, HALF)
        keys = (i + 1) * HALF
        q = stacked(qkv_ref[rows, :256]) * jnp.bfloat16(HEAD_DIM**-0.5)
        k = qkv_ref[pl.ds(2 * HALF, keys), 256:320]
        v = qkv_ref[pl.ds(2 * HALF, keys), 320:384]
        scores = dot(q, k, 1, 1)
        column = lax.broadcasted_iota(jnp.int32, (HALF, keys), 1)
        row = lax.broadcasted_iota(jnp.int32, (HALF, 1), 0) + i * HALF
        seen = (column <= row) & (column >= start_of(row, facts_ref, pack_rows))
        scores = jnp.where(jnp.concatenate([seen] * 4, axis=0), scores, MASKED)
        top = jnp.max(scores, axis=1, keepdims=True)
        weights = jnp.exp(scores - top)
        total = jnp.sum(weights, axis=1, keepdims=True)
        out = dot(weights.astype(jnp.bfloat16), v) / total
        attn_ref[pl.ds(i * HALF, HALF), :] = unstacked(out).astype(jnp.bfloat16)
        lse_ref[i] = as_row(top + jnp.log(total))


def short_forward(line, qkv, facts, pack_rows):
    rows = qkv.shape[0] - 2 * HALF
    return line(
        "short_forward",
        functools.partial(short_forward_kernel, pack_rows),
        (qkv, facts),
        [VMEM, SMEM],
        [shaped((rows, 256)), shaped((rows // HALF, 8, 4 * HALF), jnp.float32)],
        [VMEM] * 2,
    )


def long_forward_kernel(q_ref, *refs):
    far_refs, (facts_ref, short_ref, attn_ref, lse_ref) = refs[:4], refs[4:]
    within = lax.broadcasted_iota(jnp.int32, (1, HALF), 1)
    blocks = far_refs[0].shape[0] // HALF
    for half in range(2):
        rows = pl.ds(half * HALF, HALF)
        q = stacked(q_ref[rows, :256]) * jnp.bfloat16(HEAD_DIM**-0.5)
        row = lax.broadcasted_iota(jnp.int32, (HALF, 1), 0)
        position = jnp.concatenate([row + facts_ref[FIRST_PLACE + half] * HALF] * 4, axis=0)
        top = jnp.full((4 * HALF, 1), MASKED, jnp.float32)
        total = jnp.zeros((4 * HALF, 1), jnp.float32)
        out = jnp.zeros((4 * HALF, HEAD_DIM), jnp.float32)
        for i, far_ref in enumerate(far_refs):
            scores = dot(q, far_ref[:, :HEAD_DIM], 1, 1)
            key = jnp.concatenate(
                [within + facts_ref[FAR_PLACE + i * blocks + k] * HALF for k in range(blocks)],
                axis=1,
            )
            seen = key <= position
            scores = jnp.where(seen, scores, MASKED)
            now = jnp.maximum(top, jnp.max(scores, axis=1, keepdims=True))
            weights = jnp.where(seen, jnp.exp(scores - now), 0.0)
            scale = jnp.exp(top - now)
            total = total * scale + jnp.sum(weights, axis=1, keepdims=True)
            out = out * scale + dot(weights.astype(jnp.bfloat16), far_ref[:, HEAD_DIM:])
            top = now
        attn_ref[rows, :] = unstacked(out / total).astype(jnp.bfloat16)
        lse_ref[half] = as_row(top + jnp.log(total))
    packed = attn_ref.shape[0] - 2 * HALF
    attn_ref[pl.ds(2 * HALF, packed), :] = short_ref[pl.ds(0, packed), :]


def long_forward(line, q, far, facts, short, rows):
    return line(
        "long_forward",
        long_forward_kernel,
        (q, *far, facts, short),
        [VMEM] * 5 + [SMEM, VMEM],
        [shaped((rows, 256)), shaped((2, 8, 4 * HALF), jnp.float32)],
        [VMEM] * 2,
    )


def grad_terms(q, grad, k, v, seen, lse, delta):
    weights = jnp.where(seen, jnp.exp(dot(k, q, 1, 1) - lse), 0.0)
    grad_scores = (weights * (dot(v, grad, 1, 1) - delta)).astype(jnp.bfloat16)
    return (
        dot(grad_scores, k, 0, 0),
        dot(grad_scores, q),
        dot(weights.astype(jnp.bfloat16), grad),
    )


def row_product(left, right):
    return as_row(
        jnp.sum(left.astype(jnp.float32) * right.astype(jnp.float32), axis=1, keepdims=True)
    )[:1]


def short_backward_kernel(
    pack_rows, qkv_ref, facts_ref, attn_ref, grad_ref, lse_ref, cos_ref, sin_ref, out_ref,
    dk_ref, dv_ref,
):
    blocks = attn_ref.shape[0] // HALF
    scale = HEAD_DIM**-0.5
    dk_ref[...] = jnp.zeros_like(dk_ref)
    dv_ref[...] = jnp.zeros_like(dv_ref)
    for i in range(blocks):
        rows = pl.ds((i + 2) * HALF, HALF)
        keys = (i + 1) * HALF
        q = stacked(qkv_ref[rows, :256]) * jnp.bfloat16(scale)
        k = qkv_ref[pl.ds(2 * HALF, keys), 256:320]
        v = qkv_ref[pl.ds(2 * HALF, keys), 320:384]
        grad = stacked(grad_ref[rows, :])
        delta = row_product(grad, stacked(attn_ref[pl.ds(i * HALF, HALF), :]))
        key = lax.broadcasted_iota(jnp.int32, (keys, HALF), 0)
        query = lax.broadcasted_iota(jnp.int32, (1, HALF), 1) + i * HALF
        seen = (key <= query) & (key >= start_of(query, facts_ref, pack_rows))
        dq, dk, dv = grad_terms(
            q, grad, k, v, jnp.concatenate([seen] * 4, axis=1), lse_ref[i, :1], delta
        )
        out_ref[pl.ds(i * HALF, HALF), :256] = turned(
            unstacked(dq * scale), cos_ref[rows, :], -sin_ref[rows, :]
        ).astype(jnp.bfloat16)
        dk_ref[pl.ds(0, keys), :] += dk
        dv_ref[pl.ds(0, keys), :] += dv
    rows = pl.ds(2 * HALF, blocks * HALF)
    out_ref[:, 256:] = turned_key(
        jnp.concatenate([dk_ref[...], dv_ref[...]], axis=1), cos_ref[rows, :], -sin_ref[rows, :]
    ).astype(jnp.bfloat16)


def short_backward(line, qkv, facts, attn, grad, lse, cos_rows, sin_rows, pack_rows):
    rows = attn.shape[0]
    return line(
        "short_backward",
        functools.partial(short_backward_kernel, pack_rows),
        (qkv, facts, attn, grad, lse, cos_rows, sin_rows),
        [VMEM, SMEM] + [VMEM] * 5,
        [shaped((rows, 384))],
        [VMEM],
        [pltpu.VMEM((rows, HEAD_DIM), jnp.float32)] * 2,
    )[0]


def long_backward_kernel(q_ref, *refs):
    far_refs = refs[:4]
    facts_ref, attn_ref, grad_ref, lse_ref, cos_ref, sin_ref = refs[4:10]
    dq_ref, far_grad_ref, acc_ref = refs[10:]
    scale = HEAD_DIM**-0.5
    count = far_refs[0].shape[0]
    blocks = count // HALF
    queries = []
    for half in range(2):
        rows = pl.ds(half * HALF, HALF)
        grad = stacked(grad_ref[rows, :])
        column = lax.broadcasted_iota(jnp.int32, (1, HALF), 1)
        queries.append(
            (
                stacked(q_ref[rows, :256]) * jnp.bfloat16(scale),
                grad,
                lse_ref[half, :1],
                row_product(grad, stacked(attn_ref[rows, :])),
                jnp.concatenate([column + facts_ref[FIRST_PLACE + half] * HALF] * 4, axis=1),
            )
        )
    within = lax.broadcasted_iota(jnp.int32, (HALF, 1), 0)
    for i, far_ref in enumerate(far_refs):
        k, v = far_ref[:, :HEAD_DIM], far_ref[:, HEAD_DIM:]
        key = jnp.concatenate(
            [within + facts_ref[FAR_PLACE + i * blocks + n] * HALF for n in range(blocks)], axis=0
        )
        sums = []
        for half, (q, grad, lse, delta, position) in enumerate(queries):
            dq, dk, dv = grad_terms(q, grad, k, v, key <= position, lse, delta)
            acc_ref[half] = dq if i == 0 else acc_ref[half] + dq
            sums.append((dk, dv))
        total = jnp.concatenate(
            [sums[0][0] + sums[1][0], sums[0][1] + sums[1][1]], axis=1
        ).astype(jnp.bfloat16)
        rows = count // 4
        for n in range(4):
            far_grad_ref[n, pl.ds(i * rows, rows), :] = total[n * rows : (n + 1) * rows]
    for half in range(2):
        rows = pl.ds(half * HALF, HALF)
        dq_ref[rows, :] = turned(
            unstacked(acc_ref[half] * scale), cos_ref[rows, :], -sin_ref[rows, :]
        ).astype(jnp.bfloat16)


def long_backward(line, q, far, facts, attn, grad, lse, cos_rows, sin_rows):
    return line(
        "long_backward",
        long_backward_kernel,
        (q, *far, facts, attn, grad, lse, cos_rows, sin_rows),
        [VMEM] * 5 + [SMEM] + [VMEM] * 5,
        [shaped((2 * HALF, 256)), shaped((4, *far[0].shape))],
        [VMEM] * 2,
        [pltpu.VMEM((2, 4 * HALF, HEAD_DIM), jnp.float32)],
    )


def product_kernel(turned_right, left_ref, right_ref, out_ref):
    out_ref[...] = dot(left_ref[...], right_ref[...], 1, 1 if turned_right else 0).astype(
        out_ref.dtype
    )


def product(line, left, right, turned_right=False):
    rows, depth = left.shape
    width = right.shape[0] if turned_right else right.shape[1]
    block = rows // 2
    return line(
        "product",
        functools.partial(product_kernel, turned_right),
        (left, right),
        [rows_of(block, depth), once(right.shape)],
        [shaped((rows, width))],
        [rows_of(block, width)],
        grid=(2,),
    )[0]


def product_parts_kernel(terms, turned_right, *refs):
    outs = refs[2 * terms + 1 :]
    total = refs[2 * terms][...].astype(jnp.float32)
    for k in range(terms):
        total += dot(refs[2 * k][...], refs[2 * k + 1][...], 1, 1 if turned_right else 0)
    rows = outs[0].shape[0]
    for k, out_ref in enumerate(outs):
        out_ref[...] = total[k * rows : (k + 1) * rows].astype(jnp.bfloat16)


def product_parts(line, pairs, sent, turned_right=False):
    rows, width = sent.shape
    block = width // 4
    specs = []
    for left, right in pairs:
        specs.append(once(left.shape))
        if turned_right:
            specs.append(rows_of(block, right.shape[1]))
        else:
            specs.append(columns_of(right.shape[0], block))
    return line(
        "product_parts",
        functools.partial(product_parts_kernel, len(pairs), turned_right),
        [array for pair in pairs for array in pair] + [sent],
        specs + [columns_of(rows, block)],
        [shaped((rows // 4, width))] * 4,
        [columns_of(rows // 4, block)] * 4,
        grid=(4,),
    )


def merged(chunks):
    pieces = []
    for k in range(4):
        for (low, high), chunk in zip(CHUNKS, chunks):
            pieces.append(chunk[k * (high - low) : (k + 1) * (high - low)])
    return jnp.concatenate(pieces, axis=0)


def merged_product_kernel(count, with_sent, *refs):
    right = refs[count][...]
    total = dot(merged([ref[...] for ref in refs[:count]]), right)
    outs = refs[count + 1 :]
    if with_sent:
        total += outs[0][...].astype(jnp.float32)
        outs = outs[1:]
    rows = outs[0].shape[0]
    for k, out_ref in enumerate(outs):
        out_ref[...] = total[k * rows : (k + 1) * rows].astype(jnp.bfloat16)


def merged_product(line, chunks, right, sent=None):
    rows = sum([chunk.shape[0] for chunk in chunks])
    depth, width = right.shape
    block = width // 4
    count = 1 if sent is None else 4
    extra = () if sent is None else (sent,)
    return line(
        "merged_product",
        functools.partial(merged_product_kernel, len(chunks), sent is not None),
        (*chunks, right, *extra),
        [once(chunk.shape) for chunk in chunks]
        + [columns_of(depth, block)]
        + [columns_of(rows, block)] * len(extra),
        [shaped((rows // count, width))] * count,
        [columns_of(rows // count, block)] * count,
        grid=(4,),
    )


def merged_back_kernel(count, *refs):
    left = merged([ref[...] for ref in refs[:count]])
    refs[-1][...] = dot(left, refs[count][...], 1, 1).astype(jnp.bfloat16)


def merged_back(line, chunks, right):
    rows = sum([chunk.shape[0] for chunk in chunks])
    return line(
        "merged_back",
        functools.partial(merged_back_kernel, len(chunks)),
        (*chunks, right),
        [VMEM] * (len(chunks) + 1),
        [shaped((rows, right.shape[0]))],
        [VMEM],
    )[0]


def arrange_kernel(facts_ref, rows_ref, *out_refs):
    del facts_ref
    for (low, high), out_ref in zip(CHUNKS, out_refs):
        out_ref[0] = rows_ref[0, low:high, :]


def arrange(line, rows, facts):
    _, count, d = rows.shape
    after = line.last

    def kernel(facts_ref, rows_ref, *refs):
        arrange_kernel(facts_ref, rows_ref, *refs[len(after) :])

    def source(i, facts_ref):
        core = jnp.where(i < 4, facts_ref[CORE_AT], 1 - facts_ref[CORE_AT])
        return core * 4 + (facts_ref[X_AT] + i) % 4, 0, 0

    results = pl.pallas_call(
        kernel,
        grid_spec=pltpu.PrefetchScalarGridSpec(
            num_scalar_prefetch=1,
            grid=(8,),
            in_specs=[pl.BlockSpec((1, count, d), source)] + [ANY] * len(after),
            out_specs=tuple(
                pl.BlockSpec((1, high - low, d), lambda i, facts_ref: (i, 0, 0))
                for low, high in CHUNKS
            ),
        ),
        out_shape=tuple(shaped((8, high - low, d)) for low, high in CHUNKS),
        compiler_params=PARAMS,
        cost_estimate=cost("arrange"),
        name="arrange",
    )(facts, rows, *after)
    return [array.reshape(-1, d) for array in results]


def weight_grad_kernel(count, beside, *refs):
    out_ref, width = refs[-1], refs[count].shape[1]
    total = dot(refs[0][...], refs[count][...], 0, 0)
    for k in range(1, count):
        total += dot(refs[k][...], refs[count + k][...], 0, 0)
    out_ref[:, :width] = total.astype(jnp.bfloat16)
    if beside:
        out_ref[:, width:] = refs[2 * count][...]


def weight_grad(line, left, right, beside=()):
    left = [piece if isinstance(piece, tuple) else (piece, 0) for piece in left]
    columns, width = left[0][0].shape[1], right[0].shape[1]
    whole = width + sum([array.shape[1] for array in beside])

    def out_block(n):
        return pl.BlockSpec((columns // 8, n), lambda i: (i % 4 * 2 + i // 4, 0))

    return line(
        "weight_grad",
        functools.partial(weight_grad_kernel, len(left), len(beside)),
        (*[array for array, _ in left], *right, *beside),
        [
            pl.BlockSpec((part.shape[0], columns // 8), lambda i, at=at: (at, i))
            for (_, at), part in zip(left, right)
        ]
        + [once(array.shape) for array in right]
        + [out_block(array.shape[1]) for array in beside],
        [shaped((columns, whole))],
        [out_block(whole)],
        grid=(8,),
    )[0]


def mix_kernel(low, high, tokens_ref, gain_ref, *refs):
    parts, (mixed_ref, hidden_ref) = refs[:4], refs[4:]
    mixed = tokens_ref[low:high, :].astype(jnp.float32) + total_of([ref[...] for ref in parts])
    inv = lax.rsqrt(jnp.mean(mixed * mixed, axis=-1, keepdims=True) + EPS)
    mixed_ref[...] = mixed
    hidden_ref[...] = (mixed * inv * gain_ref[...]).astype(jnp.bfloat16)


def mix(line, chunk, tokens, gain, parts):
    low, high = chunk
    d = tokens.shape[1]
    return line(
        "mix",
        functools.partial(mix_kernel, low, high),
        (tokens, gain, *parts),
        [VMEM] * 6,
        [shaped((high - low, d), jnp.float32), shaped((high - low, d))],
        [VMEM] * 2,
    )


def norm_back(grad_in, values, gain):
    inv = lax.rsqrt(jnp.mean(values * values, axis=-1, keepdims=True) + EPS)
    unit = values * inv
    scaled = grad_in * gain
    return inv * (scaled - unit * jnp.mean(scaled * unit, axis=-1, keepdims=True)), unit


def mix_back_kernel(low, high, grad_ref, mixed_ref, gain_ref, *refs):
    parts, (total_ref, low_ref, part_ref) = refs[:4], refs[4:]
    grad_in = total_of([ref[...] for ref in parts])
    back, unit = norm_back(grad_in, mixed_ref[...], gain_ref[...])
    total = grad_ref[low:high, :].astype(jnp.float32) + back
    total_ref[...] = total
    low_ref[...] = total.astype(jnp.bfloat16)
    part_ref[...] = jnp.sum(grad_in * unit, axis=0, keepdims=True)


def mix_back(line, chunk, grad, mixed, gain, parts):
    low, high = chunk
    rows, d = mixed.shape
    return line(
        "mix_back",
        functools.partial(mix_back_kernel, low, high),
        (grad, mixed, gain, *parts),
        [VMEM] * 7,
        [shaped((rows, d), jnp.float32), shaped((rows, d)), shaped((1, d), jnp.float32)],
        [VMEM] * 3,
    )


def mlp_kernel(hidden_ref, grad_act_ref, gate_ref, up_ref, act_ref, gate_out_ref, up_out_ref, *refs):
    hidden = hidden_ref[...]
    gate = dot(hidden, gate_ref[...])
    up = dot(hidden, up_ref[...])
    grad_act = grad_act_ref[...].astype(jnp.float32)
    sig = jax.nn.sigmoid(gate)
    silu = gate * sig
    act_ref[...] = (silu * up).astype(jnp.bfloat16)
    grad_gate = (grad_act * up * sig * (1.0 + gate * (1.0 - sig))).astype(jnp.bfloat16)
    grad_up = (grad_act * silu).astype(jnp.bfloat16)
    gate_out_ref[...] = grad_gate
    up_out_ref[...] = grad_up
    if refs:
        i = pl.program_id(0)
        back_ref, acc_ref = refs
        part = dot(grad_gate, gate_ref[...], 1, 1) + dot(grad_up, up_ref[...], 1, 1)

        @pl.when(i == 0)
        def _():
            acc_ref[...] = part

        @pl.when((i > 0) & (i < pl.num_programs(0) - 1))
        def _():
            acc_ref[...] += part

        @pl.when(i == pl.num_programs(0) - 1)
        def _():
            back_ref[...] = (acc_ref[...] + part).astype(jnp.bfloat16)


def mlp(line, hidden, grad_act, at, w_gate, w_up, with_back):
    rows, d = hidden.shape
    width = w_gate.shape[1]
    block = width // 4
    outs = [shaped((rows, width))] * 3
    out_specs = [columns_of(rows, block)] * 3
    if with_back:
        outs.append(shaped((rows, d)))
        out_specs.append(pl.BlockSpec((rows, d), lambda i: (0, 0)))
    return line(
        "mlp",
        mlp_kernel,
        (hidden, grad_act, w_gate, w_up),
        [
            once((rows, d)),
            pl.BlockSpec((rows, block), lambda i: (at, i)),
            columns_of(d, block),
            columns_of(d, block),
        ],
        outs,
        out_specs,
        [pltpu.VMEM((rows, d), jnp.float32)] if with_back else [],
        grid=(4,),
    )


def hidden_grad_kernel(with_sent, low_ref, query_ref, kv_ref, hidden_ref, *refs):
    low = low_ref[...]
    grad = dot(low[:, :256], query_ref[...], 1, 1) + dot(low[:, 256:], kv_ref[...], 1, 1)
    refs[-1][...] = jnp.sum(grad * hidden_ref[...].astype(jnp.float32), axis=0, keepdims=True)
    if with_sent:
        grad += refs[0][...].astype(jnp.float32)
        rows = refs[1].shape[0]
        for k, out_ref in enumerate(refs[1:-1]):
            out_ref[...] = grad[k * rows : (k + 1) * rows].astype(jnp.bfloat16)
    else:
        refs[0][...] = grad.astype(jnp.bfloat16)


def hidden_grad(line, low, w_query, w_key_value, hidden, sent=None):
    rows, d = hidden.shape
    block = d // 4
    count = 1 if sent is None else 4
    extra = () if sent is None else (sent,)
    return line(
        "hidden_grad",
        functools.partial(hidden_grad_kernel, sent is not None),
        (low, w_query, w_key_value, hidden, *extra),
        [once((rows, 384)), rows_of(block, 256), rows_of(block, 128)]
        + [columns_of(rows, block)] * (1 + len(extra)),
        [shaped((rows // count, d))] * count + [shaped((1, d), jnp.float32)],
        [columns_of(rows // count, block)] * count + [columns_of(1, block)],
        grid=(4,),
    )


def copy_kernel(source_ref, out_ref):
    out_ref[...] = source_ref[...]


def copied(line, array):
    rows, width = array.shape
    block = columns_of(rows, width // 4)
    return line(
        "copied", copy_kernel, (array,), [block], [shaped((rows, width))], [block], grid=(4,)
    )[0]


def gate_kernel(*refs):
    del refs


def gated(line, arrays):
    return line(
        "gated",
        gate_kernel,
        arrays,
        [ANY] * len(arrays),
        [shaped(array.shape, array.dtype) for array in arrays],
        [ANY] * len(arrays),
        input_output_aliases={k: k for k in range(len(arrays))},
    )


def gains_kernel(own_ref, other_ref, gain_ref, mlp_ref, out_ref):
    out_ref[:1] = (own_ref[...] + other_ref[...]) / gain_ref[...]
    out_ref[1:] = mlp_ref[...]


def turn_far_kernel(grad_ref, cos_ref, sin_ref, long_ref, short_ref, out_ref):
    rows = pl.ds(0, 2 * HALF)
    packed = out_ref.shape[0] - 2 * HALF
    out_ref[rows, :256] = long_ref[...]
    out_ref[rows, 256:] = turned_key(grad_ref[...], cos_ref[rows, :], -sin_ref[rows, :]).astype(
        jnp.bfloat16
    )
    out_ref[pl.ds(2 * HALF, packed), :] = short_ref[pl.ds(0, packed), :]


def local(
    tokens,
    lengths,
    place,
    attn_gain,
    w_query,
    w_key,
    w_value,
    w_out,
    mlp_gain,
    w_gate,
    w_up,
    w_down,
    out_grad,
):
    rows, d = tokens.shape
    group_rows = rows * 8
    half_rows = rows * 4
    long_rows = 2 * HALF
    pack_rows = group_rows - long_rows
    padded_rows = -(-group_rows // HALF) * HALF
    dp_index, mp_index = lax.axis_index("dp"), lax.axis_index("mp")
    yh, z, core = dp_index // 8, dp_index // 2 % 4, dp_index % 2
    yl, x = mp_index // 4, mp_index % 4
    native = core == yl
    line = Line()
    mlp_gain_row = mlp_gain.reshape(1, d)

    tokens = send(tokens, TURN)
    lengths = send(lengths, TURN)[0]
    w_key_value = send(jnp.concatenate([w_key, w_value], axis=1), WEIGHT_HIGH)
    w_query = send(w_query, WEIGHT_LOW)
    w_out = send(w_out, WEIGHT_HIGH)
    w_gate = send(w_gate, WEIGHT_LOW)
    w_up = send(w_up, WEIGHT_HIGH)
    w_down = send(w_down, WEIGHT_LOW)
    out_grad = send(out_grad, TURN)

    step = jnp.arange(16, dtype=jnp.int32)
    far_yh = jnp.where(step % 4 >= 2, 1 - yh, yh)
    far_yl = jnp.where((step % 4 == 1) | (step % 4 == 2), 1 - yl, yl)
    far_group = (far_yh * 4 + (z + step // 4) % 4) * 2 + far_yl
    far_index = (2 * far_group[:, None] + jnp.arange(2, dtype=jnp.int32)[None, :]).reshape(-1)
    half_ids = jnp.arange(place.shape[0], dtype=jnp.int32)
    far_place = jnp.sum(jnp.where(far_index[:, None] == half_ids[None, :], place, 0), axis=1)
    facts = jnp.concatenate(
        [
            far_place[:2],
            jnp.stack([lengths[0], lengths[0] + lengths[1], core, x]),
            far_place,
        ]
    ).astype(jnp.int32)

    residual = tokens.astype(jnp.float32)
    inv_one = lax.rsqrt(jnp.mean(residual * residual, axis=-1, keepdims=True) + EPS)
    hidden_one = collect((residual * inv_one * attn_gain).astype(jnp.bfloat16))
    freq = jnp.tile(inverse_freq(HEAD_DIM), 4).reshape(1, 128)
    cos_gathered, sin_gathered, cos_ordered, sin_ordered = line(
        "tables",
        functools.partial(tables_kernel, rows),
        (facts, freq),
        [SMEM, VMEM],
        [shaped((n, 128), jnp.float32) for n in (group_rows, group_rows, padded_rows, padded_rows)],
        [VMEM] * 4,
    )
    line.last += (w_query, w_key_value, out_grad)
    hidden_own = join(line, hidden_one)
    hidden_one = (hidden_own, send(hidden_own, CORE))
    qkv = []
    for at, half in enumerate(hidden_one):
        qkv.append(
            project_qkv(line, half, w_query, w_key_value, cos_gathered, sin_gathered, at)
        )
    qkv = in_order(jnp.stack(qkv), core, x)
    qkv = jnp.pad(qkv, ((0, padded_rows - group_rows), (0, 0)))
    near_rows = qkv[:long_rows, 256:]
    ring_rows = jnp.concatenate(
        [near_rows, send(near_rows, Y_LOW), send(near_rows, Y_HIGH), send(near_rows, Y_FAR)]
    )
    far_rows = (
        ring_rows, send(ring_rows, Z_DOWN), send(ring_rows, Z_FAR), send(ring_rows, Z_UP)
    )
    line.last += (ring_rows, w_out, w_down)
    grad_rows = lax.all_gather(
        copied(line, out_grad), BOTH, axis=0, axis_index_groups=CHIP_GROUPS
    )
    short_attn, short_lse = short_forward(line, qkv, facts, pack_rows)
    attn_ordered, long_lse = long_forward(line, qkv, far_rows, facts, short_attn, group_rows)
    attn_rows = from_order(attn_ordered, core, x)
    attn_rows = [chunks_of(attn_rows[half]) for half in range(2)]

    sent = [send(product(line, part, w_out), CORE) for part in attn_rows[1]]
    mixed_parts = [
        scatter(product_parts(line, [(part, w_out)], other))
        for part, other in zip(attn_rows[0], sent)
    ]
    grad_rows = arrange(line, grad_rows, facts)
    grad_act = [product(line, part, w_down, True) for part in grad_rows]
    mixed, hidden_two = [], []
    for chunk, parts in zip(CHUNKS, mixed_parts):
        mixed_rows, hidden_rows = mix(line, chunk, tokens, mlp_gain_row, parts)
        mixed.append(mixed_rows)
        hidden_two.append(collect(hidden_rows))

    count = len(CHUNKS)
    own, other, act, gate, up, back = ([None] * count for _ in range(6))

    def first_half(n):
        own[n] = join(line, hidden_two[n])
        other[n] = send(own[n], CORE)
        act[n], gate[n], up[n] = mlp(line, own[n], grad_act[n], 0, w_gate, w_up, False)

    def second_half(n):
        *terms, sum_back = mlp(line, other[n], grad_act[n], 1, w_gate, w_up, True)
        act[n], gate[n], up[n] = zip((act[n], gate[n], up[n]), terms)
        back[n] = send(sum_back, CORE)

    hidden_parts = []
    first_half(0)
    second_half(0)
    for n in range(count):
        if n + 1 < count:
            first_half(n + 1)
        terms = [(gate[n][0], w_gate), (up[n][0], w_up)]
        hidden_parts.append(scatter(product_parts(line, terms, back[n], True)))
        if n + 1 < count:
            second_half(n + 1)
    act, gate, up = [[pair[k] for pair in part for k in range(2)] for part in (act, gate, up)]
    hidden_two = [piece for pair in zip(own, other) for piece in pair]
    grad_pieces = [(part, at) for part in grad_rows for at in range(2)]

    (down_rows,) = merged_product(line, act[1::2], w_down)
    down_rows = send(down_rows, CORE)
    down_part = weight_grad(line, grad_pieces, act)
    first_part = weight_grad(line, hidden_two, gate, (down_part,))
    grad_mixed, mixed_grad, gain_parts = [], [], []
    for n, (chunk, parts) in enumerate(zip(CHUNKS, hidden_parts)):
        total, low, gain_part = mix_back(line, chunk, out_grad, mixed[n], mlp_gain_row, parts)
        grad_mixed.append(total)
        mixed_grad.append(collect(low))
        gain_parts.append(gain_part)
    first_kept = reduce_near(gated(line, (first_part,))[0])
    second_part = weight_grad(line, hidden_two, up)
    out_parts = scatter(merged_product(line, act[0::2], w_down, down_rows))

    grad_own = [join(line, parts) for parts in mixed_grad]
    grad_other = [send(part, CORE) for part in grad_own]
    grad_attn = jnp.stack([merged_back(line, part, w_out) for part in (grad_own, grad_other)])
    grad_attn = in_order(grad_attn, core, x)
    grad_attn = jnp.pad(grad_attn, ((0, padded_rows - group_rows), (0, 0)))
    long_dq, far_terms = long_backward(
        line,
        qkv,
        far_rows,
        facts,
        attn_ordered,
        grad_attn,
        long_lse,
        cos_ordered,
        sin_ordered,
    )
    ring_terms = total_of(
        (
            far_terms[0],
            send(far_terms[1], Y_LOW),
            send(far_terms[2], Y_HIGH),
            send(far_terms[3], Y_FAR),
        )
    ).astype(jnp.bfloat16)
    near = ring_terms.reshape(4, long_rows, -1)
    far_grads = total_of(
        (near[0], send(near[1], Z_UP), send(near[2], Z_FAR), send(near[3], Z_DOWN))
    )
    out_part = weight_grad(
        line,
        [piece for pair in zip(grad_own, grad_other) for piece in pair],
        [piece for pair in zip(*attn_rows) for piece in pair],
    )
    line.last += (first_kept,)
    second_sum = reduce_y(reduce_near(gated(line, (second_part,))[0]))
    line.last += out_parts[1:]
    short_low = short_backward(
        line, qkv, facts, short_attn, grad_attn, short_lse, cos_ordered, sin_ordered, pack_rows
    )
    (low_ordered,) = line(
        "turn_far",
        turn_far_kernel,
        (far_grads, cos_ordered, sin_ordered, long_dq, short_low),
        [VMEM] * 5,
        [shaped((group_rows, 384))],
        [VMEM],
    )
    low_rows = from_order(low_ordered, core, x)
    first_sum, first_received = sum_groups(first_kept, yh, core, native)
    back, gain_other = hidden_grad(line, low_rows[1], w_query, w_key_value, hidden_one[1])
    back = send(back, CORE)
    last_part = weight_grad(line, hidden_one, (low_rows[0], low_rows[1]), (out_part,))
    line.last += first_received
    *parts, gain_own = hidden_grad(line, low_rows[0], w_query, w_key_value, hidden_one[0], back)
    grad_parts = scatter(parts)
    last_kept = reduce_ring(gated(line, (last_part,))[0], z)
    output = jnp.concatenate(mixed) + total_of(out_parts)
    output = send(output.astype(jnp.bfloat16), TURN)
    line.last += (grad_parts[1],)
    (gains,) = line(
        "gains",
        gains_kernel,
        (gain_own, gain_other, attn_gain.reshape(1, d), sum(gain_parts[1:], gain_parts[0])),
        [VMEM] * 4,
        [shaped((2, d), jnp.float32)],
        [VMEM],
    )
    gains = all_sum(gains)
    last_sum, _ = sum_groups(last_kept, yh, core, native)
    grad_tokens = (
        jnp.concatenate(grad_mixed) + norm_back(total_of(grad_parts), residual, attn_gain)[0]
    )
    grad_tokens = send(grad_tokens.astype(jnp.bfloat16), TURN)
    ff = w_gate.shape[1]
    return (
        output,
        grad_tokens,
        gains[0],
        last_sum[:, :256],
        last_sum[:, 256:320],
        last_sum[:, 320:384],
        last_sum[:, 384:].T,
        gains[1],
        first_sum[:, :ff],
        second_sum,
        first_sum[:, ff:].T,
    )


def solution(mesh):
    placed = (
        P(("dp", "mp"), None),
        P("dp", None),
        P(),
        P(),
        P(None, "mp"),
        P(None, "mp"),
        P(None, "mp"),
        P("mp", None),
        P(),
        P(None, "mp"),
        P(None, "mp"),
        P("mp", None),
        P(("dp", "mp"), None),
    )
    return jax.shard_map(
        local,
        mesh=mesh,
        in_specs=placed,
        out_specs=(
            P(("dp", "mp"), None),
            P(("dp", "mp"), None),
            P(),
            P("dp", "mp"),
            P("dp", "mp"),
            P("dp", "mp"),
            P("mp", "dp"),
            P(),
            P("dp", "mp"),
            P("dp", "mp"),
            P("mp", "dp"),
        ),
        check_vma=False,
    )
```

```python
import functools

import jax
import jax.numpy as jnp
from jax import lax
from jax.experimental import pallas as pl
from jax.experimental.pallas import tpu as pltpu
from jax.sharding import PartitionSpec as P

HEAD_DIM = 64
HALF = 128
MASKED = -1e30


EPS = 1e-05
THETA = 500000.0

BOTH = ("dp", "mp")


def place_of(yh, z, c, yl, x):
    return ((yh * 4 + z) * 2 + c) * 8 + yl * 4 + x


def pairs_of(target, sender=lambda yh, z, c, yl, x: True):
    return [
        (place_of(yh, z, c, yl, x), place_of(*target(yh, z, c, yl, x)))
        for yh in range(2)
        for z in range(4)
        for c in range(2)
        for yl in range(2)
        for x in range(4)
        if sender(yh, z, c, yl, x)
    ]


X_UP = pairs_of(lambda yh, z, c, yl, x: (yh, z, c, yl, (x + 1) % 4))
X_DOWN = pairs_of(lambda yh, z, c, yl, x: (yh, z, c, yl, (x + 3) % 4))
X_FAR = pairs_of(lambda yh, z, c, yl, x: (yh, z, c, yl, (x + 2) % 4))
Z_UP = pairs_of(lambda yh, z, c, yl, x: (yh, (z + 1) % 4, c, yl, x))
Z_DOWN = pairs_of(lambda yh, z, c, yl, x: (yh, (z + 3) % 4, c, yl, x))
Z_FAR = pairs_of(lambda yh, z, c, yl, x: (yh, (z + 2) % 4, c, yl, x))
CORE = pairs_of(lambda yh, z, c, yl, x: (yh, z, 1 - c, yl, x))
Y_LOW = pairs_of(lambda yh, z, c, yl, x: (yh, z, c, 1 - yl, x))
Y_HIGH = pairs_of(lambda yh, z, c, yl, x: (1 - yh, z, c, 1 - yl, x))
Y_FAR = pairs_of(lambda yh, z, c, yl, x: (1 - yh, z, c, yl, x))
TURN = pairs_of(lambda yh, z, c, yl, x: (yh, z, yl, c, x))
NATIVE = lambda yh, z, c, yl, x: c == yl
FOREIGN = lambda yh, z, c, yl, x: c != yl
FOREIGN_LOW = pairs_of(lambda yh, z, c, yl, x: (yh, z, c, 1 - yl, x), FOREIGN)
FOREIGN_HIGH = pairs_of(lambda yh, z, c, yl, x: (1 - yh, z, c, 1 - yl, x), FOREIGN)
NATIVE_LOW = pairs_of(lambda yh, z, c, yl, x: (yh, z, c, 1 - yl, x), NATIVE)
NATIVE_HIGH = pairs_of(lambda yh, z, c, yl, x: (1 - yh, z, c, 1 - yl, x), NATIVE)
NATIVE_CORE = pairs_of(lambda yh, z, c, yl, x: (yh, z, 1 - c, yl, x), NATIVE)
WEIGHT_LOW = pairs_of(
    lambda yh, z, c, yl, x: (yh, z, c, 1 - yl, x) if c == yl else (yh, z, 1 - c, yl, x)
)
WEIGHT_HIGH = pairs_of(
    lambda yh, z, c, yl, x: (1 - yh, z, c, 1 - yl, x) if c == yl else (yh, z, 1 - c, yl, x)
)
Z_GROUPS = [
    [place_of(yh, z, c, yl, x) for z in range(4)]
    for yh in range(2)
    for c in range(2)
    for yl in range(2)
    for x in range(4)
]


Y_GROUPS = [
    [place_of(yh, z, c, yl, x) for yh in range(2) for yl in range(2)]
    for z in range(4)
    for c in range(2)
    for x in range(4)
]
CHIP_GROUPS = [
    [place_of(yh, z, c, yl, x) for c in range(2) for x in range(4)]
    for yh in range(2)
    for z in range(4)
    for yl in range(2)
]


def send(values, pairs):
    return lax.ppermute(values, BOTH, pairs)


CHUNKS = ((0, 136),)

VMEM = pl.BlockSpec(memory_space=pltpu.VMEM)
SMEM = pl.BlockSpec(memory_space=pltpu.SMEM)
ANY = pl.BlockSpec(memory_space=pl.ANY)
PARAMS = pltpu.CompilerParams(vmem_limit_bytes=64 * 1024 * 1024)
LASTS = {
    "tables": 1,
    "join": 1,
    "project_qkv": 1,
    "short_forward": 6,
    "long_forward": 13,
    "product": 3,
    "product_parts": 5,
    "arrange": 5,
    "mix": 3,
    "mlp": 10,
    "weight_grad": 2,
    "mix_back": 4,
    "merged_product": 2,
    "merged_back": 3,
    "long_backward": 16,
    "short_backward": 10,
    "turn_far": 2,
    "hidden_grad": 5,
    "out_mix": 4,
    "final": 4,
    "gated": 1,
}


def cost(name):
    return pl.CostEstimate(
        flops=int(1.15e9 * LASTS[name]), bytes_accessed=1000, transcendentals=0
    )


def shaped(shape, dtype=jnp.bfloat16):
    return pltpu.HBM(tuple(shape), dtype)


def rows_of(block, width):
    return pl.BlockSpec((block, width), lambda i: (i, 0))


def columns_of(rows, block):
    return pl.BlockSpec((rows, block), lambda i: (0, i))


def once(shape):
    return pl.BlockSpec(tuple(shape), lambda i: (0,) * len(shape), pipeline_mode=pl.Buffered(1))


class Line:
    def __init__(self):
        self.last = ()

    def __call__(self, name, kernel, operands, in_specs, outs, out_specs, scratch=(), **grid):
        after = self.last
        count = len(operands)

        def ordered(*refs):
            kernel(*refs[:count], *refs[count + len(after) :])

        results = pl.pallas_call(
            ordered,
            out_shape=tuple(outs),
            in_specs=list(in_specs) + [ANY] * len(after),
            out_specs=tuple(out_specs),
            scratch_shapes=list(scratch),
            compiler_params=PARAMS,
            cost_estimate=cost(name),
            name=name,
            **grid,
        )(*operands, *after)
        self.last = (min(results, key=lambda array: array.size),)
        return results


def dot(left, right, left_dim=1, right_dim=0):
    return lax.dot_general(
        left, right, (((left_dim,), (right_dim,)), ((), ())), preferred_element_type=jnp.float32
    )


def total_of(parts):
    one, two, three, four = [part.astype(jnp.float32) for part in parts]
    return (one + two) + (three + four)


def scatter(parts):
    return (
        parts[0],
        send(parts[1], X_UP),
        send(parts[2], X_FAR),
        send(parts[3], X_DOWN),
    )


def collect(rows):
    return (rows, send(rows, X_DOWN), send(rows, X_FAR), send(rows, X_UP))


def in_order(pair, core, x):
    half = pair.shape[1]
    start = (4 - x) % 4 * (half // 4)
    pair = lax.dynamic_slice_in_dim(jnp.concatenate([pair, pair], axis=1), start, half, axis=1)
    return jnp.where(core == 0, pair, pair[::-1]).reshape(2 * half, -1)


def from_order(values, core, x):
    half = values.shape[0] // 2
    pair = values.reshape(2, half, -1)
    pair = jnp.where(core == 0, pair, pair[::-1])
    return lax.dynamic_slice_in_dim(
        jnp.concatenate([pair, pair], axis=1), x * (half // 4), half, axis=1
    )


def chunks_of(half):
    cut = half.reshape(4, half.shape[0] // 4, -1)
    return [cut[:, low:high].reshape(4 * (high - low), -1) for low, high in CHUNKS]


def plus(left, right):
    return (left.astype(jnp.float32) + right.astype(jnp.float32)).astype(jnp.bfloat16)


def reduce_near(grad):
    return lax.psum_scatter(
        grad, BOTH, scatter_dimension=0, tiled=True, axis_index_groups=Z_GROUPS
    )


def reduce_y(kept):
    kept = lax.psum_scatter(
        kept, BOTH, scatter_dimension=0, tiled=True, axis_index_groups=Y_GROUPS
    )
    return send(kept, TURN).astype(jnp.float32)


def reduce_ring(grad):
    here, above, far, below = jnp.split(grad, 4)
    rows = far.shape[0] // 2
    from_below, from_above = send(far[:rows], Z_UP), send(far[rows:], Z_DOWN)
    above = send(jnp.concatenate([plus(above[:rows], from_below), above[rows:]]), Z_UP)
    below = send(jnp.concatenate([below[:rows], plus(below[rows:], from_above)]), Z_DOWN)
    return (
        here.astype(jnp.float32) + above.astype(jnp.float32) + below.astype(jnp.float32)
    ).astype(jnp.bfloat16)


def sum_groups(kept, native):
    near, far = jnp.split(kept, 2)
    rows = near.shape[0] // 2
    by_low = send(far[:rows], NATIVE_LOW)
    by_high = send(far[rows:], NATIVE_HIGH)
    low = send(jnp.concatenate([near[:rows], plus(near[rows:], by_high)]), FOREIGN_LOW)
    high = send(jnp.concatenate([plus(far[:rows], by_low), far[rows:]]), FOREIGN_HIGH)
    total = near.astype(jnp.float32) + low.astype(jnp.float32) + high.astype(jnp.float32)
    passed = send(total[rows:].astype(jnp.bfloat16), NATIVE_CORE).astype(jnp.float32)
    return jnp.where(native, total[:rows], passed)


def all_sum(values):
    for group in ((CORE,), (Z_UP, Z_DOWN, Z_FAR), (Y_LOW, Y_HIGH, Y_FAR)):
        values = sum([send(values, pairs) for pairs in group], values)
    return values


def inverse_freq(head_width):
    indices = jnp.arange(head_width // 2, dtype=jnp.float32)
    base_freq = jnp.exp(-jnp.log(THETA) * 2.0 * indices / head_width)
    wavelength = 2.0 * jnp.pi / base_freq
    smooth = (8192.0 / wavelength - 1.0) / 3.0
    blended = (1.0 - smooth) * base_freq / 32.0 + smooth * base_freq
    return jnp.where(
        wavelength < 2048.0, base_freq, jnp.where(wavelength > 8192.0, base_freq / 32.0, blended)
    )


FIRST_PLACE, SECOND_START, THIRD_START, CORE_AT, X_AT, Z_AT, YH_AT, FAR_PLACE = 0, 2, 3, 4, 5, 6, 7, 8


def tables_kernel(rows, facts_ref, freq_ref, *out_refs):
    sign = jnp.where(lax.broadcasted_iota(jnp.int32, (1, 128), 1) % 64 < 32, -1.0, 1.0)
    group_rows, half_rows = rows * 8, rows * 4
    for gathered, (cos_ref, sin_ref) in enumerate((out_refs[:2], out_refs[2:])):
        row = lax.broadcasted_iota(jnp.int32, cos_ref.shape, 0)
        if gathered == 0:
            other = (row >= half_rows).astype(jnp.int32)
            rest = row - other * half_rows
            step = sum([(rest >= k * rows).astype(jnp.int32) for k in (1, 2, 3)])
            core = jnp.where(other == 0, facts_ref[CORE_AT], 1 - facts_ref[CORE_AT])
            row = core * half_rows + ((facts_ref[X_AT] + step) & 3) * rows + rest - step * rows
        packed = row - 2 * HALF
        second, third = facts_ref[SECOND_START], facts_ref[THIRD_START]
        start = jnp.where(packed >= third, third, jnp.where(packed >= second, second, 0))
        own = jnp.where(row < HALF, facts_ref[FIRST_PLACE], facts_ref[FIRST_PLACE + 1])
        position = jnp.where(row < 2 * HALF, own * HALF + (row & (HALF - 1)), packed - start)
        angles = position.astype(jnp.float32) * freq_ref[...]
        cos_ref[...] = jnp.cos(angles)
        sin_ref[...] = jnp.sin(angles) * sign


def turned(values, cos_rows, sin_rows):
    first = lax.broadcasted_iota(jnp.int32, (1, 128), 1) % 64 < 32
    tiles = []
    for at in range(0, values.shape[1], 128):
        tile = values[:, at : at + 128]
        swapped = jnp.where(first, pltpu.roll(tile, 96, 1), pltpu.roll(tile, 32, 1))
        tiles.append(tile * cos_rows + swapped * sin_rows)
    return tiles[0] if len(tiles) == 1 else jnp.concatenate(tiles, axis=1)


def turned_key(values, cos_rows, sin_rows):
    key = lax.broadcasted_iota(jnp.int32, (1, 128), 1) < HEAD_DIM
    return jnp.where(key, turned(values, cos_rows, sin_rows), values)


def join_kernel(count, *refs):
    for k in range(count):
        refs[-1][k] = refs[k][...]


def join(line, pieces):
    count = len(pieces)
    rows, width = pieces[0].shape
    block = width // 4
    (joined,) = line(
        "join",
        functools.partial(join_kernel, count),
        pieces,
        [columns_of(rows, block)] * count,
        [shaped((count, rows, width))],
        [pl.BlockSpec((count, rows, block), lambda i: (0, 0, i))],
        grid=(4,),
    )
    return joined.reshape(count * rows, width)


def qkv_kernel(hidden_ref, query_ref, kv_ref, cos_ref, sin_ref, out_ref):
    hidden = hidden_ref[...]
    cos_rows, sin_rows = cos_ref[...], sin_ref[...]
    out_ref[:, :256] = turned(dot(hidden, query_ref[...]), cos_rows, sin_rows).astype(jnp.bfloat16)
    out_ref[:, 256:] = turned_key(dot(hidden, kv_ref[...]), cos_rows, sin_rows).astype(
        jnp.bfloat16
    )


def project_qkv(line, hidden, w_query, w_key_value, cos_rows, sin_rows, at):
    rows, d = hidden.shape
    block = rows // 2
    table = pl.BlockSpec((block, 128), lambda i: (i + 2 * at, 0))
    return line(
        "project_qkv",
        qkv_kernel,
        (hidden, w_query, w_key_value, cos_rows, sin_rows),
        [rows_of(block, d), once((d, 256)), once((d, 128)), table, table],
        [shaped((rows, 384))],
        [rows_of(block, 384)],
        grid=(2,),
    )[0]


def stacked(block):
    return jnp.concatenate(
        [block[:, h * HEAD_DIM : (h + 1) * HEAD_DIM] for h in range(4)], axis=0
    )


def unstacked(block):
    rows = block.shape[0] // 4
    return jnp.concatenate([block[h * rows : (h + 1) * rows] for h in range(4)], axis=1)


def as_row(column):
    return jnp.transpose(jnp.broadcast_to(column, (column.shape[0], 128)))[:8]


def start_of(row, facts_ref):
    second, third = facts_ref[SECOND_START], facts_ref[THIRD_START]
    return jnp.where(row >= third, third, jnp.where(row >= second, second, 0))


def blocks_of(rows):
    return [(at, min(HALF, rows - at)) for at in range(0, rows, HALF)]


def short_forward_kernel(qkv_ref, facts_ref, attn_ref, lse_ref):
    for i, (at, count) in enumerate(blocks_of(attn_ref.shape[0])):
        rows = pl.ds(2 * HALF + at, count)
        keys = at + count
        q = stacked(qkv_ref[rows, :256]) * jnp.bfloat16(HEAD_DIM**-0.5)
        k = qkv_ref[pl.ds(2 * HALF, keys), 256:320]
        v = qkv_ref[pl.ds(2 * HALF, keys), 320:384]
        scores = dot(q, k, 1, 1)
        column = lax.broadcasted_iota(jnp.int32, (count, keys), 1)
        row = lax.broadcasted_iota(jnp.int32, (count, 1), 0) + at
        seen = (column <= row) & (column >= start_of(row, facts_ref))
        scores = jnp.where(jnp.concatenate([seen] * 4, axis=0), scores, MASKED)
        top = jnp.max(scores, axis=1, keepdims=True)
        weights = jnp.exp(scores - top)
        total = jnp.sum(weights, axis=1, keepdims=True)
        out = dot(weights.astype(jnp.bfloat16), v) / total
        attn_ref[pl.ds(at, count), :] = unstacked(out).astype(jnp.bfloat16)
        lse_ref[i, :, : 4 * count] = as_row(top + jnp.log(total))


def short_forward(line, qkv, facts):
    rows = qkv.shape[0] - 2 * HALF
    return line(
        "short_forward",
        short_forward_kernel,
        (qkv, facts),
        [VMEM, SMEM],
        [shaped((rows, 256)), shaped((len(blocks_of(rows)), 8, 4 * HALF), jnp.float32)],
        [VMEM] * 2,
    )


def long_forward_kernel(q_ref, *refs):
    far_refs, (facts_ref, short_ref, attn_ref, lse_ref) = refs[:4], refs[4:]
    within = lax.broadcasted_iota(jnp.int32, (1, HALF), 1)
    blocks = far_refs[0].shape[0] // HALF
    for half in range(2):
        rows = pl.ds(half * HALF, HALF)
        q = stacked(q_ref[rows, :256]) * jnp.bfloat16(HEAD_DIM**-0.5)
        row = lax.broadcasted_iota(jnp.int32, (HALF, 1), 0)
        position = jnp.concatenate([row + facts_ref[FIRST_PLACE + half] * HALF] * 4, axis=0)
        top = jnp.full((4 * HALF, 1), MASKED, jnp.float32)
        total = jnp.zeros((4 * HALF, 1), jnp.float32)
        out = jnp.zeros((4 * HALF, HEAD_DIM), jnp.float32)
        for i, far_ref in enumerate(far_refs):
            scores = dot(q, far_ref[:, :HEAD_DIM], 1, 1)
            key = jnp.concatenate(
                [within + facts_ref[FAR_PLACE + i * blocks + k] * HALF for k in range(blocks)],
                axis=1,
            )
            seen = key <= position
            scores = jnp.where(seen, scores, MASKED)
            now = jnp.maximum(top, jnp.max(scores, axis=1, keepdims=True))
            weights = jnp.where(seen, jnp.exp(scores - now), 0.0)
            scale = jnp.exp(top - now)
            total = total * scale + jnp.sum(weights, axis=1, keepdims=True)
            out = out * scale + dot(weights.astype(jnp.bfloat16), far_ref[:, HEAD_DIM:])
            top = now
        attn_ref[rows, :] = unstacked(out / total).astype(jnp.bfloat16)
        lse_ref[half] = as_row(top + jnp.log(total))
    attn_ref[pl.ds(2 * HALF, short_ref.shape[0]), :] = short_ref[...]


def long_forward(line, q, far, facts, short, rows):
    return line(
        "long_forward",
        long_forward_kernel,
        (q, *far, facts, short),
        [VMEM] * 5 + [SMEM, VMEM],
        [shaped((rows, 256)), shaped((2, 8, 4 * HALF), jnp.float32)],
        [VMEM] * 2,
    )


def grad_terms(q, grad, k, v, seen, lse, delta):
    weights = jnp.where(seen, jnp.exp(dot(k, q, 1, 1) - lse), 0.0)
    grad_scores = (weights * (dot(v, grad, 1, 1) - delta)).astype(jnp.bfloat16)
    return (
        dot(grad_scores, k, 0, 0),
        dot(grad_scores, q),
        dot(weights.astype(jnp.bfloat16), grad),
    )


def row_product(left, right):
    return as_row(
        jnp.sum(left.astype(jnp.float32) * right.astype(jnp.float32), axis=1, keepdims=True)
    )[:1]


def short_backward_kernel(
    qkv_ref, facts_ref, attn_ref, grad_ref, lse_ref, cos_ref, sin_ref, out_ref, dk_ref, dv_ref
):
    packed = attn_ref.shape[0]
    scale = HEAD_DIM**-0.5
    dk_ref[...] = jnp.zeros_like(dk_ref)
    dv_ref[...] = jnp.zeros_like(dv_ref)
    for i, (at, count) in enumerate(blocks_of(packed)):
        rows = pl.ds(2 * HALF + at, count)
        keys = at + count
        q = stacked(qkv_ref[rows, :256]) * jnp.bfloat16(scale)
        k = qkv_ref[pl.ds(2 * HALF, keys), 256:320]
        v = qkv_ref[pl.ds(2 * HALF, keys), 320:384]
        grad = stacked(grad_ref[rows, :])
        delta = row_product(grad, stacked(attn_ref[pl.ds(at, count), :]))
        wide = count if count == HALF else 4 * count
        key = lax.broadcasted_iota(jnp.int32, (keys, wide), 0)
        query = lax.rem(lax.broadcasted_iota(jnp.int32, (1, wide), 1), count) + at
        seen = (key <= query) & (key >= start_of(query, facts_ref))
        seen = jnp.concatenate([seen] * (4 * count // wide), axis=1)
        dq, dk, dv = grad_terms(
            q,
            grad,
            k,
            v,
            seen,
            lse_ref[i, :1, : 4 * count],
            delta,
        )
        out_ref[pl.ds(at, count), :256] = turned(
            unstacked(dq * scale), cos_ref[rows, :], -sin_ref[rows, :]
        ).astype(jnp.bfloat16)
        dk_ref[pl.ds(0, keys), :] += dk
        dv_ref[pl.ds(0, keys), :] += dv
    rows = pl.ds(2 * HALF, packed)
    out_ref[:, 256:] = turned_key(
        jnp.concatenate([dk_ref[...], dv_ref[...]], axis=1), cos_ref[rows, :], -sin_ref[rows, :]
    ).astype(jnp.bfloat16)


def short_backward(line, qkv, facts, attn, grad, lse, cos_rows, sin_rows):
    rows = attn.shape[0]
    return line(
        "short_backward",
        short_backward_kernel,
        (qkv, facts, attn, grad, lse, cos_rows, sin_rows),
        [VMEM, SMEM] + [VMEM] * 5,
        [shaped((rows, 384))],
        [VMEM],
        [pltpu.VMEM((rows, HEAD_DIM), jnp.float32)] * 2,
    )[0]


def long_backward_kernel(q_ref, *refs):
    far_refs = refs[:4]
    facts_ref, attn_ref, grad_ref, lse_ref, cos_ref, sin_ref = refs[4:10]
    dq_ref, far_grad_ref, acc_ref = refs[10:]
    scale = HEAD_DIM**-0.5
    count = far_refs[0].shape[0]
    blocks = count // HALF
    queries = []
    for half in range(2):
        rows = pl.ds(half * HALF, HALF)
        grad = stacked(grad_ref[rows, :])
        column = lax.broadcasted_iota(jnp.int32, (1, HALF), 1)
        queries.append(
            (
                stacked(q_ref[rows, :256]) * jnp.bfloat16(scale),
                grad,
                lse_ref[half, :1],
                row_product(grad, stacked(attn_ref[rows, :])),
                jnp.concatenate([column + facts_ref[FIRST_PLACE + half] * HALF] * 4, axis=1),
            )
        )
    within = lax.broadcasted_iota(jnp.int32, (HALF, 1), 0)
    for i, far_ref in enumerate(far_refs):
        k, v = far_ref[:, :HEAD_DIM], far_ref[:, HEAD_DIM:]
        key = jnp.concatenate(
            [within + facts_ref[FAR_PLACE + i * blocks + n] * HALF for n in range(blocks)], axis=0
        )
        sums = []
        for half, (q, grad, lse, delta, position) in enumerate(queries):
            dq, dk, dv = grad_terms(q, grad, k, v, key <= position, lse, delta)
            acc_ref[half] = dq if i == 0 else acc_ref[half] + dq
            sums.append((dk, dv))
        total = jnp.concatenate(
            [sums[0][0] + sums[1][0], sums[0][1] + sums[1][1]], axis=1
        ).astype(jnp.bfloat16)
        rows = count // 4
        for n in range(4):
            far_grad_ref[n, pl.ds(i * rows, rows), :] = total[n * rows : (n + 1) * rows]
    for half in range(2):
        rows = pl.ds(half * HALF, HALF)
        dq_ref[rows, :] = turned(
            unstacked(acc_ref[half] * scale), cos_ref[rows, :], -sin_ref[rows, :]
        ).astype(jnp.bfloat16)


def long_backward(line, q, far, facts, attn, grad, lse, cos_rows, sin_rows):
    return line(
        "long_backward",
        long_backward_kernel,
        (q, *far, facts, attn, grad, lse, cos_rows, sin_rows),
        [VMEM] * 5 + [SMEM] + [VMEM] * 5,
        [shaped((2 * HALF, 256)), shaped((4, *far[0].shape))],
        [VMEM] * 2,
        [pltpu.VMEM((2, 4 * HALF, HEAD_DIM), jnp.float32)],
    )


def product_kernel(turned_right, left_ref, right_ref, out_ref):
    out_ref[...] = dot(left_ref[...], right_ref[...], 1, 1 if turned_right else 0).astype(
        out_ref.dtype
    )


def product(line, left, right, turned_right=False):
    rows, depth = left.shape
    width = right.shape[0] if turned_right else right.shape[1]
    block = rows // 2
    return line(
        "product",
        functools.partial(product_kernel, turned_right),
        (left, right),
        [rows_of(block, depth), once(right.shape)],
        [shaped((rows, width))],
        [rows_of(block, width)],
        grid=(2,),
    )[0]


def product_parts_kernel(terms, turned_right, *refs):
    outs = refs[2 * terms + 1 :]
    total = refs[2 * terms][...].astype(jnp.float32)
    for k in range(terms):
        total += dot(refs[2 * k][...], refs[2 * k + 1][...], 1, 1 if turned_right else 0)
    rows = outs[0].shape[0]
    for k, out_ref in enumerate(outs):
        out_ref[...] = total[k * rows : (k + 1) * rows].astype(jnp.bfloat16)


def product_parts(line, pairs, sent, turned_right=False):
    rows, width = sent.shape
    block = width // 4
    specs = []
    for left, right in pairs:
        specs.append(once(left.shape))
        if turned_right:
            specs.append(rows_of(block, right.shape[1]))
        else:
            specs.append(columns_of(right.shape[0], block))
    return line(
        "product_parts",
        functools.partial(product_parts_kernel, len(pairs), turned_right),
        [array for pair in pairs for array in pair] + [sent],
        specs + [columns_of(rows, block)],
        [shaped((rows // 4, width))] * 4,
        [columns_of(rows // 4, block)] * 4,
        grid=(4,),
    )


def merged(chunks):
    pieces = []
    for k in range(4):
        for (low, high), chunk in zip(CHUNKS, chunks):
            pieces.append(chunk[k * (high - low) : (k + 1) * (high - low)])
    return jnp.concatenate(pieces, axis=0)


def merged_product_kernel(count, with_sent, *refs):
    left = merged([ref[...] for ref in refs[:count]])
    total = dot(left, refs[count][...])
    outs = refs[count + 1 :]
    if with_sent:
        total += outs[0][...].astype(jnp.float32)
        outs = outs[1:]
    rows = outs[0].shape[0]
    for k, out_ref in enumerate(outs):
        out_ref[...] = total[k * rows : (k + 1) * rows].astype(jnp.bfloat16)


def merged_product(line, chunks, right, sent=None):
    rows = sum([chunk.shape[0] for chunk in chunks])
    depth, width = right.shape
    block = width // 4
    count = 1 if sent is None else 4
    extra = () if sent is None else (sent,)
    return line(
        "merged_product",
        functools.partial(merged_product_kernel, len(chunks), sent is not None),
        (*chunks, right, *extra),
        [once(chunk.shape) for chunk in chunks]
        + [columns_of(depth, block)]
        + [columns_of(rows, block)] * len(extra),
        [shaped((rows // count, width))] * count,
        [columns_of(rows // count, block)] * count,
        grid=(4,),
    )


def merged_back_kernel(count, *refs):
    left = merged([ref[...] for ref in refs[:count]])
    refs[-1][...] = dot(left, refs[count][...], 1, 1).astype(jnp.bfloat16)


def merged_back(line, chunks, right):
    rows = sum([chunk.shape[0] for chunk in chunks])
    return line(
        "merged_back",
        functools.partial(merged_back_kernel, len(chunks)),
        (*chunks, right),
        [VMEM] * (len(chunks) + 1),
        [shaped((rows, right.shape[0]))],
        [VMEM],
    )[0]


def arrange_kernel(facts_ref, rows_ref, *out_refs):
    del facts_ref
    for (low, high), out_ref in zip(CHUNKS, out_refs):
        out_ref[0] = rows_ref[0, low:high, :]


def arrange(line, rows, facts):
    _, count, d = rows.shape
    after = line.last

    def kernel(facts_ref, rows_ref, *refs):
        arrange_kernel(facts_ref, rows_ref, *refs[len(after) :])

    def source(i, facts_ref):
        core = jnp.where(i < 4, facts_ref[CORE_AT], 1 - facts_ref[CORE_AT])
        return core * 4 + (facts_ref[X_AT] + i) % 4, 0, 0

    results = pl.pallas_call(
        kernel,
        grid_spec=pltpu.PrefetchScalarGridSpec(
            num_scalar_prefetch=1,
            grid=(8,),
            in_specs=[pl.BlockSpec((1, count, d), source)] + [ANY] * len(after),
            out_specs=tuple(
                pl.BlockSpec((1, high - low, d), lambda i, facts_ref: (i, 0, 0))
                for low, high in CHUNKS
            ),
        ),
        out_shape=tuple(shaped((8, high - low, d)) for low, high in CHUNKS),
        compiler_params=PARAMS,
        cost_estimate=cost("arrange"),
        name="arrange",
    )(facts, rows, *after)
    return [array.reshape(-1, d) for array in results]


def weight_grad_kernel(count, beside, facts, *refs):
    facts_ref, *refs = refs if facts else (None, *refs)
    out_ref, width = refs[-1], refs[count].shape[1]
    total = dot(refs[0][...], refs[count][...], 0, 0)
    for k in range(1, count):
        total += dot(refs[k][...], refs[count + k][...], 0, 0)
    total = total.astype(jnp.bfloat16)
    if facts:
        rows = total.shape[0] // 2
        own_first = jnp.concatenate([total[rows:], total[:rows]])
        total = jnp.where(facts_ref[CORE_AT] == 0, total, own_first)
    out_ref[:, :width] = total
    if beside:
        out_ref[:, width:] = refs[2 * count][...]


def weight_grad(line, left, right, beside=(), facts=None):
    left = [piece if isinstance(piece, tuple) else (piece, 0) for piece in left]
    columns, width = left[0][0].shape[1], right[0].shape[1]
    whole = width + sum([array.shape[1] for array in beside])
    block = columns // 8

    def place(i, *facts_ref):
        if facts_ref:
            z = (i - facts_ref[0][Z_AT]) % 4
            yh = (i // 4 + facts_ref[0][YH_AT]) % 2
            return z * 2 + yh, 0
        return i % 4 * 2 + i // 4, 0

    def whole_block(i, *facts_ref):
        return 0, 0

    operands = (*[array for array, _ in left], *right, *beside)
    in_specs = (
        [
            pl.BlockSpec((part.shape[0], block), lambda i, *_, at=at: (at, i))
            for (_, at), part in zip(left, right)
        ]
        + [pl.BlockSpec(part.shape, whole_block, pipeline_mode=pl.Buffered(1)) for part in right]
        + [pl.BlockSpec((block, array.shape[1]), place) for array in beside]
    )
    out_spec = pl.BlockSpec((block, whole), place)
    kernel = functools.partial(weight_grad_kernel, len(left), len(beside), facts is not None)
    if facts is None:
        return line(
            "weight_grad",
            kernel,
            operands,
            in_specs,
            [shaped((columns, whole))],
            [out_spec],
            grid=(8,),
        )[0]
    after, count = line.last, len(operands) + 1

    def ordered(*refs):
        kernel(*refs[:count], *refs[count + len(after) :])

    result = pl.pallas_call(
        ordered,
        grid_spec=pltpu.PrefetchScalarGridSpec(
            num_scalar_prefetch=1,
            grid=(8,),
            in_specs=in_specs + [ANY] * len(after),
            out_specs=out_spec,
        ),
        out_shape=shaped((columns, whole)),
        compiler_params=PARAMS,
        cost_estimate=cost("weight_grad"),
        name="weight_grad",
    )(facts, *operands, *after)
    line.last = (result,)
    return result


def mix_kernel(low, high, tokens_ref, gain_ref, *refs):
    parts, (mixed_ref, hidden_ref) = refs[:4], refs[4:]
    mixed = tokens_ref[low:high, :].astype(jnp.float32) + total_of([ref[...] for ref in parts])
    inv = lax.rsqrt(jnp.mean(mixed * mixed, axis=-1, keepdims=True) + EPS)
    mixed_ref[...] = mixed
    hidden_ref[...] = (mixed * inv * gain_ref[...]).astype(jnp.bfloat16)


def mix(line, chunk, tokens, gain, parts):
    low, high = chunk
    d = tokens.shape[1]
    return line(
        "mix",
        functools.partial(mix_kernel, low, high),
        (tokens, gain, *parts),
        [VMEM] * 6,
        [shaped((high - low, d), jnp.float32), shaped((high - low, d))],
        [VMEM] * 2,
    )


def norm_back(grad_in, values, gain):
    inv = lax.rsqrt(jnp.mean(values * values, axis=-1, keepdims=True) + EPS)
    unit = values * inv
    scaled = grad_in * gain
    return inv * (scaled - unit * jnp.mean(scaled * unit, axis=-1, keepdims=True)), unit


def mix_back_kernel(low, high, grad_ref, mixed_ref, gain_ref, *refs):
    parts, (total_ref, low_ref, part_ref) = refs[:4], refs[4:]
    grad_in = total_of([ref[...] for ref in parts])
    back, unit = norm_back(grad_in, mixed_ref[...], gain_ref[...])
    total = grad_ref[low:high, :].astype(jnp.float32) + back
    total_ref[...] = total
    low_ref[...] = total.astype(jnp.bfloat16)
    part_ref[...] = jnp.sum(grad_in * unit, axis=0, keepdims=True)


def mix_back(line, chunk, grad, mixed, gain, parts):
    low, high = chunk
    rows, d = mixed.shape
    return line(
        "mix_back",
        functools.partial(mix_back_kernel, low, high),
        (grad, mixed, gain, *parts),
        [VMEM] * 7,
        [shaped((rows, d), jnp.float32), shaped((rows, d)), shaped((1, d), jnp.float32)],
        [VMEM] * 3,
    )


def mlp_kernel(hidden_ref, grad_act_ref, gate_ref, up_ref, act_ref, gate_out_ref, up_out_ref, *refs):
    hidden = hidden_ref[...]
    gate = dot(hidden, gate_ref[...])
    up = dot(hidden, up_ref[...])
    grad_act = grad_act_ref[...].astype(jnp.float32)
    sig = jax.nn.sigmoid(gate)
    silu = gate * sig
    act_ref[...] = (silu * up).astype(jnp.bfloat16)
    grad_gate = (grad_act * up * sig * (1.0 + gate * (1.0 - sig))).astype(jnp.bfloat16)
    grad_up = (grad_act * silu).astype(jnp.bfloat16)
    gate_out_ref[...] = grad_gate
    up_out_ref[...] = grad_up
    if refs:
        i = pl.program_id(0)
        back_ref, acc_ref = refs
        part = dot(grad_gate, gate_ref[...], 1, 1) + dot(grad_up, up_ref[...], 1, 1)

        @pl.when(i == 0)
        def _():
            acc_ref[...] = part

        @pl.when((i > 0) & (i < pl.num_programs(0) - 1))
        def _():
            acc_ref[...] += part

        @pl.when(i == pl.num_programs(0) - 1)
        def _():
            back_ref[...] = (acc_ref[...] + part).astype(jnp.bfloat16)


def mlp(line, hidden, grad_act, at, w_gate, w_up, with_back):
    rows, d = hidden.shape
    width = w_gate.shape[1]
    block = width // 4
    outs = [shaped((rows, width))] * 3
    out_specs = [columns_of(rows, block)] * 3
    if with_back:
        outs.append(shaped((rows, d)))
        out_specs.append(pl.BlockSpec((rows, d), lambda i: (0, 0)))
    return line(
        "mlp",
        mlp_kernel,
        (hidden, grad_act, w_gate, w_up),
        [
            once((rows, d)),
            pl.BlockSpec((rows, block), lambda i: (at, i)),
            columns_of(d, block),
            columns_of(d, block),
        ],
        outs,
        out_specs,
        [pltpu.VMEM((rows, d), jnp.float32)] if with_back else [],
        grid=(4,),
    )


def hidden_grad_kernel(with_sent, low_ref, query_ref, kv_ref, hidden_ref, *refs):
    low = low_ref[...]
    grad = dot(low[:, :256], query_ref[...], 1, 1) + dot(low[:, 256:], kv_ref[...], 1, 1)
    gain = jnp.sum(grad * hidden_ref[...].astype(jnp.float32), axis=0, keepdims=True)
    if not with_sent:
        refs[0][...] = grad.astype(jnp.bfloat16)
        refs[1][...] = gain
        return
    sent_ref, gain_ref, mlp_gain_ref, *outs = refs
    grad += sent_ref[...].astype(jnp.float32)
    rows = outs[0].shape[0] - 8
    tail = []
    for values in (gain + gain_ref[...], mlp_gain_ref[...]):
        high = values.astype(jnp.bfloat16)
        tail += [high, (values - high.astype(jnp.float32)).astype(jnp.bfloat16)]
    tail = jnp.concatenate(tail + [jnp.zeros_like(tail[0])] * 4, axis=0)
    for k, out_ref in enumerate(outs):
        part = grad[k * rows : (k + 1) * rows].astype(jnp.bfloat16)
        out_ref[...] = jnp.concatenate([part, tail], axis=0)


def hidden_grad(line, low, w_query, w_key_value, hidden, sent=()):
    rows, d = hidden.shape
    block = d // 4
    if sent:
        outs = [shaped((rows // 4 + 8, d))] * 4
        out_specs = [columns_of(rows // 4 + 8, block)] * 4
    else:
        outs = [shaped((rows, d)), shaped((1, d), jnp.float32)]
        out_specs = [columns_of(rows, block), columns_of(1, block)]
    return line(
        "hidden_grad",
        functools.partial(hidden_grad_kernel, bool(sent)),
        (low, w_query, w_key_value, hidden, *sent),
        [once((rows, 384)), rows_of(block, 256), rows_of(block, 128), columns_of(rows, block)]
        + [columns_of(array.shape[0], block) for array in sent],
        outs,
        out_specs,
        grid=(4,),
    )


def gate_kernel(*refs):
    del refs


def gated(line, arrays):
    line.last = tuple([array for array in line.last if all([array is not one for one in arrays])])
    return line(
        "gated",
        gate_kernel,
        arrays,
        [ANY] * len(arrays),
        [shaped(array.shape, array.dtype) for array in arrays],
        [ANY] * len(arrays),
        input_output_aliases={k: k for k in range(len(arrays))},
    )


def out_mix_kernel(*refs):
    mixed = jnp.concatenate([ref[...] for ref in refs[:-5]], axis=0)
    refs[-1][...] = (mixed + total_of([ref[...] for ref in refs[-5:-1]])).astype(jnp.bfloat16)


def final_kernel(tokens_ref, gain_ref, *refs):
    out_ref, gains_ref = refs[-2:]
    total = total_of([ref[...] for ref in refs[-6:-2]])
    rows = out_ref.shape[0]
    back, _ = norm_back(total[:rows], tokens_ref[...].astype(jnp.float32), gain_ref[...])
    mixed = jnp.concatenate([ref[...] for ref in refs[:-6]], axis=0)
    out_ref[...] = (mixed + back).astype(jnp.bfloat16)
    sums = total[rows : rows + 8]
    gains_ref[...] = jnp.concatenate([sums[:1] + sums[1:2], sums[2:3] + sums[3:4]], axis=0)


def turn_far_kernel(grad_ref, cos_ref, sin_ref, long_ref, short_ref, out_ref):
    rows = pl.ds(0, 2 * HALF)
    out_ref[rows, :256] = long_ref[...]
    out_ref[rows, 256:] = turned_key(grad_ref[...], cos_ref[rows, :], -sin_ref[rows, :]).astype(
        jnp.bfloat16
    )
    out_ref[pl.ds(2 * HALF, short_ref.shape[0]), :] = short_ref[...]


def local(
    tokens,
    lengths,
    place,
    attn_gain,
    w_query,
    w_key,
    w_value,
    w_out,
    mlp_gain,
    w_gate,
    w_up,
    w_down,
    out_grad,
):
    rows, d = tokens.shape
    group_rows = rows * 8
    half_rows = rows * 4
    long_rows = 2 * HALF
    dp_index, mp_index = lax.axis_index("dp"), lax.axis_index("mp")
    yh, z, core = dp_index // 8, dp_index // 2 % 4, dp_index % 2
    yl, x = mp_index // 4, mp_index % 4
    native = core == yl
    line = Line()
    mlp_gain_row = mlp_gain.reshape(1, d)

    tokens = send(tokens, TURN)
    lengths = send(lengths, TURN)[0]
    w_key_value = send(jnp.concatenate([w_key, w_value], axis=1), WEIGHT_LOW)
    w_query = send(w_query, WEIGHT_LOW)
    w_out = send(w_out, WEIGHT_LOW)
    w_down = send(w_down, WEIGHT_HIGH)
    w_gate = send(w_gate, WEIGHT_LOW)
    w_up = send(w_up, WEIGHT_HIGH)
    out_grad = send(out_grad, TURN)

    step = jnp.arange(16, dtype=jnp.int32)
    far_yh = jnp.where(step % 4 >= 2, 1 - yh, yh)
    far_yl = jnp.where((step % 4 == 1) | (step % 4 == 2), 1 - yl, yl)
    far_group = (far_yh * 4 + (z + step // 4) % 4) * 2 + far_yl
    far_index = (2 * far_group[:, None] + jnp.arange(2, dtype=jnp.int32)[None, :]).reshape(-1)
    half_ids = jnp.arange(place.shape[0], dtype=jnp.int32)
    far_place = jnp.sum(jnp.where(far_index[:, None] == half_ids[None, :], place, 0), axis=1)
    facts = jnp.concatenate(
        [
            far_place[:2],
            jnp.stack([lengths[0], lengths[0] + lengths[1], core, x, z, yh]),
            far_place,
        ]
    ).astype(jnp.int32)

    residual = tokens.astype(jnp.float32)
    inv_one = lax.rsqrt(jnp.mean(residual * residual, axis=-1, keepdims=True) + EPS)
    hidden_one = collect((residual * inv_one * attn_gain).astype(jnp.bfloat16))
    freq = jnp.tile(inverse_freq(HEAD_DIM), 4).reshape(1, 128)
    line.last += (w_query, w_key_value)
    cos_gathered, sin_gathered, cos_ordered, sin_ordered = line(
        "tables",
        functools.partial(tables_kernel, rows),
        (facts, freq),
        [SMEM, VMEM],
        [shaped((n, 128), jnp.float32) for n in (group_rows,) * 4],
        [VMEM] * 4,
    )
    hidden_own = join(line, hidden_one)
    hidden_one = (hidden_own, send(hidden_own, CORE))
    qkv = []
    for at, half in enumerate(hidden_one):
        line.last += (w_down,) * at
        qkv.append(
            project_qkv(line, half, w_query, w_key_value, cos_gathered, sin_gathered, at)
        )
    (out_grad,) = gated(line, (out_grad,))
    grad_rows = lax.all_gather(out_grad, BOTH, axis=0, axis_index_groups=CHIP_GROUPS)
    qkv = in_order(jnp.stack(qkv), core, x)
    near_rows = qkv[:long_rows, 256:]
    ring_rows = jnp.concatenate(
        [near_rows, send(near_rows, Y_LOW), send(near_rows, Y_HIGH), send(near_rows, Y_FAR)]
    )
    far_rows = (
        ring_rows, send(ring_rows, Z_DOWN), send(ring_rows, Z_FAR), send(ring_rows, Z_UP)
    )
    line.last += (ring_rows, w_out)
    short_attn, short_lse = short_forward(line, qkv, facts)
    attn_ordered, long_lse = long_forward(line, qkv, far_rows, facts, short_attn, group_rows)
    attn_rows = from_order(attn_ordered, core, x)
    attn_rows = [chunks_of(attn_rows[half]) for half in range(2)]

    sent = [send(product(line, part, w_out), CORE) for part in attn_rows[1]]
    mixed_parts = [
        scatter(product_parts(line, [(part, w_out)], other))
        for part, other in zip(attn_rows[0], sent)
    ]
    grad_rows = arrange(line, grad_rows, facts)
    grad_act = [product(line, part, w_down, True) for part in grad_rows]
    mixed, hidden_two = [], []
    for chunk, parts in zip(CHUNKS, mixed_parts):
        mixed_rows, hidden_rows = mix(line, chunk, tokens, mlp_gain_row, parts)
        mixed.append(mixed_rows)
        hidden_two.append(collect(hidden_rows))

    count = len(CHUNKS)
    own, other, act, gate, up, back = ([None] * count for _ in range(6))

    def first_half(n):
        own[n] = join(line, hidden_two[n])
        other[n] = send(own[n], CORE)
        act[n], gate[n], up[n] = mlp(line, own[n], grad_act[n], 0, w_gate, w_up, False)

    def second_half(n):
        *terms, sum_back = mlp(line, other[n], grad_act[n], 1, w_gate, w_up, True)
        act[n], gate[n], up[n] = zip((act[n], gate[n], up[n]), terms)
        back[n] = send(sum_back, CORE)

    hidden_parts = []
    first_half(0)
    second_half(0)
    for n in range(count):
        if n + 1 < count:
            first_half(n + 1)
        if n + 1 == count:
            (down_rows,) = merged_product(line, [part[1] for part in act], w_down)
            down_rows = send(down_rows, CORE)
        terms = [(gate[n][0], w_gate), (up[n][0], w_up)]
        hidden_parts.append(scatter(product_parts(line, terms, back[n], True)))
        if n + 1 < count:
            second_half(n + 1)
    act, gate, up = [[pair[k] for pair in part for k in range(2)] for part in (act, gate, up)]
    hidden_two = [piece for pair in zip(own, other) for piece in pair]

    pieces = [(part, at) for part in grad_rows for at in range(2)]
    ff_part = weight_grad(line, pieces, act)
    ff_part = weight_grad(line, hidden_two, gate, (ff_part,))
    ff_part = weight_grad(line, hidden_two, up, (ff_part,))
    grad_mixed, mixed_grad, gain_parts = [], [], []
    for n, (chunk, parts) in enumerate(zip(CHUNKS, hidden_parts)):
        total, low, gain_part = mix_back(line, chunk, out_grad, mixed[n], mlp_gain_row, parts)
        grad_mixed.append(total)
        mixed_grad.append(collect(low))
        gain_parts.append(gain_part)
    ff_sum = reduce_y(reduce_near(gated(line, (ff_part,))[0]))
    out_parts = scatter(merged_product(line, act[0::2], w_down, down_rows))

    grad_own = [join(line, parts) for parts in mixed_grad]
    grad_other = [send(part, CORE) for part in grad_own]
    grad_attn = jnp.stack([merged_back(line, part, w_out) for part in (grad_own, grad_other)])
    grad_attn = in_order(grad_attn, core, x)
    long_dq, far_terms = long_backward(
        line,
        qkv,
        far_rows,
        facts,
        attn_ordered,
        grad_attn,
        long_lse,
        cos_ordered,
        sin_ordered,
    )
    ring_terms = total_of(
        (
            far_terms[0],
            send(far_terms[1], Y_LOW),
            send(far_terms[2], Y_HIGH),
            send(far_terms[3], Y_FAR),
        )
    ).astype(jnp.bfloat16)
    near = ring_terms.reshape(4, long_rows, -1)
    far_grads = total_of(
        (near[0], send(near[1], Z_UP), send(near[2], Z_FAR), send(near[3], Z_DOWN))
    )
    line.last += out_parts[1:]
    short_low = short_backward(
        line, qkv, facts, short_attn, grad_attn, short_lse, cos_ordered, sin_ordered
    )
    out_part = weight_grad(
        line,
        [piece for pair in zip(grad_own, grad_other) for piece in pair],
        [piece for pair in zip(*attn_rows) for piece in pair],
        (),
        facts,
    )
    (low_ordered,) = line(
        "turn_far",
        turn_far_kernel,
        (far_grads, cos_ordered, sin_ordered, long_dq, short_low),
        [VMEM] * 5,
        [shaped((group_rows, 384))],
        [VMEM],
    )
    low_rows = from_order(low_ordered, core, x)
    back, gain_other = hidden_grad(line, low_rows[1], w_query, w_key_value, hidden_one[1])
    back = send(back, CORE)
    last_part = weight_grad(line, hidden_one, (low_rows[0], low_rows[1]), (out_part,), facts)
    grad_parts = scatter(
        hidden_grad(
            line,
            low_rows[0],
            w_query,
            w_key_value,
            hidden_one[0],
            (back, gain_other, sum(gain_parts[1:], gain_parts[0])),
        )[:4]
    )
    (output,) = line(
        "out_mix",
        out_mix_kernel,
        (*mixed, *out_parts),
        [VMEM] * (len(mixed) + 4),
        [shaped((rows, d))],
        [VMEM],
    )
    output = send(output, TURN)
    last_kept = reduce_ring(gated(line, (last_part,))[0])
    grad_tokens, gains = line(
        "final",
        final_kernel,
        (tokens, attn_gain.reshape(1, d), *grad_mixed, *grad_parts),
        [VMEM] * (2 + len(grad_mixed) + 4),
        [shaped((rows, d)), shaped((2, d), jnp.float32)],
        [VMEM] * 2,
    )
    grad_tokens = send(grad_tokens, TURN)
    gains = all_sum(gains)
    last_sum = sum_groups(last_kept, native)
    ff = w_gate.shape[1]
    return (
        output,
        grad_tokens,
        gains[0] / attn_gain,
        last_sum[:, :256],
        last_sum[:, 256:320],
        last_sum[:, 320:384],
        last_sum[:, 384:].T,
        gains[1],
        ff_sum[:, ff : 2 * ff],
        ff_sum[:, :ff],
        ff_sum[:, 2 * ff :].T,
    )


def solution(mesh):
    placed = (
        P(("dp", "mp"), None),
        P("dp", None),
        P(),
        P(),
        P(None, "mp"),
        P(None, "mp"),
        P(None, "mp"),
        P("mp", None),
        P(),
        P(None, "mp"),
        P(None, "mp"),
        P("mp", None),
        P(("dp", "mp"), None),
    )
    return jax.shard_map(
        local,
        mesh=mesh,
        in_specs=placed,
        out_specs=(
            P(("dp", "mp"), None),
            P(("dp", "mp"), None),
            P(),
            P("dp", "mp"),
            P("dp", "mp"),
            P("dp", "mp"),
            P("mp", "dp"),
            P(),
            P("dp", "mp"),
            P("dp", "mp"),
            P("mp", "dp"),
        ),
        check_vma=False,
    )
```

```python
import functools

import jax
import jax.numpy as jnp
from jax import lax
from jax.experimental import pallas as pl
from jax.experimental.pallas import tpu as pltpu
from jax.sharding import PartitionSpec as P

HEAD_DIM = 64
HALF = 128
MASKED = -1e30


EPS = 1e-05
THETA = 500000.0

BOTH = ("dp", "mp")


def place_of(yh, z, c, yl, x):
    return ((yh * 4 + z) * 2 + c) * 8 + yl * 4 + x


def pairs_of(target, sender=lambda yh, z, c, yl, x: True):
    return [
        (place_of(yh, z, c, yl, x), place_of(*target(yh, z, c, yl, x)))
        for yh in range(2)
        for z in range(4)
        for c in range(2)
        for yl in range(2)
        for x in range(4)
        if sender(yh, z, c, yl, x)
    ]


X_UP = pairs_of(lambda yh, z, c, yl, x: (yh, z, c, yl, (x + 1) % 4))
X_DOWN = pairs_of(lambda yh, z, c, yl, x: (yh, z, c, yl, (x + 3) % 4))
X_FAR = pairs_of(lambda yh, z, c, yl, x: (yh, z, c, yl, (x + 2) % 4))
Z_UP = pairs_of(lambda yh, z, c, yl, x: (yh, (z + 1) % 4, c, yl, x))
Z_DOWN = pairs_of(lambda yh, z, c, yl, x: (yh, (z + 3) % 4, c, yl, x))
Z_FAR = pairs_of(lambda yh, z, c, yl, x: (yh, (z + 2) % 4, c, yl, x))
CORE = pairs_of(lambda yh, z, c, yl, x: (yh, z, 1 - c, yl, x))
Y_LOW = pairs_of(lambda yh, z, c, yl, x: (yh, z, c, 1 - yl, x))
Y_HIGH = pairs_of(lambda yh, z, c, yl, x: (1 - yh, z, c, 1 - yl, x))
Y_FAR = pairs_of(lambda yh, z, c, yl, x: (1 - yh, z, c, yl, x))
TURN = pairs_of(lambda yh, z, c, yl, x: (yh, z, yl, c, x))
NATIVE = lambda yh, z, c, yl, x: c == yl
FOREIGN = lambda yh, z, c, yl, x: c != yl
FOREIGN_TURN = pairs_of(lambda yh, z, c, yl, x: (yh, z, yl, c, x), FOREIGN)
FOREIGN_LOW = pairs_of(lambda yh, z, c, yl, x: (yh, z, c, 1 - yl, x), FOREIGN)
FOREIGN_HIGH = pairs_of(lambda yh, z, c, yl, x: (1 - yh, z, c, 1 - yl, x), FOREIGN)
NATIVE_FAR = pairs_of(lambda yh, z, c, yl, x: (1 - yh, z, c, yl, x), NATIVE)
NATIVE_CORE = pairs_of(lambda yh, z, c, yl, x: (yh, z, 1 - c, yl, x), NATIVE)
WEIGHT_LOW = pairs_of(
    lambda yh, z, c, yl, x: (yh, z, c, 1 - yl, x) if c == yl else (yh, z, 1 - c, yl, x)
)
WEIGHT_HIGH = pairs_of(
    lambda yh, z, c, yl, x: (1 - yh, z, c, 1 - yl, x) if c == yl else (yh, z, 1 - c, yl, x)
)
Z_GROUPS = [
    [place_of(yh, z, c, yl, x) for z in range(4)]
    for yh in range(2)
    for c in range(2)
    for yl in range(2)
    for x in range(4)
]


Y_GROUPS = [
    [place_of(yh, z, c, yl, x) for yh in range(2) for yl in range(2)]
    for z in range(4)
    for c in range(2)
    for x in range(4)
]
CHIP_GROUPS = [
    [place_of(yh, z, c, yl, x) for c in range(2) for x in range(4)]
    for yh in range(2)
    for z in range(4)
    for yl in range(2)
]


def send(values, pairs):
    return lax.ppermute(values, BOTH, pairs)


CHUNKS = ((0, 136),)

VMEM = pl.BlockSpec(memory_space=pltpu.VMEM)
SMEM = pl.BlockSpec(memory_space=pltpu.SMEM)
ANY = pl.BlockSpec(memory_space=pl.ANY)
PARAMS = pltpu.CompilerParams(vmem_limit_bytes=64 * 1024 * 1024)
LASTS = {
    "tables": 1,
    "join": 1,
    "project_qkv": 1,
    "short_forward": 6,
    "long_forward": 13,
    "product": 3,
    "product_parts": 5,
    "arrange": 5,
    "mix": 3,
    "mlp": 10,
    "weight_grad": 2,
    "mix_back": 4,
    "merged_product": 2,
    "merged_back": 3,
    "long_backward": 16,
    "short_backward": 10,
    "turn_far": 2,
    "hidden_grad": 5,
    "out_mix": 4,
    "final": 4,
    "gated": 1,
}


def cost(name):
    return pl.CostEstimate(
        flops=int(1.15e9 * LASTS[name]), bytes_accessed=1000, transcendentals=0
    )


def shaped(shape, dtype=jnp.bfloat16):
    return pltpu.HBM(tuple(shape), dtype)


def rows_of(block, width):
    return pl.BlockSpec((block, width), lambda i: (i, 0))


def columns_of(rows, block):
    return pl.BlockSpec((rows, block), lambda i: (0, i))


def once(shape):
    return pl.BlockSpec(tuple(shape), lambda i: (0,) * len(shape), pipeline_mode=pl.Buffered(1))


class Line:
    def __init__(self):
        self.last = ()

    def __call__(self, name, kernel, operands, in_specs, outs, out_specs, scratch=(), **grid):
        after = self.last
        count = len(operands)

        def ordered(*refs):
            kernel(*refs[:count], *refs[count + len(after) :])

        results = pl.pallas_call(
            ordered,
            out_shape=tuple(outs),
            in_specs=list(in_specs) + [ANY] * len(after),
            out_specs=tuple(out_specs),
            scratch_shapes=list(scratch),
            compiler_params=PARAMS,
            cost_estimate=cost(name),
            name=name,
            **grid,
        )(*operands, *after)
        self.last = (min(results, key=lambda array: array.size),)
        return results


def turn(values, native):
    return jnp.where(native, values, send(values, FOREIGN_TURN))


def dot(left, right, left_dim=1, right_dim=0):
    return lax.dot_general(
        left, right, (((left_dim,), (right_dim,)), ((), ())), preferred_element_type=jnp.float32
    )


def total_of(parts):
    one, two, three, four = [part.astype(jnp.float32) for part in parts]
    return (one + two) + (three + four)


def scatter(parts):
    return (
        parts[0],
        send(parts[1], X_UP),
        send(parts[2], X_FAR),
        send(parts[3], X_DOWN),
    )


def collect(rows):
    return (rows, send(rows, X_DOWN), send(rows, X_FAR), send(rows, X_UP))


def in_order(pair, core, x):
    half = pair.shape[1]
    start = (4 - x) % 4 * (half // 4)
    pair = lax.dynamic_slice_in_dim(jnp.concatenate([pair, pair], axis=1), start, half, axis=1)
    return jnp.where(core == 0, pair, pair[::-1]).reshape(2 * half, -1)


def from_order(values, core, x):
    half = values.shape[0] // 2
    pair = values.reshape(2, half, -1)
    pair = jnp.where(core == 0, pair, pair[::-1])
    return lax.dynamic_slice_in_dim(
        jnp.concatenate([pair, pair], axis=1), x * (half // 4), half, axis=1
    )


def chunks_of(half):
    cut = half.reshape(4, half.shape[0] // 4, -1)
    return [cut[:, low:high].reshape(4 * (high - low), -1) for low, high in CHUNKS]


def plus(left, right):
    return (left.astype(jnp.float32) + right.astype(jnp.float32)).astype(jnp.bfloat16)


def reduce_near(grad):
    return lax.psum_scatter(
        grad, BOTH, scatter_dimension=0, tiled=True, axis_index_groups=Z_GROUPS
    )


def reduce_y(kept):
    kept = lax.psum_scatter(
        kept, BOTH, scatter_dimension=0, tiled=True, axis_index_groups=Y_GROUPS
    )
    return send(kept, TURN).astype(jnp.float32)


def reduce_ring(grad):
    here, above, far, below = jnp.split(grad, 4)
    rows = far.shape[0] // 2
    from_below, from_above = send(far[:rows], Z_UP), send(far[rows:], Z_DOWN)
    above = send(jnp.concatenate([plus(above[:rows], from_below), above[rows:]]), Z_UP)
    below = send(jnp.concatenate([below[:rows], plus(below[rows:], from_above)]), Z_DOWN)
    total = here.astype(jnp.float32) + above.astype(jnp.float32) + below.astype(jnp.float32)
    return total.astype(jnp.bfloat16), (from_below, from_above)


def sum_groups(kept, native):
    near, far = jnp.split(kept, 2)
    across, low, high = send(far, NATIVE_FAR), send(near, FOREIGN_LOW), send(far, FOREIGN_HIGH)
    total = total_of((near, low, high, across))
    rows = total.shape[0] // 2
    passed = send(total[rows:].astype(jnp.bfloat16), NATIVE_CORE).astype(jnp.float32)
    return jnp.where(native, total[:rows], passed)


def all_sum(values):
    for group in ((CORE,), (Z_UP, Z_DOWN, Z_FAR), (Y_LOW, Y_HIGH, Y_FAR)):
        values = sum([send(values, pairs) for pairs in group], values)
    return values


def inverse_freq(head_width):
    indices = jnp.arange(head_width // 2, dtype=jnp.float32)
    base_freq = jnp.exp(-jnp.log(THETA) * 2.0 * indices / head_width)
    wavelength = 2.0 * jnp.pi / base_freq
    smooth = (8192.0 / wavelength - 1.0) / 3.0
    blended = (1.0 - smooth) * base_freq / 32.0 + smooth * base_freq
    return jnp.where(
        wavelength < 2048.0, base_freq, jnp.where(wavelength > 8192.0, base_freq / 32.0, blended)
    )


FIRST_PLACE, SECOND_START, THIRD_START, CORE_AT, X_AT, Z_AT, YH_AT, FAR_PLACE = 0, 2, 3, 4, 5, 6, 7, 8


def tables_kernel(rows, facts_ref, freq_ref, *out_refs):
    sign = jnp.where(lax.broadcasted_iota(jnp.int32, (1, 128), 1) % 64 < 32, -1.0, 1.0)
    group_rows, half_rows = rows * 8, rows * 4
    for gathered, (cos_ref, sin_ref) in enumerate((out_refs[:2], out_refs[2:])):
        row = lax.broadcasted_iota(jnp.int32, cos_ref.shape, 0)
        if gathered == 0:
            other = (row >= half_rows).astype(jnp.int32)
            rest = row - other * half_rows
            step = sum([(rest >= k * rows).astype(jnp.int32) for k in (1, 2, 3)])
            core = jnp.where(other == 0, facts_ref[CORE_AT], 1 - facts_ref[CORE_AT])
            row = core * half_rows + ((facts_ref[X_AT] + step) & 3) * rows + rest - step * rows
        packed = row - 2 * HALF
        second, third = facts_ref[SECOND_START], facts_ref[THIRD_START]
        start = jnp.where(packed >= third, third, jnp.where(packed >= second, second, 0))
        own = jnp.where(row < HALF, facts_ref[FIRST_PLACE], facts_ref[FIRST_PLACE + 1])
        position = jnp.where(row < 2 * HALF, own * HALF + (row & (HALF - 1)), packed - start)
        angles = position.astype(jnp.float32) * freq_ref[...]
        cos_ref[...] = jnp.cos(angles)
        sin_ref[...] = jnp.sin(angles) * sign


def turned(values, cos_rows, sin_rows):
    first = lax.broadcasted_iota(jnp.int32, (1, 128), 1) % 64 < 32
    tiles = []
    for at in range(0, values.shape[1], 128):
        tile = values[:, at : at + 128]
        swapped = jnp.where(first, pltpu.roll(tile, 96, 1), pltpu.roll(tile, 32, 1))
        tiles.append(tile * cos_rows + swapped * sin_rows)
    return tiles[0] if len(tiles) == 1 else jnp.concatenate(tiles, axis=1)


def turned_key(values, cos_rows, sin_rows):
    key = lax.broadcasted_iota(jnp.int32, (1, 128), 1) < HEAD_DIM
    return jnp.where(key, turned(values, cos_rows, sin_rows), values)


def join_kernel(count, *refs):
    for k in range(count):
        refs[-1][k] = refs[k][...]


def join(line, pieces):
    count = len(pieces)
    rows, width = pieces[0].shape
    block = width // 2
    (joined,) = line(
        "join",
        functools.partial(join_kernel, count),
        pieces,
        [columns_of(rows, block)] * count,
        [shaped((count, rows, width))],
        [pl.BlockSpec((count, rows, block), lambda i: (0, 0, i))],
        grid=(2,),
    )
    return joined.reshape(count * rows, width)


def qkv_kernel(hidden_ref, query_ref, kv_ref, cos_ref, sin_ref, out_ref):
    hidden = hidden_ref[...]
    cos_rows, sin_rows = cos_ref[...], sin_ref[...]
    out_ref[:, :256] = turned(dot(hidden, query_ref[...]), cos_rows, sin_rows).astype(jnp.bfloat16)
    out_ref[:, 256:] = turned_key(dot(hidden, kv_ref[...]), cos_rows, sin_rows).astype(
        jnp.bfloat16
    )


def project_qkv(line, hidden, w_query, w_key_value, cos_rows, sin_rows, at):
    rows, d = hidden.shape
    block = rows // 2
    table = pl.BlockSpec((block, 128), lambda i: (i + 2 * at, 0))
    return line(
        "project_qkv",
        qkv_kernel,
        (hidden, w_query, w_key_value, cos_rows, sin_rows),
        [rows_of(block, d), once((d, 256)), once((d, 128)), table, table],
        [shaped((rows, 384))],
        [rows_of(block, 384)],
        grid=(2,),
    )[0]


def stacked(block):
    return jnp.concatenate(
        [block[:, h * HEAD_DIM : (h + 1) * HEAD_DIM] for h in range(4)], axis=0
    )


def unstacked(block):
    rows = block.shape[0] // 4
    return jnp.concatenate([block[h * rows : (h + 1) * rows] for h in range(4)], axis=1)


def as_row(column):
    return jnp.transpose(jnp.broadcast_to(column, (column.shape[0], 128)))[:8]


def start_of(row, facts_ref):
    second, third = facts_ref[SECOND_START], facts_ref[THIRD_START]
    return jnp.where(row >= third, third, jnp.where(row >= second, second, 0))


def blocks_of(rows):
    return [(at, min(HALF, rows - at)) for at in range(0, rows, HALF)]


def short_forward_kernel(qkv_ref, facts_ref, attn_ref, lse_ref):
    for i, (at, count) in enumerate(blocks_of(attn_ref.shape[0])):
        rows = pl.ds(2 * HALF + at, count)
        keys = at + count
        q = stacked(qkv_ref[rows, :256]) * jnp.bfloat16(HEAD_DIM**-0.5)
        k = qkv_ref[pl.ds(2 * HALF, keys), 256:320]
        v = qkv_ref[pl.ds(2 * HALF, keys), 320:384]
        scores = dot(q, k, 1, 1)
        column = lax.broadcasted_iota(jnp.int32, (count, keys), 1)
        row = lax.broadcasted_iota(jnp.int32, (count, 1), 0) + at
        seen = (column <= row) & (column >= start_of(row, facts_ref))
        scores = jnp.where(jnp.concatenate([seen] * 4, axis=0), scores, MASKED)
        top = jnp.max(scores, axis=1, keepdims=True)
        weights = jnp.exp(scores - top)
        total = jnp.sum(weights, axis=1, keepdims=True)
        out = dot(weights.astype(jnp.bfloat16), v) / total
        attn_ref[pl.ds(at, count), :] = unstacked(out).astype(jnp.bfloat16)
        lse_ref[i, :, : 4 * count] = as_row(top + jnp.log(total))


def short_forward(line, qkv, facts):
    rows = qkv.shape[0] - 2 * HALF
    return line(
        "short_forward",
        short_forward_kernel,
        (qkv, facts),
        [VMEM, SMEM],
        [shaped((rows, 256)), shaped((len(blocks_of(rows)), 8, 4 * HALF), jnp.float32)],
        [VMEM] * 2,
    )


def long_forward_kernel(q_ref, *refs):
    far_refs, (facts_ref, short_ref, attn_ref, lse_ref) = refs[:4], refs[4:]
    within = lax.broadcasted_iota(jnp.int32, (1, HALF), 1)
    blocks = far_refs[0].shape[0] // HALF
    for half in range(2):
        rows = pl.ds(half * HALF, HALF)
        q = stacked(q_ref[rows, :256]) * jnp.bfloat16(HEAD_DIM**-0.5)
        row = lax.broadcasted_iota(jnp.int32, (HALF, 1), 0)
        position = jnp.concatenate([row + facts_ref[FIRST_PLACE + half] * HALF] * 4, axis=0)
        top = jnp.full((4 * HALF, 1), MASKED, jnp.float32)
        total = jnp.zeros((4 * HALF, 1), jnp.float32)
        out = jnp.zeros((4 * HALF, HEAD_DIM), jnp.float32)
        for i, far_ref in enumerate(far_refs):
            scores = dot(q, far_ref[:, :HEAD_DIM], 1, 1)
            key = jnp.concatenate(
                [within + facts_ref[FAR_PLACE + i * blocks + k] * HALF for k in range(blocks)],
                axis=1,
            )
            seen = key <= position
            scores = jnp.where(seen, scores, MASKED)
            now = jnp.maximum(top, jnp.max(scores, axis=1, keepdims=True))
            weights = jnp.where(seen, jnp.exp(scores - now), 0.0)
            scale = jnp.exp(top - now)
            total = total * scale + jnp.sum(weights, axis=1, keepdims=True)
            out = out * scale + dot(weights.astype(jnp.bfloat16), far_ref[:, HEAD_DIM:])
            top = now
        attn_ref[rows, :] = unstacked(out / total).astype(jnp.bfloat16)
        lse_ref[half] = as_row(top + jnp.log(total))
    attn_ref[pl.ds(2 * HALF, short_ref.shape[0]), :] = short_ref[...]


def long_forward(line, q, far, facts, short, rows):
    return line(
        "long_forward",
        long_forward_kernel,
        (q, *far, facts, short),
        [VMEM] * 5 + [SMEM, VMEM],
        [shaped((rows, 256)), shaped((2, 8, 4 * HALF), jnp.float32)],
        [VMEM] * 2,
    )


def grad_terms(q, grad, k, v, seen, lse, delta):
    weights = jnp.where(seen, jnp.exp(dot(k, q, 1, 1) - lse), 0.0)
    grad_scores = (weights * (dot(v, grad, 1, 1) - delta)).astype(jnp.bfloat16)
    return (
        dot(grad_scores, k, 0, 0),
        dot(grad_scores, q),
        dot(weights.astype(jnp.bfloat16), grad),
    )


def row_product(left, right):
    return as_row(
        jnp.sum(left.astype(jnp.float32) * right.astype(jnp.float32), axis=1, keepdims=True)
    )[:1]


def short_backward_kernel(
    qkv_ref, facts_ref, attn_ref, grad_ref, lse_ref, cos_ref, sin_ref, out_ref, dk_ref, dv_ref
):
    packed = attn_ref.shape[0]
    scale = HEAD_DIM**-0.5
    dk_ref[...] = jnp.zeros_like(dk_ref)
    dv_ref[...] = jnp.zeros_like(dv_ref)
    for i, (at, count) in enumerate(blocks_of(packed)):
        rows = pl.ds(2 * HALF + at, count)
        keys = at + count
        q = stacked(qkv_ref[rows, :256]) * jnp.bfloat16(scale)
        k = qkv_ref[pl.ds(2 * HALF, keys), 256:320]
        v = qkv_ref[pl.ds(2 * HALF, keys), 320:384]
        grad = stacked(grad_ref[rows, :])
        delta = row_product(grad, stacked(attn_ref[pl.ds(at, count), :]))
        wide = count if count == HALF else 4 * count
        key = lax.broadcasted_iota(jnp.int32, (keys, wide), 0)
        query = lax.rem(lax.broadcasted_iota(jnp.int32, (1, wide), 1), count) + at
        seen = (key <= query) & (key >= start_of(query, facts_ref))
        seen = jnp.concatenate([seen] * (4 * count // wide), axis=1)
        dq, dk, dv = grad_terms(
            q,
            grad,
            k,
            v,
            seen,
            lse_ref[i, :1, : 4 * count],
            delta,
        )
        out_ref[pl.ds(at, count), :256] = turned(
            unstacked(dq * scale), cos_ref[rows, :], -sin_ref[rows, :]
        ).astype(jnp.bfloat16)
        dk_ref[pl.ds(0, keys), :] += dk
        dv_ref[pl.ds(0, keys), :] += dv
    rows = pl.ds(2 * HALF, packed)
    out_ref[:, 256:] = turned_key(
        jnp.concatenate([dk_ref[...], dv_ref[...]], axis=1), cos_ref[rows, :], -sin_ref[rows, :]
    ).astype(jnp.bfloat16)


def short_backward(line, qkv, facts, attn, grad, lse, cos_rows, sin_rows):
    rows = attn.shape[0]
    return line(
        "short_backward",
        short_backward_kernel,
        (qkv, facts, attn, grad, lse, cos_rows, sin_rows),
        [VMEM, SMEM] + [VMEM] * 5,
        [shaped((rows, 384))],
        [VMEM],
        [pltpu.VMEM((rows, HEAD_DIM), jnp.float32)] * 2,
    )[0]


def long_backward_kernel(q_ref, *refs):
    far_refs = refs[:4]
    facts_ref, attn_ref, grad_ref, lse_ref, cos_ref, sin_ref = refs[4:10]
    dq_ref, far_grad_ref, acc_ref = refs[10:]
    scale = HEAD_DIM**-0.5
    count = far_refs[0].shape[0]
    blocks = count // HALF
    queries = []
    for half in range(2):
        rows = pl.ds(half * HALF, HALF)
        grad = stacked(grad_ref[rows, :])
        column = lax.broadcasted_iota(jnp.int32, (1, HALF), 1)
        queries.append(
            (
                stacked(q_ref[rows, :256]) * jnp.bfloat16(scale),
                grad,
                lse_ref[half, :1],
                row_product(grad, stacked(attn_ref[rows, :])),
                jnp.concatenate([column + facts_ref[FIRST_PLACE + half] * HALF] * 4, axis=1),
            )
        )
    within = lax.broadcasted_iota(jnp.int32, (HALF, 1), 0)
    for i, far_ref in enumerate(far_refs):
        k, v = far_ref[:, :HEAD_DIM], far_ref[:, HEAD_DIM:]
        key = jnp.concatenate(
            [within + facts_ref[FAR_PLACE + i * blocks + n] * HALF for n in range(blocks)], axis=0
        )
        sums = []
        for half, (q, grad, lse, delta, position) in enumerate(queries):
            dq, dk, dv = grad_terms(q, grad, k, v, key <= position, lse, delta)
            acc_ref[half] = dq if i == 0 else acc_ref[half] + dq
            sums.append((dk, dv))
        total = jnp.concatenate(
            [sums[0][0] + sums[1][0], sums[0][1] + sums[1][1]], axis=1
        ).astype(jnp.bfloat16)
        rows = count // 4
        for n in range(4):
            far_grad_ref[n, pl.ds(i * rows, rows), :] = total[n * rows : (n + 1) * rows]
    for half in range(2):
        rows = pl.ds(half * HALF, HALF)
        dq_ref[rows, :] = turned(
            unstacked(acc_ref[half] * scale), cos_ref[rows, :], -sin_ref[rows, :]
        ).astype(jnp.bfloat16)


def long_backward(line, q, far, facts, attn, grad, lse, cos_rows, sin_rows):
    return line(
        "long_backward",
        long_backward_kernel,
        (q, *far, facts, attn, grad, lse, cos_rows, sin_rows),
        [VMEM] * 5 + [SMEM] + [VMEM] * 5,
        [shaped((2 * HALF, 256)), shaped((4, *far[0].shape))],
        [VMEM] * 2,
        [pltpu.VMEM((2, 4 * HALF, HEAD_DIM), jnp.float32)],
    )


def product_kernel(turned_right, left_ref, right_ref, out_ref):
    out_ref[...] = dot(left_ref[...], right_ref[...], 1, 1 if turned_right else 0).astype(
        out_ref.dtype
    )


def product(line, left, right, turned_right=False):
    rows, depth = left.shape
    width = right.shape[0] if turned_right else right.shape[1]
    block = rows // 2
    return line(
        "product",
        functools.partial(product_kernel, turned_right),
        (left, right),
        [rows_of(block, depth), once(right.shape)],
        [shaped((rows, width))],
        [rows_of(block, width)],
        grid=(2,),
    )[0]


def product_parts_kernel(terms, turned_right, *refs):
    outs = refs[2 * terms + 1 :]
    total = refs[2 * terms][...].astype(jnp.float32)
    for k in range(terms):
        total += dot(refs[2 * k][...], refs[2 * k + 1][...], 1, 1 if turned_right else 0)
    rows = outs[0].shape[0]
    for k, out_ref in enumerate(outs):
        out_ref[...] = total[k * rows : (k + 1) * rows].astype(jnp.bfloat16)


def product_parts(line, pairs, sent, turned_right=False):
    rows, width = sent.shape
    steps = 2 * len(pairs)
    block = width // steps
    specs = []
    for left, right in pairs:
        specs.append(once(left.shape))
        if turned_right:
            specs.append(rows_of(block, right.shape[1]))
        else:
            specs.append(columns_of(right.shape[0], block))
    return line(
        "product_parts",
        functools.partial(product_parts_kernel, len(pairs), turned_right),
        [array for pair in pairs for array in pair] + [sent],
        specs + [columns_of(rows, block)],
        [shaped((rows // 4, width))] * 4,
        [columns_of(rows // 4, block)] * 4,
        grid=(steps,),
    )


def merged(chunks):
    pieces = []
    for k in range(4):
        for (low, high), chunk in zip(CHUNKS, chunks):
            pieces.append(chunk[k * (high - low) : (k + 1) * (high - low)])
    return jnp.concatenate(pieces, axis=0)


def merged_product_kernel(count, with_sent, *refs):
    left = merged([ref[...] for ref in refs[:count]])
    total = dot(left, refs[count][...])
    outs = refs[count + 1 :]
    if with_sent:
        total += outs[0][...].astype(jnp.float32)
        outs = outs[1:]
    rows = outs[0].shape[0]
    for k, out_ref in enumerate(outs):
        out_ref[...] = total[k * rows : (k + 1) * rows].astype(jnp.bfloat16)


def merged_product(line, chunks, right, sent=None):
    rows = sum([chunk.shape[0] for chunk in chunks])
    depth, width = right.shape
    block = width // 2
    count = 1 if sent is None else 4
    extra = () if sent is None else (sent,)
    return line(
        "merged_product",
        functools.partial(merged_product_kernel, len(chunks), sent is not None),
        (*chunks, right, *extra),
        [once(chunk.shape) for chunk in chunks]
        + [columns_of(depth, block)]
        + [columns_of(rows, block)] * len(extra),
        [shaped((rows // count, width))] * count,
        [columns_of(rows // count, block)] * count,
        grid=(2,),
    )


def merged_back_kernel(count, *refs):
    left = merged([ref[...] for ref in refs[:count]])
    refs[-1][...] = dot(left, refs[count][...], 1, 1).astype(jnp.bfloat16)


def merged_back(line, chunks, right):
    rows = sum([chunk.shape[0] for chunk in chunks])
    return line(
        "merged_back",
        functools.partial(merged_back_kernel, len(chunks)),
        (*chunks, right),
        [VMEM] * (len(chunks) + 1),
        [shaped((rows, right.shape[0]))],
        [VMEM],
    )[0]


def arrange_kernel(facts_ref, rows_ref, *out_refs):
    del facts_ref
    for (low, high), out_ref in zip(CHUNKS, out_refs):
        out_ref[0] = rows_ref[0, low:high, :]


def arrange(line, rows, facts):
    _, count, d = rows.shape
    after = line.last

    def kernel(facts_ref, rows_ref, *refs):
        arrange_kernel(facts_ref, rows_ref, *refs[len(after) :])

    def source(i, facts_ref):
        core = jnp.where(i < 4, facts_ref[CORE_AT], 1 - facts_ref[CORE_AT])
        return core * 4 + (facts_ref[X_AT] + i) % 4, 0, 0

    results = pl.pallas_call(
        kernel,
        grid_spec=pltpu.PrefetchScalarGridSpec(
            num_scalar_prefetch=1,
            grid=(8,),
            in_specs=[pl.BlockSpec((1, count, d), source)] + [ANY] * len(after),
            out_specs=tuple(
                pl.BlockSpec((1, high - low, d), lambda i, facts_ref: (i, 0, 0))
                for low, high in CHUNKS
            ),
        ),
        out_shape=tuple(shaped((8, high - low, d)) for low, high in CHUNKS),
        compiler_params=PARAMS,
        cost_estimate=cost("arrange"),
        name="arrange",
    )(facts, rows, *after)
    return [array.reshape(-1, d) for array in results]


def weight_grad_kernel(count, beside, facts, *refs):
    facts_ref, *refs = refs if facts else (None, *refs)
    out_ref, width = refs[-1], refs[count].shape[1]
    total = dot(refs[0][...], refs[count][...], 0, 0)
    for k in range(1, count):
        total += dot(refs[k][...], refs[count + k][...], 0, 0)
    total = total.astype(jnp.bfloat16)
    if facts:
        rows = total.shape[0] // 2
        own_first = jnp.concatenate([total[rows:], total[:rows]])
        total = jnp.where(facts_ref[CORE_AT] == 0, total, own_first)
    out_ref[:, :width] = total
    if beside:
        out_ref[:, width:] = refs[2 * count][...]


def weight_grad(line, left, right, beside=(), facts=None):
    left = [piece if isinstance(piece, tuple) else (piece, 0) for piece in left]
    columns, width = left[0][0].shape[1], right[0].shape[1]
    whole = width + sum([array.shape[1] for array in beside])
    block = columns // 8

    def place(i, *facts_ref):
        if facts_ref:
            z = (i - facts_ref[0][Z_AT]) % 4
            yh = (i // 4 + facts_ref[0][YH_AT]) % 2
            return z * 2 + yh, 0
        return i % 4 * 2 + i // 4, 0

    def whole_block(i, *facts_ref):
        return 0, 0

    operands = (*[array for array, _ in left], *right, *beside)
    in_specs = (
        [
            pl.BlockSpec((part.shape[0], block), lambda i, *_, at=at: (at, i))
            for (_, at), part in zip(left, right)
        ]
        + [pl.BlockSpec(part.shape, whole_block, pipeline_mode=pl.Buffered(1)) for part in right]
        + [pl.BlockSpec((block, array.shape[1]), place) for array in beside]
    )
    out_spec = pl.BlockSpec((block, whole), place)
    kernel = functools.partial(weight_grad_kernel, len(left), len(beside), facts is not None)
    if facts is None:
        return line(
            "weight_grad",
            kernel,
            operands,
            in_specs,
            [shaped((columns, whole))],
            [out_spec],
            grid=(8,),
        )[0]
    after, count = line.last, len(operands) + 1

    def ordered(*refs):
        kernel(*refs[:count], *refs[count + len(after) :])

    result = pl.pallas_call(
        ordered,
        grid_spec=pltpu.PrefetchScalarGridSpec(
            num_scalar_prefetch=1,
            grid=(8,),
            in_specs=in_specs + [ANY] * len(after),
            out_specs=out_spec,
        ),
        out_shape=shaped((columns, whole)),
        compiler_params=PARAMS,
        cost_estimate=cost("weight_grad"),
        name="weight_grad",
    )(facts, *operands, *after)
    line.last = (result,)
    return result


def mix_kernel(low, high, tokens_ref, gain_ref, *refs):
    parts, (mixed_ref, hidden_ref) = refs[:4], refs[4:]
    mixed = tokens_ref[low:high, :].astype(jnp.float32) + total_of([ref[...] for ref in parts])
    inv = lax.rsqrt(jnp.mean(mixed * mixed, axis=-1, keepdims=True) + EPS)
    mixed_ref[...] = mixed
    hidden_ref[...] = (mixed * inv * gain_ref[...]).astype(jnp.bfloat16)


def mix(line, chunk, tokens, gain, parts):
    low, high = chunk
    d = tokens.shape[1]
    return line(
        "mix",
        functools.partial(mix_kernel, low, high),
        (tokens, gain, *parts),
        [VMEM] * 6,
        [shaped((high - low, d), jnp.float32), shaped((high - low, d))],
        [VMEM] * 2,
    )


def norm_back(grad_in, values, gain):
    inv = lax.rsqrt(jnp.mean(values * values, axis=-1, keepdims=True) + EPS)
    unit = values * inv
    scaled = grad_in * gain
    return inv * (scaled - unit * jnp.mean(scaled * unit, axis=-1, keepdims=True)), unit


def mix_back_kernel(low, high, grad_ref, mixed_ref, gain_ref, *refs):
    parts, (total_ref, low_ref, part_ref) = refs[:4], refs[4:]
    grad_in = total_of([ref[...] for ref in parts])
    back, unit = norm_back(grad_in, mixed_ref[...], gain_ref[...])
    total = grad_ref[low:high, :].astype(jnp.float32) + back
    total_ref[...] = total
    low_ref[...] = total.astype(jnp.bfloat16)
    part_ref[...] = jnp.sum(grad_in * unit, axis=0, keepdims=True)


def mix_back(line, chunk, grad, mixed, gain, parts):
    low, high = chunk
    rows, d = mixed.shape
    return line(
        "mix_back",
        functools.partial(mix_back_kernel, low, high),
        (grad, mixed, gain, *parts),
        [VMEM] * 7,
        [shaped((rows, d), jnp.float32), shaped((rows, d)), shaped((1, d), jnp.float32)],
        [VMEM] * 3,
    )


def mlp_kernel(hidden_ref, grad_act_ref, gate_ref, up_ref, act_ref, gate_out_ref, up_out_ref, *refs):
    hidden = hidden_ref[...]
    gate = dot(hidden, gate_ref[...])
    up = dot(hidden, up_ref[...])
    grad_act = grad_act_ref[...].astype(jnp.float32)
    sig = jax.nn.sigmoid(gate)
    silu = gate * sig
    act_ref[...] = (silu * up).astype(jnp.bfloat16)
    grad_gate = (grad_act * up * sig * (1.0 + gate * (1.0 - sig))).astype(jnp.bfloat16)
    grad_up = (grad_act * silu).astype(jnp.bfloat16)
    gate_out_ref[...] = grad_gate
    up_out_ref[...] = grad_up
    if refs:
        refs[0][...] = (
            dot(grad_gate, gate_ref[...], 1, 1) + dot(grad_up, up_ref[...], 1, 1)
        ).astype(jnp.bfloat16)


def mlp(line, hidden, grad_act, at, w_gate, w_up, with_back):
    rows, d = hidden.shape
    width = w_gate.shape[1]
    if with_back:
        block = rows // 2
        specs = [
            rows_of(block, d),
            pl.BlockSpec((block, width), lambda i: (2 * at + i, 0)),
            once((d, width)),
            once((d, width)),
        ]
        out_specs = [rows_of(block, width)] * 3 + [rows_of(block, d)]
    else:
        block = width // 4
        specs = [
            once((rows, d)),
            pl.BlockSpec((rows, block), lambda i: (at, i)),
            columns_of(d, block),
            columns_of(d, block),
        ]
        out_specs = [columns_of(rows, block)] * 3
    return line(
        "mlp",
        mlp_kernel,
        (hidden, grad_act, w_gate, w_up),
        specs,
        [shaped((rows, width))] * 3 + [shaped((rows, d))] * with_back,
        out_specs,
        grid=(2 if with_back else 4,),
    )


def hidden_grad_kernel(with_sent, low_ref, query_ref, kv_ref, hidden_ref, *refs):
    low = low_ref[...]
    grad = dot(low[:, :256], query_ref[...], 1, 1) + dot(low[:, 256:], kv_ref[...], 1, 1)
    gain = jnp.sum(grad * hidden_ref[...].astype(jnp.float32), axis=0, keepdims=True)
    if not with_sent:
        refs[0][...] = grad.astype(jnp.bfloat16)
        refs[1][...] = gain
        return
    sent_ref, gain_ref, mlp_gain_ref, *outs = refs
    grad += sent_ref[...].astype(jnp.float32)
    rows = outs[0].shape[0] - 8
    tail = []
    for values in (gain + gain_ref[...], mlp_gain_ref[...]):
        high = values.astype(jnp.bfloat16)
        tail += [high, (values - high.astype(jnp.float32)).astype(jnp.bfloat16)]
    tail = jnp.concatenate(tail + [jnp.zeros_like(tail[0])] * 4, axis=0)
    for k, out_ref in enumerate(outs):
        part = grad[k * rows : (k + 1) * rows].astype(jnp.bfloat16)
        out_ref[...] = jnp.concatenate([part, tail], axis=0)


def hidden_grad(line, low, w_query, w_key_value, hidden, sent=()):
    rows, d = hidden.shape
    block = d // 2
    if sent:
        outs = [shaped((rows // 4 + 8, d))] * 4
        out_specs = [columns_of(rows // 4 + 8, block)] * 4
    else:
        outs = [shaped((rows, d)), shaped((1, d), jnp.float32)]
        out_specs = [columns_of(rows, block), columns_of(1, block)]
    return line(
        "hidden_grad",
        functools.partial(hidden_grad_kernel, bool(sent)),
        (low, w_query, w_key_value, hidden, *sent),
        [once((rows, 384)), rows_of(block, 256), rows_of(block, 128), columns_of(rows, block)]
        + [columns_of(array.shape[0], block) for array in sent],
        outs,
        out_specs,
        grid=(2,),
    )


def gate_kernel(*refs):
    del refs


def gated(line, arrays):
    line.last = tuple([array for array in line.last if all([array is not one for one in arrays])])
    return line(
        "gated",
        gate_kernel,
        arrays,
        [ANY] * len(arrays),
        [shaped(array.shape, array.dtype) for array in arrays],
        [ANY] * len(arrays),
        input_output_aliases={k: k for k in range(len(arrays))},
    )


def out_mix_kernel(*refs):
    mixed = jnp.concatenate([ref[...] for ref in refs[:-5]], axis=0)
    refs[-1][...] = (mixed + total_of([ref[...] for ref in refs[-5:-1]])).astype(jnp.bfloat16)


def final_kernel(tokens_ref, gain_ref, *refs):
    out_ref, gains_ref = refs[-2:]
    total = total_of([ref[...] for ref in refs[-6:-2]])
    rows = out_ref.shape[0]
    back, _ = norm_back(total[:rows], tokens_ref[...].astype(jnp.float32), gain_ref[...])
    mixed = jnp.concatenate([ref[...] for ref in refs[:-6]], axis=0)
    out_ref[...] = (mixed + back).astype(jnp.bfloat16)
    sums = total[rows : rows + 8]
    gains_ref[...] = jnp.concatenate([sums[:1] + sums[1:2], sums[2:3] + sums[3:4]], axis=0)


def turn_far_kernel(grad_ref, cos_ref, sin_ref, long_ref, short_ref, out_ref):
    rows = pl.ds(0, 2 * HALF)
    out_ref[rows, :256] = long_ref[...]
    out_ref[rows, 256:] = turned_key(grad_ref[...], cos_ref[rows, :], -sin_ref[rows, :]).astype(
        jnp.bfloat16
    )
    out_ref[pl.ds(2 * HALF, short_ref.shape[0]), :] = short_ref[...]


def local(
    tokens,
    lengths,
    place,
    attn_gain,
    w_query,
    w_key,
    w_value,
    w_out,
    mlp_gain,
    w_gate,
    w_up,
    w_down,
    out_grad,
):
    rows, d = tokens.shape
    group_rows = rows * 8
    half_rows = rows * 4
    long_rows = 2 * HALF
    dp_index, mp_index = lax.axis_index("dp"), lax.axis_index("mp")
    yh, z, core = dp_index // 8, dp_index // 2 % 4, dp_index % 2
    yl, x = mp_index // 4, mp_index % 4
    native = core == yl
    line = Line()
    mlp_gain_row = mlp_gain.reshape(1, d)

    tokens = send(tokens, TURN)
    lengths = send(lengths, TURN)[0]
    w_key_value = send(jnp.concatenate([w_key, w_value], axis=1), WEIGHT_LOW)
    w_query = send(w_query, WEIGHT_LOW)
    w_out = send(w_out, WEIGHT_LOW)
    w_down = send(w_down, WEIGHT_HIGH)
    w_gate = send(w_gate, WEIGHT_LOW)
    w_up = send(w_up, WEIGHT_HIGH)
    out_grad = turn(out_grad, native)

    step = jnp.arange(16, dtype=jnp.int32)
    far_yh = jnp.where(step % 4 >= 2, 1 - yh, yh)
    far_yl = jnp.where((step % 4 == 1) | (step % 4 == 2), 1 - yl, yl)
    far_group = (far_yh * 4 + (z + step // 4) % 4) * 2 + far_yl
    far_index = (2 * far_group[:, None] + jnp.arange(2, dtype=jnp.int32)[None, :]).reshape(-1)
    half_ids = jnp.arange(place.shape[0], dtype=jnp.int32)
    far_place = jnp.sum(jnp.where(far_index[:, None] == half_ids[None, :], place, 0), axis=1)
    facts = jnp.concatenate(
        [
            far_place[:2],
            jnp.stack([lengths[0], lengths[0] + lengths[1], core, x, z, yh]),
            far_place,
        ]
    ).astype(jnp.int32)

    residual = tokens.astype(jnp.float32)
    inv_one = lax.rsqrt(jnp.mean(residual * residual, axis=-1, keepdims=True) + EPS)
    hidden_one = collect((residual * inv_one * attn_gain).astype(jnp.bfloat16))
    freq = jnp.tile(inverse_freq(HEAD_DIM), 4).reshape(1, 128)
    line.last += (w_query, w_key_value)
    cos_gathered, sin_gathered, cos_ordered, sin_ordered = line(
        "tables",
        functools.partial(tables_kernel, rows),
        (facts, freq),
        [SMEM, VMEM],
        [shaped((n, 128), jnp.float32) for n in (group_rows,) * 4],
        [VMEM] * 4,
    )
    hidden_own = join(line, hidden_one)
    hidden_one = (hidden_own, send(hidden_own, CORE))
    qkv = []
    for at, half in enumerate(hidden_one):
        line.last += (w_down,) * at
        qkv.append(
            project_qkv(line, half, w_query, w_key_value, cos_gathered, sin_gathered, at)
        )
    (out_grad,) = gated(line, (out_grad,))
    grad_rows = lax.all_gather(out_grad, BOTH, axis=0, axis_index_groups=CHIP_GROUPS)
    qkv = in_order(jnp.stack(qkv), core, x)
    near_rows = qkv[:long_rows, 256:]
    ring_rows = jnp.concatenate(
        [near_rows, send(near_rows, Y_LOW), send(near_rows, Y_HIGH), send(near_rows, Y_FAR)]
    )
    far_rows = (
        ring_rows, send(ring_rows, Z_DOWN), send(ring_rows, Z_FAR), send(ring_rows, Z_UP)
    )
    line.last += (ring_rows,)
    short_attn, short_lse = short_forward(line, qkv, facts)
    attn_ordered, long_lse = long_forward(line, qkv, far_rows, facts, short_attn, group_rows)
    attn_rows = from_order(attn_ordered, core, x)
    attn_rows = [chunks_of(attn_rows[half]) for half in range(2)]

    sent = [send(product(line, part, w_out), CORE) for part in attn_rows[1]]
    mixed_parts = [
        scatter(product_parts(line, [(part, w_out)], other))
        for part, other in zip(attn_rows[0], sent)
    ]
    grad_rows = arrange(line, grad_rows, facts)
    grad_act = [product(line, part, w_down, True) for part in grad_rows]
    mixed, hidden_two = [], []
    for chunk, parts in zip(CHUNKS, mixed_parts):
        mixed_rows, hidden_rows = mix(line, chunk, tokens, mlp_gain_row, parts)
        mixed.append(mixed_rows)
        hidden_two.append(collect(hidden_rows))

    count = len(CHUNKS)
    own, other, act, gate, up, back = ([None] * count for _ in range(6))

    def first_half(n):
        own[n] = join(line, hidden_two[n])
        other[n] = send(own[n], CORE)
        act[n], gate[n], up[n] = mlp(line, own[n], grad_act[n], 0, w_gate, w_up, False)

    def second_half(n):
        *terms, sum_back = mlp(line, other[n], grad_act[n], 1, w_gate, w_up, True)
        act[n], gate[n], up[n] = zip((act[n], gate[n], up[n]), terms)
        back[n] = send(sum_back, CORE)

    hidden_parts = []
    first_half(0)
    second_half(0)
    for n in range(count):
        if n + 1 < count:
            first_half(n + 1)
        if n + 1 == count:
            (down_rows,) = merged_product(line, [part[1] for part in act], w_down)
            down_rows = send(down_rows, CORE)
        terms = [(gate[n][0], w_gate), (up[n][0], w_up)]
        hidden_parts.append(scatter(product_parts(line, terms, back[n], True)))
        if n + 1 < count:
            second_half(n + 1)
    act, gate, up = [[pair[k] for pair in part for k in range(2)] for part in (act, gate, up)]
    hidden_two = [piece for pair in zip(own, other) for piece in pair]

    pieces = [(part, at) for part in grad_rows for at in range(2)]
    both_part = weight_grad(line, hidden_two, up, (weight_grad(line, hidden_two, gate),))
    grad_mixed, mixed_grad, gain_parts = [], [], []
    for n, (chunk, parts) in enumerate(zip(CHUNKS, hidden_parts)):
        total, low, gain_part = mix_back(line, chunk, out_grad, mixed[n], mlp_gain_row, parts)
        grad_mixed.append(total)
        mixed_grad.append(collect(low))
        gain_parts.append(gain_part)
    both_kept = reduce_near(gated(line, (both_part,))[0])
    down_part = weight_grad(line, pieces, act)
    out_parts = scatter(merged_product(line, act[0::2], w_down, down_rows))

    grad_own = [join(line, parts) for parts in mixed_grad]
    grad_other = [send(part, CORE) for part in grad_own]
    grad_attn = jnp.stack([merged_back(line, part, w_out) for part in (grad_own, grad_other)])
    grad_attn = in_order(grad_attn, core, x)
    long_dq, far_terms = long_backward(
        line,
        qkv,
        far_rows,
        facts,
        attn_ordered,
        grad_attn,
        long_lse,
        cos_ordered,
        sin_ordered,
    )
    ring_terms = total_of(
        (
            far_terms[0],
            send(far_terms[1], Y_LOW),
            send(far_terms[2], Y_HIGH),
            send(far_terms[3], Y_FAR),
        )
    ).astype(jnp.bfloat16)
    near = ring_terms.reshape(4, long_rows, -1)
    far_grads = total_of(
        (near[0], send(near[1], Z_UP), send(near[2], Z_FAR), send(near[3], Z_DOWN))
    )
    line.last += out_parts[1:]
    short_low = short_backward(
        line, qkv, facts, short_attn, grad_attn, short_lse, cos_ordered, sin_ordered
    )
    out_part = weight_grad(
        line,
        [piece for pair in zip(grad_own, grad_other) for piece in pair],
        [piece for pair in zip(*attn_rows) for piece in pair],
        (),
        facts,
    )
    (low_ordered,) = line(
        "turn_far",
        turn_far_kernel,
        (far_grads, cos_ordered, sin_ordered, long_dq, short_low),
        [VMEM] * 5,
        [shaped((group_rows, 384))],
        [VMEM],
    )
    low_rows = from_order(low_ordered, core, x)
    line.last += (both_kept,)
    down_kept = reduce_near(gated(line, (down_part,))[0])
    back, gain_other = hidden_grad(line, low_rows[1], w_query, w_key_value, hidden_one[1])
    back = send(back, CORE)
    last_part = weight_grad(line, hidden_one, (low_rows[0], low_rows[1]), (out_part,), facts)
    grad_parts = scatter(
        hidden_grad(
            line,
            low_rows[0],
            w_query,
            w_key_value,
            hidden_one[0],
            (back, gain_other, sum(gain_parts[1:], gain_parts[0])),
        )[:4]
    )
    last_kept, first_hop = reduce_ring(gated(line, (last_part,))[0])
    (output,) = line(
        "out_mix",
        out_mix_kernel,
        (*mixed, *out_parts),
        [VMEM] * (len(mixed) + 4),
        [shaped((rows, d))],
        [VMEM],
    )
    output = turn(output, native)
    line.last += first_hop
    grad_tokens, gains = line(
        "final",
        final_kernel,
        (tokens, attn_gain.reshape(1, d), *grad_mixed, *grad_parts),
        [VMEM] * (2 + len(grad_mixed) + 4),
        [shaped((rows, d)), shaped((2, d), jnp.float32)],
        [VMEM] * 2,
    )
    both_kept, down_kept = gated(line, (both_kept, down_kept))
    ff_sum = reduce_y(jnp.concatenate([both_kept, down_kept], axis=1))
    grad_tokens = turn(grad_tokens, native)
    gains = all_sum(gains)
    last_sum = sum_groups(last_kept, native)
    ff = w_gate.shape[1]
    return (
        output,
        grad_tokens,
        gains[0] / attn_gain,
        last_sum[:, :256],
        last_sum[:, 256:320],
        last_sum[:, 320:384],
        last_sum[:, 384:].T,
        gains[1],
        ff_sum[:, ff : 2 * ff],
        ff_sum[:, :ff],
        ff_sum[:, 2 * ff :].T,
    )


def solution(mesh):
    placed = (
        P(("dp", "mp"), None),
        P("dp", None),
        P(),
        P(),
        P(None, "mp"),
        P(None, "mp"),
        P(None, "mp"),
        P("mp", None),
        P(),
        P(None, "mp"),
        P(None, "mp"),
        P("mp", None),
        P(("dp", "mp"), None),
    )
    return jax.shard_map(
        local,
        mesh=mesh,
        in_specs=placed,
        out_specs=(
            P(("dp", "mp"), None),
            P(("dp", "mp"), None),
            P(),
            P("dp", "mp"),
            P("dp", "mp"),
            P("dp", "mp"),
            P("mp", "dp"),
            P(),
            P("dp", "mp"),
            P("dp", "mp"),
            P("mp", "dp"),
        ),
        check_vma=False,
    )
```

```python
import functools

import jax
import jax.numpy as jnp
from jax import lax
from jax.experimental import pallas as pl
from jax.experimental.pallas import tpu as pltpu
from jax.sharding import PartitionSpec as P

HEAD_DIM = 64
HALF = 128
MASKED = -1e30


EPS = 1e-05
THETA = 500000.0

BOTH = ("dp", "mp")


def place_of(yh, z, c, yl, x):
    return ((yh * 4 + z) * 2 + c) * 8 + yl * 4 + x


def pairs_of(target, sender=lambda yh, z, c, yl, x: True):
    return [
        (place_of(yh, z, c, yl, x), place_of(*target(yh, z, c, yl, x)))
        for yh in range(2)
        for z in range(4)
        for c in range(2)
        for yl in range(2)
        for x in range(4)
        if sender(yh, z, c, yl, x)
    ]


X_UP = pairs_of(lambda yh, z, c, yl, x: (yh, z, c, yl, (x + 1) % 4))
X_DOWN = pairs_of(lambda yh, z, c, yl, x: (yh, z, c, yl, (x + 3) % 4))
X_FAR = pairs_of(lambda yh, z, c, yl, x: (yh, z, c, yl, (x + 2) % 4))
Z_UP = pairs_of(lambda yh, z, c, yl, x: (yh, (z + 1) % 4, c, yl, x))
Z_DOWN = pairs_of(lambda yh, z, c, yl, x: (yh, (z + 3) % 4, c, yl, x))
Z_NEXT = pairs_of(lambda yh, z, c, yl, x: (yh, z ^ 1, c, yl, x))
Z_FAR = pairs_of(lambda yh, z, c, yl, x: (yh, (z + 2) % 4, c, yl, x))
CORE = pairs_of(lambda yh, z, c, yl, x: (yh, z, 1 - c, yl, x))
Y_LOW = pairs_of(lambda yh, z, c, yl, x: (yh, z, c, 1 - yl, x))
Y_HIGH = pairs_of(lambda yh, z, c, yl, x: (1 - yh, z, c, 1 - yl, x))
Y_FAR = pairs_of(lambda yh, z, c, yl, x: (1 - yh, z, c, yl, x))
TURN = pairs_of(lambda yh, z, c, yl, x: (yh, z, yl, c, x))
NATIVE = lambda yh, z, c, yl, x: c == yl
FOREIGN = lambda yh, z, c, yl, x: c != yl
FOREIGN_TURN = pairs_of(lambda yh, z, c, yl, x: (yh, z, yl, c, x), FOREIGN)
FOREIGN_LOW = pairs_of(lambda yh, z, c, yl, x: (yh, z, c, 1 - yl, x), FOREIGN)
FOREIGN_HIGH = pairs_of(lambda yh, z, c, yl, x: (1 - yh, z, c, 1 - yl, x), FOREIGN)
NATIVE_FAR = pairs_of(lambda yh, z, c, yl, x: (1 - yh, z, c, yl, x), NATIVE)
NATIVE_CORE = pairs_of(lambda yh, z, c, yl, x: (yh, z, 1 - c, yl, x), NATIVE)
WEIGHT_LOW = pairs_of(
    lambda yh, z, c, yl, x: (yh, z, c, 1 - yl, x) if c == yl else (yh, z, 1 - c, yl, x)
)
WEIGHT_HIGH = pairs_of(
    lambda yh, z, c, yl, x: (1 - yh, z, c, 1 - yl, x) if c == yl else (yh, z, 1 - c, yl, x)
)
Z_GROUPS = [
    [place_of(yh, z, c, yl, x) for z in range(4)]
    for yh in range(2)
    for c in range(2)
    for yl in range(2)
    for x in range(4)
]


Y_GROUPS = [
    [place_of(yh, z, c, yl, x) for yh in range(2) for yl in range(2)]
    for z in range(4)
    for c in range(2)
    for x in range(4)
]
CHIP_GROUPS = [
    [place_of(yh, z, c, yl, x) for c in range(2) for x in range(4)]
    for yh in range(2)
    for z in range(4)
    for yl in range(2)
]


def send(values, pairs):
    return lax.ppermute(values, BOTH, pairs)


CHUNKS = ((0, 136),)

VMEM = pl.BlockSpec(memory_space=pltpu.VMEM)
SMEM = pl.BlockSpec(memory_space=pltpu.SMEM)
ANY = pl.BlockSpec(memory_space=pl.ANY)
PARAMS = pltpu.CompilerParams(vmem_limit_bytes=64 * 1024 * 1024)
LASTS = {
    "tables": 1,
    "join": 1,
    "project_qkv": 1,
    "short_forward": 6,
    "long_forward": 13,
    "product": 3,
    "product_parts": 5,
    "arrange": 5,
    "mix": 3,
    "mlp": 10,
    "weight_grad": 2,
    "mix_back": 4,
    "merged_product": 2,
    "merged_back": 3,
    "long_backward": 16,
    "short_backward": 10,
    "turn_far": 2,
    "hidden_grad": 5,
    "out_mix": 4,
    "final": 4,
    "gated": 1,
}


def cost(name):
    return pl.CostEstimate(
        flops=int(1.15e9 * LASTS[name]), bytes_accessed=1000, transcendentals=0
    )


def shaped(shape, dtype=jnp.bfloat16):
    return pltpu.HBM(tuple(shape), dtype)


def rows_of(block, width):
    return pl.BlockSpec((block, width), lambda i: (i, 0))


def columns_of(rows, block):
    return pl.BlockSpec((rows, block), lambda i: (0, i))


def once(shape):
    return pl.BlockSpec(tuple(shape), lambda i: (0,) * len(shape), pipeline_mode=pl.Buffered(1))


class Line:
    def __init__(self):
        self.last = ()

    def __call__(self, name, kernel, operands, in_specs, outs, out_specs, scratch=(), **grid):
        after = self.last
        count = len(operands)

        def ordered(*refs):
            kernel(*refs[:count], *refs[count + len(after) :])

        results = pl.pallas_call(
            ordered,
            out_shape=tuple(outs),
            in_specs=list(in_specs) + [ANY] * len(after),
            out_specs=tuple(out_specs),
            scratch_shapes=list(scratch),
            compiler_params=PARAMS,
            cost_estimate=cost(name),
            name=name,
            **grid,
        )(*operands, *after)
        self.last = (min(results, key=lambda array: array.size),)
        return results


def turn(values, native):
    return jnp.where(native, values, send(values, FOREIGN_TURN))


def dot(left, right, left_dim=1, right_dim=0):
    return lax.dot_general(
        left, right, (((left_dim,), (right_dim,)), ((), ())), preferred_element_type=jnp.float32
    )


def total_of(parts):
    one, two, three, four = [part.astype(jnp.float32) for part in parts]
    return (one + two) + (three + four)


def scatter(parts):
    return (
        parts[0],
        send(parts[1], X_UP),
        send(parts[2], X_FAR),
        send(parts[3], X_DOWN),
    )


def collect(rows):
    return (rows, send(rows, X_DOWN), send(rows, X_FAR), send(rows, X_UP))


def in_order(pair, core, x):
    half = pair.shape[1]
    start = (4 - x) % 4 * (half // 4)
    pair = lax.dynamic_slice_in_dim(jnp.concatenate([pair, pair], axis=1), start, half, axis=1)
    return jnp.where(core == 0, pair, pair[::-1]).reshape(2 * half, -1)


def from_order(values, core, x):
    half = values.shape[0] // 2
    pair = values.reshape(2, half, -1)
    pair = jnp.where(core == 0, pair, pair[::-1])
    return lax.dynamic_slice_in_dim(
        jnp.concatenate([pair, pair], axis=1), x * (half // 4), half, axis=1
    )


def chunks_of(half):
    cut = half.reshape(4, half.shape[0] // 4, -1)
    return [cut[:, low:high].reshape(4 * (high - low), -1) for low, high in CHUNKS]


def plus(left, right):
    return (left.astype(jnp.float32) + right.astype(jnp.float32)).astype(jnp.bfloat16)


def reduce_near(grad):
    return lax.psum_scatter(
        grad, BOTH, scatter_dimension=0, tiled=True, axis_index_groups=Z_GROUPS
    )


def reduce_y(kept):
    kept = lax.psum_scatter(
        kept, BOTH, scatter_dimension=0, tiled=True, axis_index_groups=Y_GROUPS
    )
    return send(kept, TURN).astype(jnp.float32)


def reduce_ring(grad):
    here, above, far, below = jnp.split(grad, 4)
    rows = far.shape[0] // 2
    from_below, from_above = send(far[:rows], Z_UP), send(far[rows:], Z_DOWN)
    above = send(jnp.concatenate([plus(above[:rows], from_below), above[rows:]]), Z_UP)
    below = send(jnp.concatenate([below[:rows], plus(below[rows:], from_above)]), Z_DOWN)
    total = here.astype(jnp.float32) + above.astype(jnp.float32) + below.astype(jnp.float32)
    return total.astype(jnp.bfloat16), (from_below, from_above)


def sum_groups(kept, native):
    near, far = jnp.split(kept, 2)
    across, low, high = send(far, NATIVE_FAR), send(near, FOREIGN_LOW), send(far, FOREIGN_HIGH)
    total = total_of((near, low, high, across))
    rows = total.shape[0] // 2
    passed = send(total[rows:].astype(jnp.bfloat16), NATIVE_CORE).astype(jnp.float32)
    return jnp.where(native, total[:rows], passed)


def all_sum(values):
    for pairs in (CORE, Y_LOW, Y_FAR, Z_NEXT, Z_FAR):
        values += send(values, pairs)
    return values


def inverse_freq(head_width):
    indices = jnp.arange(head_width // 2, dtype=jnp.float32)
    base_freq = jnp.exp(-jnp.log(THETA) * 2.0 * indices / head_width)
    wavelength = 2.0 * jnp.pi / base_freq
    smooth = (8192.0 / wavelength - 1.0) / 3.0
    blended = (1.0 - smooth) * base_freq / 32.0 + smooth * base_freq
    return jnp.where(
        wavelength < 2048.0, base_freq, jnp.where(wavelength > 8192.0, base_freq / 32.0, blended)
    )


FIRST_PLACE, SECOND_START, THIRD_START, CORE_AT, X_AT, Z_AT, YH_AT, FAR_PLACE = 0, 2, 3, 4, 5, 6, 7, 8


def tables_kernel(rows, facts_ref, freq_ref, *out_refs):
    sign = jnp.where(lax.broadcasted_iota(jnp.int32, (1, 128), 1) % 64 < 32, -1.0, 1.0)
    group_rows, half_rows = rows * 8, rows * 4
    for gathered, (cos_ref, sin_ref) in enumerate((out_refs[:2], out_refs[2:])):
        row = lax.broadcasted_iota(jnp.int32, cos_ref.shape, 0)
        if gathered == 0:
            other = (row >= half_rows).astype(jnp.int32)
            rest = row - other * half_rows
            step = sum([(rest >= k * rows).astype(jnp.int32) for k in (1, 2, 3)])
            core = jnp.where(other == 0, facts_ref[CORE_AT], 1 - facts_ref[CORE_AT])
            row = core * half_rows + ((facts_ref[X_AT] + step) & 3) * rows + rest - step * rows
        packed = row - 2 * HALF
        second, third = facts_ref[SECOND_START], facts_ref[THIRD_START]
        start = jnp.where(packed >= third, third, jnp.where(packed >= second, second, 0))
        own = jnp.where(row < HALF, facts_ref[FIRST_PLACE], facts_ref[FIRST_PLACE + 1])
        position = jnp.where(row < 2 * HALF, own * HALF + (row & (HALF - 1)), packed - start)
        angles = position.astype(jnp.float32) * freq_ref[...]
        cos_ref[...] = jnp.cos(angles)
        sin_ref[...] = jnp.sin(angles) * sign


def turned(values, cos_rows, sin_rows):
    first = lax.broadcasted_iota(jnp.int32, (1, 128), 1) % 64 < 32
    tiles = []
    for at in range(0, values.shape[1], 128):
        tile = values[:, at : at + 128]
        swapped = jnp.where(first, pltpu.roll(tile, 96, 1), pltpu.roll(tile, 32, 1))
        tiles.append(tile * cos_rows + swapped * sin_rows)
    return tiles[0] if len(tiles) == 1 else jnp.concatenate(tiles, axis=1)


def turned_key(values, cos_rows, sin_rows):
    key = lax.broadcasted_iota(jnp.int32, (1, 128), 1) < HEAD_DIM
    return jnp.where(key, turned(values, cos_rows, sin_rows), values)


def join_kernel(count, *refs):
    for k in range(count):
        refs[-1][k] = refs[k][...]


def join(line, pieces):
    count = len(pieces)
    rows, width = pieces[0].shape
    block = width // 2
    (joined,) = line(
        "join",
        functools.partial(join_kernel, count),
        pieces,
        [columns_of(rows, block)] * count,
        [shaped((count, rows, width))],
        [pl.BlockSpec((count, rows, block), lambda i: (0, 0, i))],
        grid=(2,),
    )
    return joined.reshape(count * rows, width)


def qkv_kernel(hidden_ref, query_ref, kv_ref, cos_ref, sin_ref, out_ref):
    hidden = hidden_ref[...]
    cos_rows, sin_rows = cos_ref[...], sin_ref[...]
    out_ref[:, :256] = turned(dot(hidden, query_ref[...]), cos_rows, sin_rows).astype(jnp.bfloat16)
    out_ref[:, 256:] = turned_key(dot(hidden, kv_ref[...]), cos_rows, sin_rows).astype(
        jnp.bfloat16
    )


def project_qkv(line, hidden, w_query, w_key_value, cos_rows, sin_rows, at):
    rows, d = hidden.shape
    block = rows // 2
    table = pl.BlockSpec((block, 128), lambda i: (i + 2 * at, 0))
    return line(
        "project_qkv",
        qkv_kernel,
        (hidden, w_query, w_key_value, cos_rows, sin_rows),
        [rows_of(block, d), once((d, 256)), once((d, 128)), table, table],
        [shaped((rows, 384))],
        [rows_of(block, 384)],
        grid=(2,),
    )[0]


def stacked(block):
    return jnp.concatenate(
        [block[:, h * HEAD_DIM : (h + 1) * HEAD_DIM] for h in range(4)], axis=0
    )


def unstacked(block):
    rows = block.shape[0] // 4
    return jnp.concatenate([block[h * rows : (h + 1) * rows] for h in range(4)], axis=1)


def as_row(column):
    return jnp.transpose(jnp.broadcast_to(column, (column.shape[0], 128)))[:8]


def start_of(row, facts_ref):
    second, third = facts_ref[SECOND_START], facts_ref[THIRD_START]
    return jnp.where(row >= third, third, jnp.where(row >= second, second, 0))


def blocks_of(rows):
    return [(at, min(HALF, rows - at)) for at in range(0, rows, HALF)]


def short_forward_kernel(qkv_ref, facts_ref, attn_ref, lse_ref):
    for i, (at, count) in enumerate(blocks_of(attn_ref.shape[0])):
        rows = pl.ds(2 * HALF + at, count)
        keys = at + count
        q = stacked(qkv_ref[rows, :256]) * jnp.bfloat16(HEAD_DIM**-0.5)
        k = qkv_ref[pl.ds(2 * HALF, keys), 256:320]
        v = qkv_ref[pl.ds(2 * HALF, keys), 320:384]
        scores = dot(q, k, 1, 1)
        column = lax.broadcasted_iota(jnp.int32, (count, keys), 1)
        row = lax.broadcasted_iota(jnp.int32, (count, 1), 0) + at
        seen = (column <= row) & (column >= start_of(row, facts_ref))
        scores = jnp.where(jnp.concatenate([seen] * 4, axis=0), scores, MASKED)
        top = jnp.max(scores, axis=1, keepdims=True)
        weights = jnp.exp(scores - top)
        total = jnp.sum(weights, axis=1, keepdims=True)
        out = dot(weights.astype(jnp.bfloat16), v) / total
        attn_ref[pl.ds(at, count), :] = unstacked(out).astype(jnp.bfloat16)
        lse_ref[i, :, : 4 * count] = as_row(top + jnp.log(total))


def short_forward(line, qkv, facts):
    rows = qkv.shape[0] - 2 * HALF
    return line(
        "short_forward",
        short_forward_kernel,
        (qkv, facts),
        [VMEM, SMEM],
        [shaped((rows, 256)), shaped((len(blocks_of(rows)), 8, 4 * HALF), jnp.float32)],
        [VMEM] * 2,
    )


def long_forward_kernel(q_ref, *refs):
    far_refs, (facts_ref, short_ref, attn_ref, lse_ref) = refs[:4], refs[4:]
    within = lax.broadcasted_iota(jnp.int32, (1, HALF), 1)
    blocks = far_refs[0].shape[0] // HALF
    for half in range(2):
        rows = pl.ds(half * HALF, HALF)
        q = stacked(q_ref[rows, :256]) * jnp.bfloat16(HEAD_DIM**-0.5)
        row = lax.broadcasted_iota(jnp.int32, (HALF, 1), 0)
        position = jnp.concatenate([row + facts_ref[FIRST_PLACE + half] * HALF] * 4, axis=0)
        top = jnp.full((4 * HALF, 1), MASKED, jnp.float32)
        total = jnp.zeros((4 * HALF, 1), jnp.float32)
        out = jnp.zeros((4 * HALF, HEAD_DIM), jnp.float32)
        for i, far_ref in enumerate(far_refs):
            scores = dot(q, far_ref[:, :HEAD_DIM], 1, 1)
            key = jnp.concatenate(
                [within + facts_ref[FAR_PLACE + i * blocks + k] * HALF for k in range(blocks)],
                axis=1,
            )
            seen = key <= position
            scores = jnp.where(seen, scores, MASKED)
            now = jnp.maximum(top, jnp.max(scores, axis=1, keepdims=True))
            weights = jnp.exp(scores - now)
            scale = jnp.exp(top - now)
            total = total * scale + jnp.sum(weights, axis=1, keepdims=True)
            out = out * scale + dot(weights.astype(jnp.bfloat16), far_ref[:, HEAD_DIM:])
            top = now
        attn_ref[rows, :] = unstacked(out / total).astype(jnp.bfloat16)
        lse_ref[half] = as_row(top + jnp.log(total))
    attn_ref[pl.ds(2 * HALF, short_ref.shape[0]), :] = short_ref[...]


def long_forward(line, q, far, facts, short, rows):
    return line(
        "long_forward",
        long_forward_kernel,
        (q, *far, facts, short),
        [VMEM] * 5 + [SMEM, VMEM],
        [shaped((rows, 256)), shaped((2, 8, 4 * HALF), jnp.float32)],
        [VMEM] * 2,
    )


def grad_terms(q, grad, k, v, seen, lse, delta):
    weights = jnp.where(seen, jnp.exp(dot(k, q, 1, 1) - lse), 0.0)
    grad_scores = (weights * (dot(v, grad, 1, 1) - delta)).astype(jnp.bfloat16)
    return (
        dot(grad_scores, k, 0, 0),
        dot(grad_scores, q),
        dot(weights.astype(jnp.bfloat16), grad),
    )


def row_product(left, right):
    return as_row(
        jnp.sum(left.astype(jnp.float32) * right.astype(jnp.float32), axis=1, keepdims=True)
    )[:1]


def short_backward_kernel(
    qkv_ref, facts_ref, attn_ref, grad_ref, lse_ref, cos_ref, sin_ref, out_ref, dk_ref, dv_ref
):
    packed = attn_ref.shape[0]
    scale = HEAD_DIM**-0.5
    dk_ref[...] = jnp.zeros_like(dk_ref)
    dv_ref[...] = jnp.zeros_like(dv_ref)
    for i, (at, count) in enumerate(blocks_of(packed)):
        rows = pl.ds(2 * HALF + at, count)
        keys = at + count
        q = stacked(qkv_ref[rows, :256]) * jnp.bfloat16(scale)
        k = qkv_ref[pl.ds(2 * HALF, keys), 256:320]
        v = qkv_ref[pl.ds(2 * HALF, keys), 320:384]
        grad = stacked(grad_ref[rows, :])
        delta = row_product(grad, stacked(attn_ref[pl.ds(at, count), :]))
        wide = count if count == HALF else 4 * count
        key = lax.broadcasted_iota(jnp.int32, (keys, wide), 0)
        query = lax.rem(lax.broadcasted_iota(jnp.int32, (1, wide), 1), count) + at
        seen = (key <= query) & (key >= start_of(query, facts_ref))
        seen = jnp.concatenate([seen] * (4 * count // wide), axis=1)
        dq, dk, dv = grad_terms(
            q,
            grad,
            k,
            v,
            seen,
            lse_ref[i, :1, : 4 * count],
            delta,
        )
        out_ref[pl.ds(at, count), :256] = turned(
            unstacked(dq * scale), cos_ref[rows, :], -sin_ref[rows, :]
        ).astype(jnp.bfloat16)
        dk_ref[pl.ds(0, keys), :] += dk
        dv_ref[pl.ds(0, keys), :] += dv
    rows = pl.ds(2 * HALF, packed)
    out_ref[:, 256:] = turned_key(
        jnp.concatenate([dk_ref[...], dv_ref[...]], axis=1), cos_ref[rows, :], -sin_ref[rows, :]
    ).astype(jnp.bfloat16)


def short_backward(line, qkv, facts, attn, grad, lse, cos_rows, sin_rows):
    rows = attn.shape[0]
    return line(
        "short_backward",
        short_backward_kernel,
        (qkv, facts, attn, grad, lse, cos_rows, sin_rows),
        [VMEM, SMEM] + [VMEM] * 5,
        [shaped((rows, 384))],
        [VMEM],
        [pltpu.VMEM((rows, HEAD_DIM), jnp.float32)] * 2,
    )[0]


def long_backward_kernel(q_ref, *refs):
    far_refs = refs[:4]
    facts_ref, attn_ref, grad_ref, lse_ref, cos_ref, sin_ref = refs[4:10]
    dq_ref, far_grad_ref, acc_ref = refs[10:]
    scale = HEAD_DIM**-0.5
    count = far_refs[0].shape[0]
    blocks = count // HALF
    queries = []
    for half in range(2):
        rows = pl.ds(half * HALF, HALF)
        grad = stacked(grad_ref[rows, :])
        column = lax.broadcasted_iota(jnp.int32, (1, HALF), 1)
        queries.append(
            (
                stacked(q_ref[rows, :256]) * jnp.bfloat16(scale),
                grad,
                lse_ref[half, :1],
                row_product(grad, stacked(attn_ref[rows, :])),
                jnp.concatenate([column + facts_ref[FIRST_PLACE + half] * HALF] * 4, axis=1),
            )
        )
    within = lax.broadcasted_iota(jnp.int32, (HALF, 1), 0)
    for i, far_ref in enumerate(far_refs):
        k, v = far_ref[:, :HEAD_DIM], far_ref[:, HEAD_DIM:]
        key = jnp.concatenate(
            [within + facts_ref[FAR_PLACE + i * blocks + n] * HALF for n in range(blocks)], axis=0
        )
        sums = []
        for half, (q, grad, lse, delta, position) in enumerate(queries):
            dq, dk, dv = grad_terms(q, grad, k, v, key <= position, lse, delta)
            acc_ref[half] = dq if i == 0 else acc_ref[half] + dq
            sums.append((dk, dv))
        total = jnp.concatenate(
            [sums[0][0] + sums[1][0], sums[0][1] + sums[1][1]], axis=1
        ).astype(jnp.bfloat16)
        rows = count // 4
        for n in range(4):
            far_grad_ref[n, pl.ds(i * rows, rows), :] = total[n * rows : (n + 1) * rows]
    for half in range(2):
        rows = pl.ds(half * HALF, HALF)
        dq_ref[rows, :] = turned(
            unstacked(acc_ref[half] * scale), cos_ref[rows, :], -sin_ref[rows, :]
        ).astype(jnp.bfloat16)


def long_backward(line, q, far, facts, attn, grad, lse, cos_rows, sin_rows):
    return line(
        "long_backward",
        long_backward_kernel,
        (q, *far, facts, attn, grad, lse, cos_rows, sin_rows),
        [VMEM] * 5 + [SMEM] + [VMEM] * 5,
        [shaped((2 * HALF, 256)), shaped((4, *far[0].shape))],
        [VMEM] * 2,
        [pltpu.VMEM((2, 4 * HALF, HEAD_DIM), jnp.float32)],
    )


def product_kernel(turned_right, left_ref, right_ref, out_ref):
    out_ref[...] = dot(left_ref[...], right_ref[...], 1, 1 if turned_right else 0).astype(
        out_ref.dtype
    )


def product(line, left, right, turned_right=False):
    rows, depth = left.shape
    width = right.shape[0] if turned_right else right.shape[1]
    block = rows // 2
    return line(
        "product",
        functools.partial(product_kernel, turned_right),
        (left, right),
        [rows_of(block, depth), once(right.shape)],
        [shaped((rows, width))],
        [rows_of(block, width)],
        grid=(2,),
    )[0]


def product_parts_kernel(terms, turned_right, *refs):
    outs = refs[2 * terms + 1 :]
    total = refs[2 * terms][...].astype(jnp.float32)
    for k in range(terms):
        total += dot(refs[2 * k][...], refs[2 * k + 1][...], 1, 1 if turned_right else 0)
    rows = outs[0].shape[0]
    for k, out_ref in enumerate(outs):
        out_ref[...] = total[k * rows : (k + 1) * rows].astype(jnp.bfloat16)


def product_parts(line, pairs, sent, turned_right=False):
    rows, width = sent.shape
    steps = 2 * len(pairs)
    block = width // steps
    specs = []
    for left, right in pairs:
        specs.append(once(left.shape))
        if turned_right:
            specs.append(rows_of(block, right.shape[1]))
        else:
            specs.append(columns_of(right.shape[0], block))
    return line(
        "product_parts",
        functools.partial(product_parts_kernel, len(pairs), turned_right),
        [array for pair in pairs for array in pair] + [sent],
        specs + [columns_of(rows, block)],
        [shaped((rows // 4, width))] * 4,
        [columns_of(rows // 4, block)] * 4,
        grid=(steps,),
    )


def merged(chunks):
    pieces = []
    for k in range(4):
        for (low, high), chunk in zip(CHUNKS, chunks):
            pieces.append(chunk[k * (high - low) : (k + 1) * (high - low)])
    return jnp.concatenate(pieces, axis=0)


def merged_product_kernel(count, with_sent, *refs):
    left = merged([ref[...] for ref in refs[:count]])
    total = dot(left, refs[count][...])
    outs = refs[count + 1 :]
    if with_sent:
        total += outs[0][...].astype(jnp.float32)
        outs = outs[1:]
    rows = outs[0].shape[0]
    for k, out_ref in enumerate(outs):
        out_ref[...] = total[k * rows : (k + 1) * rows].astype(jnp.bfloat16)


def merged_product(line, chunks, right, sent=None):
    rows = sum([chunk.shape[0] for chunk in chunks])
    depth, width = right.shape
    block = width // 2
    count = 1 if sent is None else 4
    extra = () if sent is None else (sent,)
    return line(
        "merged_product",
        functools.partial(merged_product_kernel, len(chunks), sent is not None),
        (*chunks, right, *extra),
        [once(chunk.shape) for chunk in chunks]
        + [columns_of(depth, block)]
        + [columns_of(rows, block)] * len(extra),
        [shaped((rows // count, width))] * count,
        [columns_of(rows // count, block)] * count,
        grid=(2,),
    )


def merged_back_kernel(count, *refs):
    left = merged([ref[...] for ref in refs[:count]])
    refs[-1][...] = dot(left, refs[count][...], 1, 1).astype(jnp.bfloat16)


def merged_back(line, chunks, right):
    rows = sum([chunk.shape[0] for chunk in chunks])
    return line(
        "merged_back",
        functools.partial(merged_back_kernel, len(chunks)),
        (*chunks, right),
        [VMEM] * (len(chunks) + 1),
        [shaped((rows, right.shape[0]))],
        [VMEM],
    )[0]


def arrange_kernel(facts_ref, rows_ref, *out_refs):
    del facts_ref
    for (low, high), out_ref in zip(CHUNKS, out_refs):
        out_ref[0] = rows_ref[0, low:high, :]


def arrange(line, rows, facts):
    _, count, d = rows.shape
    after = line.last

    def kernel(facts_ref, rows_ref, *refs):
        arrange_kernel(facts_ref, rows_ref, *refs[len(after) :])

    def source(i, facts_ref):
        core = jnp.where(i < 4, facts_ref[CORE_AT], 1 - facts_ref[CORE_AT])
        return core * 4 + (facts_ref[X_AT] + i) % 4, 0, 0

    results = pl.pallas_call(
        kernel,
        grid_spec=pltpu.PrefetchScalarGridSpec(
            num_scalar_prefetch=1,
            grid=(8,),
            in_specs=[pl.BlockSpec((1, count, d), source)] + [ANY] * len(after),
            out_specs=tuple(
                pl.BlockSpec((1, high - low, d), lambda i, facts_ref: (i, 0, 0))
                for low, high in CHUNKS
            ),
        ),
        out_shape=tuple(shaped((8, high - low, d)) for low, high in CHUNKS),
        compiler_params=PARAMS,
        cost_estimate=cost("arrange"),
        name="arrange",
    )(facts, rows, *after)
    return [array.reshape(-1, d) for array in results]


def weight_grad_kernel(count, beside, facts, *refs):
    facts_ref, *refs = refs if facts else (None, *refs)
    out_ref, width = refs[-1], refs[count].shape[1]
    total = dot(refs[0][...], refs[count][...], 0, 0)
    for k in range(1, count):
        total += dot(refs[k][...], refs[count + k][...], 0, 0)
    total = total.astype(jnp.bfloat16)
    if facts:
        rows = total.shape[0] // 2
        own_first = jnp.concatenate([total[rows:], total[:rows]])
        total = jnp.where(facts_ref[CORE_AT] == 0, total, own_first)
    out_ref[:, :width] = total
    if beside:
        out_ref[:, width:] = refs[2 * count][...]


def weight_grad(line, left, right, beside=(), facts=None):
    left = [piece if isinstance(piece, tuple) else (piece, 0) for piece in left]
    columns, width = left[0][0].shape[1], right[0].shape[1]
    whole = width + sum([array.shape[1] for array in beside])
    block = columns // 8

    def place(i, *facts_ref):
        if facts_ref:
            z = (i - facts_ref[0][Z_AT]) % 4
            yh = (i // 4 + facts_ref[0][YH_AT]) % 2
            return z * 2 + yh, 0
        return i % 4 * 2 + i // 4, 0

    def whole_block(i, *facts_ref):
        return 0, 0

    operands = (*[array for array, _ in left], *right, *beside)
    in_specs = (
        [
            pl.BlockSpec((part.shape[0], block), lambda i, *_, at=at: (at, i))
            for (_, at), part in zip(left, right)
        ]
        + [pl.BlockSpec(part.shape, whole_block, pipeline_mode=pl.Buffered(1)) for part in right]
        + [pl.BlockSpec((block, array.shape[1]), place) for array in beside]
    )
    out_spec = pl.BlockSpec((block, whole), place)
    kernel = functools.partial(weight_grad_kernel, len(left), len(beside), facts is not None)
    if facts is None:
        return line(
            "weight_grad",
            kernel,
            operands,
            in_specs,
            [shaped((columns, whole))],
            [out_spec],
            grid=(8,),
        )[0]
    after, count = line.last, len(operands) + 1

    def ordered(*refs):
        kernel(*refs[:count], *refs[count + len(after) :])

    result = pl.pallas_call(
        ordered,
        grid_spec=pltpu.PrefetchScalarGridSpec(
            num_scalar_prefetch=1,
            grid=(8,),
            in_specs=in_specs + [ANY] * len(after),
            out_specs=out_spec,
        ),
        out_shape=shaped((columns, whole)),
        compiler_params=PARAMS,
        cost_estimate=cost("weight_grad"),
        name="weight_grad",
    )(facts, *operands, *after)
    line.last = (result,)
    return result


def mix_kernel(low, high, tokens_ref, gain_ref, *refs):
    parts, (mixed_ref, hidden_ref) = refs[:4], refs[4:]
    mixed = tokens_ref[low:high, :].astype(jnp.float32) + total_of([ref[...] for ref in parts])
    inv = lax.rsqrt(jnp.mean(mixed * mixed, axis=-1, keepdims=True) + EPS)
    mixed_ref[...] = mixed
    hidden_ref[...] = (mixed * inv * gain_ref[...]).astype(jnp.bfloat16)


def mix(line, chunk, tokens, gain, parts):
    low, high = chunk
    d = tokens.shape[1]
    return line(
        "mix",
        functools.partial(mix_kernel, low, high),
        (tokens, gain, *parts),
        [VMEM] * 6,
        [shaped((high - low, d), jnp.float32), shaped((high - low, d))],
        [VMEM] * 2,
    )


def norm_back(grad_in, values, gain):
    inv = lax.rsqrt(jnp.mean(values * values, axis=-1, keepdims=True) + EPS)
    unit = values * inv
    scaled = grad_in * gain
    return inv * (scaled - unit * jnp.mean(scaled * unit, axis=-1, keepdims=True)), unit


def mix_back_kernel(low, high, grad_ref, mixed_ref, gain_ref, *refs):
    parts, (total_ref, low_ref, part_ref) = refs[:4], refs[4:]
    grad_in = total_of([ref[...] for ref in parts])
    back, unit = norm_back(grad_in, mixed_ref[...], gain_ref[...])
    total = grad_ref[low:high, :].astype(jnp.float32) + back
    total_ref[...] = total
    low_ref[...] = total.astype(jnp.bfloat16)
    part_ref[...] = jnp.sum(grad_in * unit, axis=0, keepdims=True)


def mix_back(line, chunk, grad, mixed, gain, parts):
    low, high = chunk
    rows, d = mixed.shape
    return line(
        "mix_back",
        functools.partial(mix_back_kernel, low, high),
        (grad, mixed, gain, *parts),
        [VMEM] * 7,
        [shaped((rows, d), jnp.float32), shaped((rows, d)), shaped((1, d), jnp.float32)],
        [VMEM] * 3,
    )


def mlp_kernel(hidden_ref, grad_act_ref, gate_ref, up_ref, act_ref, gate_out_ref, up_out_ref, *refs):
    hidden = hidden_ref[...]
    gate = dot(hidden, gate_ref[...])
    up = dot(hidden, up_ref[...])
    grad_act = grad_act_ref[...].astype(jnp.float32)
    sig = jax.nn.sigmoid(gate)
    silu = gate * sig
    act_ref[...] = (silu * up).astype(jnp.bfloat16)
    grad_gate = (grad_act * up * sig * (1.0 + gate * (1.0 - sig))).astype(jnp.bfloat16)
    grad_up = (grad_act * silu).astype(jnp.bfloat16)
    gate_out_ref[...] = grad_gate
    up_out_ref[...] = grad_up
    if refs:
        refs[0][...] = (
            dot(grad_gate, gate_ref[...], 1, 1) + dot(grad_up, up_ref[...], 1, 1)
        ).astype(jnp.bfloat16)


def mlp(line, hidden, grad_act, at, w_gate, w_up, with_back):
    rows, d = hidden.shape
    width = w_gate.shape[1]
    if with_back:
        block = rows // 2
        specs = [
            rows_of(block, d),
            pl.BlockSpec((block, width), lambda i: (2 * at + i, 0)),
            once((d, width)),
            once((d, width)),
        ]
        out_specs = [rows_of(block, width)] * 3 + [rows_of(block, d)]
    else:
        block = width // 4
        specs = [
            once((rows, d)),
            pl.BlockSpec((rows, block), lambda i: (at, i)),
            columns_of(d, block),
            columns_of(d, block),
        ]
        out_specs = [columns_of(rows, block)] * 3
    return line(
        "mlp",
        mlp_kernel,
        (hidden, grad_act, w_gate, w_up),
        specs,
        [shaped((rows, width))] * 3 + [shaped((rows, d))] * with_back,
        out_specs,
        grid=(2 if with_back else 4,),
    )


def hidden_grad_kernel(with_sent, low_ref, query_ref, kv_ref, hidden_ref, *refs):
    low = low_ref[...]
    grad = dot(low[:, :256], query_ref[...], 1, 1) + dot(low[:, 256:], kv_ref[...], 1, 1)
    gain = jnp.sum(grad * hidden_ref[...].astype(jnp.float32), axis=0, keepdims=True)
    if not with_sent:
        refs[0][...] = grad.astype(jnp.bfloat16)
        refs[1][...] = gain
        return
    sent_ref, gain_ref, mlp_gain_ref, *outs = refs
    grad += sent_ref[...].astype(jnp.float32)
    rows = outs[0].shape[0] - 8
    tail = []
    for values in (gain + gain_ref[...], mlp_gain_ref[...]):
        high = values.astype(jnp.bfloat16)
        tail += [high, (values - high.astype(jnp.float32)).astype(jnp.bfloat16)]
    tail = jnp.concatenate(tail + [jnp.zeros_like(tail[0])] * 4, axis=0)
    for k, out_ref in enumerate(outs):
        part = grad[k * rows : (k + 1) * rows].astype(jnp.bfloat16)
        out_ref[...] = jnp.concatenate([part, tail], axis=0)


def hidden_grad(line, low, w_query, w_key_value, hidden, sent=()):
    rows, d = hidden.shape
    block = d // 2
    if sent:
        outs = [shaped((rows // 4 + 8, d))] * 4
        out_specs = [columns_of(rows // 4 + 8, block)] * 4
    else:
        outs = [shaped((rows, d)), shaped((1, d), jnp.float32)]
        out_specs = [columns_of(rows, block), columns_of(1, block)]
    return line(
        "hidden_grad",
        functools.partial(hidden_grad_kernel, bool(sent)),
        (low, w_query, w_key_value, hidden, *sent),
        [once((rows, 384)), rows_of(block, 256), rows_of(block, 128), columns_of(rows, block)]
        + [columns_of(array.shape[0], block) for array in sent],
        outs,
        out_specs,
        grid=(2,),
    )


def gate_kernel(*refs):
    del refs


def gated(line, arrays):
    line.last = tuple([array for array in line.last if all([array is not one for one in arrays])])
    return line(
        "gated",
        gate_kernel,
        arrays,
        [ANY] * len(arrays),
        [shaped(array.shape, array.dtype) for array in arrays],
        [ANY] * len(arrays),
        input_output_aliases={k: k for k in range(len(arrays))},
    )


def out_mix_kernel(*refs):
    mixed = jnp.concatenate([ref[...] for ref in refs[:-5]], axis=0)
    refs[-1][...] = (mixed + total_of([ref[...] for ref in refs[-5:-1]])).astype(jnp.bfloat16)


def final_kernel(tokens_ref, gain_ref, *refs):
    out_ref, gains_ref = refs[-2:]
    total = total_of([ref[...] for ref in refs[-6:-2]])
    rows = out_ref.shape[0]
    back, _ = norm_back(total[:rows], tokens_ref[...].astype(jnp.float32), gain_ref[...])
    mixed = jnp.concatenate([ref[...] for ref in refs[:-6]], axis=0)
    out_ref[...] = (mixed + back).astype(jnp.bfloat16)
    sums = total[rows : rows + 8]
    gains_ref[...] = jnp.concatenate([sums[:1] + sums[1:2], sums[2:3] + sums[3:4]], axis=0)


def turn_far_kernel(grad_ref, cos_ref, sin_ref, long_ref, short_ref, out_ref):
    rows = pl.ds(0, 2 * HALF)
    out_ref[rows, :256] = long_ref[...]
    out_ref[rows, 256:] = turned_key(grad_ref[...], cos_ref[rows, :], -sin_ref[rows, :]).astype(
        jnp.bfloat16
    )
    out_ref[pl.ds(2 * HALF, short_ref.shape[0]), :] = short_ref[...]


def local(
    tokens,
    lengths,
    place,
    attn_gain,
    w_query,
    w_key,
    w_value,
    w_out,
    mlp_gain,
    w_gate,
    w_up,
    w_down,
    out_grad,
):
    rows, d = tokens.shape
    group_rows = rows * 8
    half_rows = rows * 4
    long_rows = 2 * HALF
    dp_index, mp_index = lax.axis_index("dp"), lax.axis_index("mp")
    yh, z, core = dp_index // 8, dp_index // 2 % 4, dp_index % 2
    yl, x = mp_index // 4, mp_index % 4
    native = core == yl
    line = Line()
    mlp_gain_row = mlp_gain.reshape(1, d)

    tokens = send(tokens, TURN)
    lengths = send(lengths, TURN)[0]
    w_key_value = send(jnp.concatenate([w_key, w_value], axis=1), WEIGHT_LOW)
    w_query = send(w_query, WEIGHT_LOW)
    w_out = send(w_out, WEIGHT_LOW)
    w_down = send(w_down, WEIGHT_HIGH)
    w_gate = send(w_gate, WEIGHT_LOW)
    w_up = send(w_up, WEIGHT_HIGH)
    out_grad = turn(out_grad, native)

    step = jnp.arange(16, dtype=jnp.int32)
    far_yh = jnp.where(step % 4 >= 2, 1 - yh, yh)
    far_yl = jnp.where((step % 4 == 1) | (step % 4 == 2), 1 - yl, yl)
    far_group = (far_yh * 4 + (z + step // 4) % 4) * 2 + far_yl
    far_index = (2 * far_group[:, None] + jnp.arange(2, dtype=jnp.int32)[None, :]).reshape(-1)
    half_ids = jnp.arange(place.shape[0], dtype=jnp.int32)
    far_place = jnp.sum(jnp.where(far_index[:, None] == half_ids[None, :], place, 0), axis=1)
    facts = jnp.concatenate(
        [
            far_place[:2],
            jnp.stack([lengths[0], lengths[0] + lengths[1], core, x, z, yh]),
            far_place,
        ]
    ).astype(jnp.int32)

    residual = tokens.astype(jnp.float32)
    inv_one = lax.rsqrt(jnp.mean(residual * residual, axis=-1, keepdims=True) + EPS)
    hidden_one = collect((residual * inv_one * attn_gain).astype(jnp.bfloat16))
    freq = jnp.tile(inverse_freq(HEAD_DIM), 4).reshape(1, 128)
    line.last += (w_query, w_key_value)
    cos_gathered, sin_gathered, cos_ordered, sin_ordered = line(
        "tables",
        functools.partial(tables_kernel, rows),
        (facts, freq),
        [SMEM, VMEM],
        [shaped((n, 128), jnp.float32) for n in (group_rows,) * 4],
        [VMEM] * 4,
    )
    hidden_own = join(line, hidden_one)
    hidden_one = (hidden_own, send(hidden_own, CORE))
    qkv = []
    for at, half in enumerate(hidden_one):
        line.last += (w_down,) * at
        qkv.append(
            project_qkv(line, half, w_query, w_key_value, cos_gathered, sin_gathered, at)
        )
    (out_grad,) = gated(line, (out_grad,))
    grad_rows = lax.all_gather(out_grad, BOTH, axis=0, axis_index_groups=CHIP_GROUPS)
    qkv = in_order(jnp.stack(qkv), core, x)
    near_rows = qkv[:long_rows, 256:]
    ring_rows = jnp.concatenate(
        [near_rows, send(near_rows, Y_LOW), send(near_rows, Y_HIGH), send(near_rows, Y_FAR)]
    )
    far_rows = (
        ring_rows, send(ring_rows, Z_DOWN), send(ring_rows, Z_FAR), send(ring_rows, Z_UP)
    )
    line.last += (ring_rows,)
    short_attn, short_lse = short_forward(line, qkv, facts)
    attn_ordered, long_lse = long_forward(line, qkv, far_rows, facts, short_attn, group_rows)
    attn_rows = from_order(attn_ordered, core, x)
    attn_rows = [chunks_of(attn_rows[half]) for half in range(2)]

    sent = [send(product(line, part, w_out), CORE) for part in attn_rows[1]]
    mixed_parts = [
        scatter(product_parts(line, [(part, w_out)], other))
        for part, other in zip(attn_rows[0], sent)
    ]
    grad_rows = arrange(line, grad_rows, facts)
    grad_act = [product(line, part, w_down, True) for part in grad_rows]
    mixed, hidden_two = [], []
    for chunk, parts in zip(CHUNKS, mixed_parts):
        mixed_rows, hidden_rows = mix(line, chunk, tokens, mlp_gain_row, parts)
        mixed.append(mixed_rows)
        hidden_two.append(collect(hidden_rows))

    count = len(CHUNKS)
    own, other, act, gate, up, back = ([None] * count for _ in range(6))

    def first_half(n):
        own[n] = join(line, hidden_two[n])
        other[n] = send(own[n], CORE)
        act[n], gate[n], up[n] = mlp(line, own[n], grad_act[n], 0, w_gate, w_up, False)

    def second_half(n):
        *terms, sum_back = mlp(line, other[n], grad_act[n], 1, w_gate, w_up, True)
        act[n], gate[n], up[n] = zip((act[n], gate[n], up[n]), terms)
        back[n] = send(sum_back, CORE)

    hidden_parts = []
    first_half(0)
    second_half(0)
    for n in range(count):
        if n + 1 < count:
            first_half(n + 1)
        if n + 1 == count:
            (down_rows,) = merged_product(line, [part[1] for part in act], w_down)
            down_rows = send(down_rows, CORE)
        terms = [(gate[n][0], w_gate), (up[n][0], w_up)]
        hidden_parts.append(scatter(product_parts(line, terms, back[n], True)))
        if n + 1 < count:
            second_half(n + 1)
    act, gate, up = [[pair[k] for pair in part for k in range(2)] for part in (act, gate, up)]
    hidden_two = [piece for pair in zip(own, other) for piece in pair]

    pieces = [(part, at) for part in grad_rows for at in range(2)]
    both_part = weight_grad(line, hidden_two, up, (weight_grad(line, hidden_two, gate),))
    grad_mixed, mixed_grad, gain_parts = [], [], []
    for n, (chunk, parts) in enumerate(zip(CHUNKS, hidden_parts)):
        total, low, gain_part = mix_back(line, chunk, out_grad, mixed[n], mlp_gain_row, parts)
        grad_mixed.append(total)
        mixed_grad.append(collect(low))
        gain_parts.append(gain_part)
    both_kept = reduce_near(gated(line, (both_part,))[0])
    down_part = weight_grad(line, pieces, act)
    out_parts = scatter(merged_product(line, act[0::2], w_down, down_rows))

    grad_own = [join(line, parts) for parts in mixed_grad]
    grad_other = [send(part, CORE) for part in grad_own]
    grad_attn = jnp.stack([merged_back(line, part, w_out) for part in (grad_own, grad_other)])
    grad_attn = in_order(grad_attn, core, x)
    long_dq, far_terms = long_backward(
        line,
        qkv,
        far_rows,
        facts,
        attn_ordered,
        grad_attn,
        long_lse,
        cos_ordered,
        sin_ordered,
    )
    ring_terms = total_of(
        (
            far_terms[0],
            send(far_terms[1], Y_LOW),
            send(far_terms[2], Y_HIGH),
            send(far_terms[3], Y_FAR),
        )
    ).astype(jnp.bfloat16)
    near = ring_terms.reshape(4, long_rows, -1)
    far_grads = total_of(
        (near[0], send(near[1], Z_UP), send(near[2], Z_FAR), send(near[3], Z_DOWN))
    )
    line.last += out_parts[1:]
    short_low = short_backward(
        line, qkv, facts, short_attn, grad_attn, short_lse, cos_ordered, sin_ordered
    )
    out_part = weight_grad(
        line,
        [piece for pair in zip(grad_own, grad_other) for piece in pair],
        [piece for pair in zip(*attn_rows) for piece in pair],
        (),
        facts,
    )
    (low_ordered,) = line(
        "turn_far",
        turn_far_kernel,
        (far_grads, cos_ordered, sin_ordered, long_dq, short_low),
        [VMEM] * 5,
        [shaped((group_rows, 384))],
        [VMEM],
    )
    low_rows = from_order(low_ordered, core, x)
    line.last += (both_kept,)
    down_kept = reduce_near(gated(line, (down_part,))[0])
    back, gain_other = hidden_grad(line, low_rows[1], w_query, w_key_value, hidden_one[1])
    back = send(back, CORE)
    last_part = weight_grad(line, hidden_one, (low_rows[0], low_rows[1]), (out_part,), facts)
    grad_parts = scatter(
        hidden_grad(
            line,
            low_rows[0],
            w_query,
            w_key_value,
            hidden_one[0],
            (back, gain_other, sum(gain_parts[1:], gain_parts[0])),
        )[:4]
    )
    last_kept, first_hop = reduce_ring(gated(line, (last_part,))[0])
    (output,) = line(
        "out_mix",
        out_mix_kernel,
        (*mixed, *out_parts),
        [VMEM] * (len(mixed) + 4),
        [shaped((rows, d))],
        [VMEM],
    )
    output = turn(output, native)
    line.last += first_hop
    grad_tokens, gains = line(
        "final",
        final_kernel,
        (tokens, attn_gain.reshape(1, d), *grad_mixed, *grad_parts),
        [VMEM] * (2 + len(grad_mixed) + 4),
        [shaped((rows, d)), shaped((2, d), jnp.float32)],
        [VMEM] * 2,
    )
    both_kept, down_kept = gated(line, (both_kept, down_kept))
    ff_sum = reduce_y(jnp.concatenate([both_kept, down_kept], axis=1))
    grad_tokens = turn(grad_tokens, native)
    gains = all_sum(gains)
    last_sum = sum_groups(last_kept, native)
    ff = w_gate.shape[1]
    return (
        output,
        grad_tokens,
        gains[0] / attn_gain,
        last_sum[:, :256],
        last_sum[:, 256:320],
        last_sum[:, 320:384],
        last_sum[:, 384:].T,
        gains[1],
        ff_sum[:, ff : 2 * ff],
        ff_sum[:, :ff],
        ff_sum[:, 2 * ff :].T,
    )


def solution(mesh):
    placed = (
        P(("dp", "mp"), None),
        P("dp", None),
        P(),
        P(),
        P(None, "mp"),
        P(None, "mp"),
        P(None, "mp"),
        P("mp", None),
        P(),
        P(None, "mp"),
        P(None, "mp"),
        P("mp", None),
        P(("dp", "mp"), None),
    )
    return jax.shard_map(
        local,
        mesh=mesh,
        in_specs=placed,
        out_specs=(
            P(("dp", "mp"), None),
            P(("dp", "mp"), None),
            P(),
            P("dp", "mp"),
            P("dp", "mp"),
            P("dp", "mp"),
            P("mp", "dp"),
            P(),
            P("dp", "mp"),
            P("dp", "mp"),
            P("mp", "dp"),
        ),
        check_vma=False,
    )
```

```python
import functools

import jax
import jax.numpy as jnp
from jax import lax
from jax.experimental import pallas as pl
from jax.experimental.pallas import tpu as pltpu
from jax.sharding import PartitionSpec as P

HEAD_DIM = 64
HALF = 128
MASKED = -1e30


EPS = 1e-05
THETA = 500000.0

BOTH = ("dp", "mp")


def place_of(yh, z, c, yl, x):
    return ((yh * 4 + z) * 2 + c) * 8 + yl * 4 + x


def pairs_of(target, sender=lambda yh, z, c, yl, x: True):
    return [
        (place_of(yh, z, c, yl, x), place_of(*target(yh, z, c, yl, x)))
        for yh in range(2)
        for z in range(4)
        for c in range(2)
        for yl in range(2)
        for x in range(4)
        if sender(yh, z, c, yl, x)
    ]


X_UP = pairs_of(lambda yh, z, c, yl, x: (yh, z, c, yl, (x + 1) % 4))
X_DOWN = pairs_of(lambda yh, z, c, yl, x: (yh, z, c, yl, (x + 3) % 4))
X_FAR = pairs_of(lambda yh, z, c, yl, x: (yh, z, c, yl, (x + 2) % 4))
Z_UP = pairs_of(lambda yh, z, c, yl, x: (yh, (z + 1) % 4, c, yl, x))
Z_DOWN = pairs_of(lambda yh, z, c, yl, x: (yh, (z + 3) % 4, c, yl, x))
Z_NEXT = pairs_of(lambda yh, z, c, yl, x: (yh, z ^ 1, c, yl, x))
Z_FAR = pairs_of(lambda yh, z, c, yl, x: (yh, (z + 2) % 4, c, yl, x))
CORE = pairs_of(lambda yh, z, c, yl, x: (yh, z, 1 - c, yl, x))
Y_LOW = pairs_of(lambda yh, z, c, yl, x: (yh, z, c, 1 - yl, x))
Y_HIGH = pairs_of(lambda yh, z, c, yl, x: (1 - yh, z, c, 1 - yl, x))
Y_FAR = pairs_of(lambda yh, z, c, yl, x: (1 - yh, z, c, yl, x))
TURN = pairs_of(lambda yh, z, c, yl, x: (yh, z, yl, c, x))
NATIVE = lambda yh, z, c, yl, x: c == yl
FOREIGN = lambda yh, z, c, yl, x: c != yl
FOREIGN_TURN = pairs_of(lambda yh, z, c, yl, x: (yh, z, yl, c, x), FOREIGN)
FOREIGN_LOW = pairs_of(lambda yh, z, c, yl, x: (yh, z, c, 1 - yl, x), FOREIGN)
FOREIGN_HIGH = pairs_of(lambda yh, z, c, yl, x: (1 - yh, z, c, 1 - yl, x), FOREIGN)
NATIVE_FAR = pairs_of(lambda yh, z, c, yl, x: (1 - yh, z, c, yl, x), NATIVE)
NATIVE_CORE = pairs_of(lambda yh, z, c, yl, x: (yh, z, 1 - c, yl, x), NATIVE)
WEIGHT_LOW = pairs_of(
    lambda yh, z, c, yl, x: (yh, z, c, 1 - yl, x) if c == yl else (yh, z, 1 - c, yl, x)
)
WEIGHT_HIGH = pairs_of(
    lambda yh, z, c, yl, x: (1 - yh, z, c, 1 - yl, x) if c == yl else (yh, z, 1 - c, yl, x)
)
Z_GROUPS = [
    [place_of(yh, z, c, yl, x) for z in range(4)]
    for yh in range(2)
    for c in range(2)
    for yl in range(2)
    for x in range(4)
]


Y_GROUPS = [
    [place_of(yh, z, c, yl, x) for yh in range(2) for yl in range(2)]
    for z in range(4)
    for c in range(2)
    for x in range(4)
]
CHIP_GROUPS = [
    [place_of(yh, z, c, yl, x) for c in range(2) for x in range(4)]
    for yh in range(2)
    for z in range(4)
    for yl in range(2)
]


def send(values, pairs):
    return lax.ppermute(values, BOTH, pairs)


CHUNKS = ((0, 136),)

VMEM = pl.BlockSpec(memory_space=pltpu.VMEM)
SMEM = pl.BlockSpec(memory_space=pltpu.SMEM)
ANY = pl.BlockSpec(memory_space=pl.ANY)
PARAMS = pltpu.CompilerParams(vmem_limit_bytes=64 * 1024 * 1024)
LASTS = {
    "tables": 1,
    "join": 1,
    "project_qkv": 1,
    "short_forward": 6,
    "long_forward": 13,
    "product": 3,
    "product_parts": 5,
    "arrange": 5,
    "mix": 3,
    "mlp": 10,
    "weight_grad": 2,
    "mix_back": 4,
    "merged_product": 2,
    "merged_back": 3,
    "long_backward": 16,
    "short_backward": 10,
    "turn_far": 2,
    "hidden_grad": 5,
    "out_mix": 4,
    "final": 4,
    "gated": 1,
}


def cost(name):
    return pl.CostEstimate(
        flops=int(1.15e9 * LASTS[name]), bytes_accessed=1000, transcendentals=0
    )


def shaped(shape, dtype=jnp.bfloat16):
    return pltpu.HBM(tuple(shape), dtype)


def rows_of(block, width):
    return pl.BlockSpec((block, width), lambda i: (i, 0))


def columns_of(rows, block):
    return pl.BlockSpec((rows, block), lambda i: (0, i))


def once(shape):
    return pl.BlockSpec(tuple(shape), lambda i: (0,) * len(shape), pipeline_mode=pl.Buffered(1))


class Line:
    def __init__(self):
        self.last = ()

    def __call__(self, name, kernel, operands, in_specs, outs, out_specs, scratch=(), **grid):
        after = self.last
        count = len(operands)

        def ordered(*refs):
            kernel(*refs[:count], *refs[count + len(after) :])

        results = pl.pallas_call(
            ordered,
            out_shape=tuple(outs),
            in_specs=list(in_specs) + [ANY] * len(after),
            out_specs=tuple(out_specs),
            scratch_shapes=list(scratch),
            compiler_params=PARAMS,
            cost_estimate=cost(name),
            name=name,
            **grid,
        )(*operands, *after)
        self.last = (min(results, key=lambda array: array.size),)
        return results


def turn(values, native):
    return jnp.where(native, values, send(values, FOREIGN_TURN))


def dot(left, right, left_dim=1, right_dim=0):
    return lax.dot_general(
        left, right, (((left_dim,), (right_dim,)), ((), ())), preferred_element_type=jnp.float32
    )


def total_of(parts):
    one, two, three, four = [part.astype(jnp.float32) for part in parts]
    return (one + two) + (three + four)


def scatter(parts):
    return (
        parts[0],
        send(parts[1], X_UP),
        send(parts[2], X_FAR),
        send(parts[3], X_DOWN),
    )


def collect(rows):
    return (rows, send(rows, X_DOWN), send(rows, X_FAR), send(rows, X_UP))


def in_order(pair, core, x):
    half = pair.shape[1]
    start = (4 - x) % 4 * (half // 4)
    pair = lax.dynamic_slice_in_dim(jnp.concatenate([pair, pair], axis=1), start, half, axis=1)
    return jnp.where(core == 0, pair, pair[::-1]).reshape(2 * half, -1)


def from_order(values, core, x):
    half = values.shape[0] // 2
    pair = values.reshape(2, half, -1)
    pair = jnp.where(core == 0, pair, pair[::-1])
    return lax.dynamic_slice_in_dim(
        jnp.concatenate([pair, pair], axis=1), x * (half // 4), half, axis=1
    )


def chunks_of(half):
    cut = half.reshape(4, half.shape[0] // 4, -1)
    return [cut[:, low:high].reshape(4 * (high - low), -1) for low, high in CHUNKS]


def plus(left, right):
    return (left.astype(jnp.float32) + right.astype(jnp.float32)).astype(jnp.bfloat16)


def reduce_near(grad):
    return lax.psum_scatter(
        grad, BOTH, scatter_dimension=0, tiled=True, axis_index_groups=Z_GROUPS
    )


def reduce_y(kept, native):
    kept = lax.psum_scatter(
        kept, BOTH, scatter_dimension=0, tiled=True, axis_index_groups=Y_GROUPS
    )
    return turn(kept, native).astype(jnp.float32)


def reduce_ring(grad):
    here, above, far, below = jnp.split(grad, 4)
    rows = far.shape[0] // 2
    from_below, from_above = send(far[:rows], Z_UP), send(far[rows:], Z_DOWN)
    above = send(jnp.concatenate([plus(above[:rows], from_below), above[rows:]]), Z_UP)
    below = send(jnp.concatenate([below[:rows], plus(below[rows:], from_above)]), Z_DOWN)
    total = here.astype(jnp.float32) + above.astype(jnp.float32) + below.astype(jnp.float32)
    return total.astype(jnp.bfloat16), (from_below, from_above)


def sum_groups(kept, native):
    near, far = jnp.split(kept, 2)
    across, low, high = send(far, NATIVE_FAR), send(near, FOREIGN_LOW), send(far, FOREIGN_HIGH)
    total = total_of((near, low, high, across))
    rows = total.shape[0] // 2
    passed = send(total[rows:].astype(jnp.bfloat16), NATIVE_CORE).astype(jnp.float32)
    return jnp.where(native, total[:rows], passed)


def all_sum(values):
    for pairs in (CORE, Y_LOW, Y_FAR, Z_NEXT, Z_FAR):
        values += send(values, pairs)
    return values


def inverse_freq(head_width):
    indices = jnp.arange(head_width // 2, dtype=jnp.float32)
    base_freq = jnp.exp(-jnp.log(THETA) * 2.0 * indices / head_width)
    wavelength = 2.0 * jnp.pi / base_freq
    smooth = (8192.0 / wavelength - 1.0) / 3.0
    blended = (1.0 - smooth) * base_freq / 32.0 + smooth * base_freq
    return jnp.where(
        wavelength < 2048.0, base_freq, jnp.where(wavelength > 8192.0, base_freq / 32.0, blended)
    )


FIRST_PLACE, SECOND_START, THIRD_START, CORE_AT, X_AT, Z_AT, YH_AT, FAR_PLACE = 0, 2, 3, 4, 5, 6, 7, 8


def tables_kernel(rows, facts_ref, freq_ref, *out_refs):
    sign = jnp.where(lax.broadcasted_iota(jnp.int32, (1, 128), 1) % 64 < 32, -1.0, 1.0)
    group_rows, half_rows = rows * 8, rows * 4
    for gathered, (cos_ref, sin_ref) in enumerate((out_refs[:2], out_refs[2:])):
        row = lax.broadcasted_iota(jnp.int32, cos_ref.shape, 0)
        if gathered == 0:
            other = (row >= half_rows).astype(jnp.int32)
            rest = row - other * half_rows
            step = sum([(rest >= k * rows).astype(jnp.int32) for k in (1, 2, 3)])
            core = jnp.where(other == 0, facts_ref[CORE_AT], 1 - facts_ref[CORE_AT])
            row = core * half_rows + ((facts_ref[X_AT] + step) & 3) * rows + rest - step * rows
        packed = row - 2 * HALF
        second, third = facts_ref[SECOND_START], facts_ref[THIRD_START]
        start = jnp.where(packed >= third, third, jnp.where(packed >= second, second, 0))
        own = jnp.where(row < HALF, facts_ref[FIRST_PLACE], facts_ref[FIRST_PLACE + 1])
        position = jnp.where(row < 2 * HALF, own * HALF + (row & (HALF - 1)), packed - start)
        angles = position.astype(jnp.float32) * freq_ref[...]
        cos_ref[...] = jnp.cos(angles)
        sin_ref[...] = jnp.sin(angles) * sign


def turned(values, cos_rows, sin_rows):
    first = lax.broadcasted_iota(jnp.int32, (1, 128), 1) % 64 < 32
    tiles = []
    for at in range(0, values.shape[1], 128):
        tile = values[:, at : at + 128]
        swapped = jnp.where(first, pltpu.roll(tile, 96, 1), pltpu.roll(tile, 32, 1))
        tiles.append(tile * cos_rows + swapped * sin_rows)
    return tiles[0] if len(tiles) == 1 else jnp.concatenate(tiles, axis=1)


def turned_key(values, cos_rows, sin_rows):
    key = lax.broadcasted_iota(jnp.int32, (1, 128), 1) < HEAD_DIM
    return jnp.where(key, turned(values, cos_rows, sin_rows), values)


def join_kernel(count, *refs):
    for k in range(count):
        refs[-1][k] = refs[k][...]


def join(line, pieces):
    count = len(pieces)
    rows, width = pieces[0].shape
    block = width // 2
    (joined,) = line(
        "join",
        functools.partial(join_kernel, count),
        pieces,
        [columns_of(rows, block)] * count,
        [shaped((count, rows, width))],
        [pl.BlockSpec((count, rows, block), lambda i: (0, 0, i))],
        grid=(2,),
    )
    return joined.reshape(count * rows, width)


def qkv_kernel(hidden_ref, query_ref, kv_ref, cos_ref, sin_ref, out_ref):
    hidden = hidden_ref[...]
    cos_rows, sin_rows = cos_ref[...], sin_ref[...]
    out_ref[:, :256] = turned(dot(hidden, query_ref[...]), cos_rows, sin_rows).astype(jnp.bfloat16)
    out_ref[:, 256:] = turned_key(dot(hidden, kv_ref[...]), cos_rows, sin_rows).astype(
        jnp.bfloat16
    )


def project_qkv(line, hidden, w_query, w_key_value, cos_rows, sin_rows, at):
    rows, d = hidden.shape
    block = rows // 2
    table = pl.BlockSpec((block, 128), lambda i: (i + 2 * at, 0))
    return line(
        "project_qkv",
        qkv_kernel,
        (hidden, w_query, w_key_value, cos_rows, sin_rows),
        [rows_of(block, d), once((d, 256)), once((d, 128)), table, table],
        [shaped((rows, 384))],
        [rows_of(block, 384)],
        grid=(2,),
    )[0]


def stacked(block):
    return jnp.concatenate(
        [block[:, h * HEAD_DIM : (h + 1) * HEAD_DIM] for h in range(4)], axis=0
    )


def unstacked(block):
    rows = block.shape[0] // 4
    return jnp.concatenate([block[h * rows : (h + 1) * rows] for h in range(4)], axis=1)


def as_row(column):
    return jnp.transpose(jnp.broadcast_to(column, (column.shape[0], 128)))[:8]


def start_of(row, facts_ref):
    second, third = facts_ref[SECOND_START], facts_ref[THIRD_START]
    return jnp.where(row >= third, third, jnp.where(row >= second, second, 0))


def blocks_of(rows):
    return [(at, min(HALF, rows - at)) for at in range(0, rows, HALF)]


def short_forward_kernel(qkv_ref, facts_ref, attn_ref, lse_ref):
    for i, (at, count) in enumerate(blocks_of(attn_ref.shape[0])):
        rows = pl.ds(2 * HALF + at, count)
        keys = at + count
        q = stacked(qkv_ref[rows, :256]) * jnp.bfloat16(HEAD_DIM**-0.5)
        k = qkv_ref[pl.ds(2 * HALF, keys), 256:320]
        v = qkv_ref[pl.ds(2 * HALF, keys), 320:384]
        scores = dot(q, k, 1, 1)
        column = lax.broadcasted_iota(jnp.int32, (count, keys), 1)
        row = lax.broadcasted_iota(jnp.int32, (count, 1), 0) + at
        seen = (column <= row) & (column >= start_of(row, facts_ref))
        scores = jnp.where(jnp.concatenate([seen] * 4, axis=0), scores, MASKED)
        top = jnp.max(scores, axis=1, keepdims=True)
        weights = jnp.exp(scores - top)
        total = jnp.sum(weights, axis=1, keepdims=True)
        out = dot(weights.astype(jnp.bfloat16), v) / total
        attn_ref[pl.ds(at, count), :] = unstacked(out).astype(jnp.bfloat16)
        lse_ref[i, :, : 4 * count] = as_row(top + jnp.log(total))


def short_forward(line, qkv, facts):
    rows = qkv.shape[0] - 2 * HALF
    return line(
        "short_forward",
        short_forward_kernel,
        (qkv, facts),
        [VMEM, SMEM],
        [shaped((rows, 256)), shaped((len(blocks_of(rows)), 8, 4 * HALF), jnp.float32)],
        [VMEM] * 2,
    )


def long_forward_kernel(q_ref, *refs):
    far_refs, (facts_ref, short_ref, attn_ref, lse_ref) = refs[:4], refs[4:]
    within = lax.broadcasted_iota(jnp.int32, (1, HALF), 1)
    blocks = far_refs[0].shape[0] // HALF
    for half in range(2):
        rows = pl.ds(half * HALF, HALF)
        q = stacked(q_ref[rows, :256]) * jnp.bfloat16(HEAD_DIM**-0.5)
        row = lax.broadcasted_iota(jnp.int32, (HALF, 1), 0)
        position = jnp.concatenate([row + facts_ref[FIRST_PLACE + half] * HALF] * 4, axis=0)
        top = jnp.full((4 * HALF, 1), MASKED, jnp.float32)
        total = jnp.zeros((4 * HALF, 1), jnp.float32)
        out = jnp.zeros((4 * HALF, HEAD_DIM), jnp.float32)
        for i, far_ref in enumerate(far_refs):
            scores = dot(q, far_ref[:, :HEAD_DIM], 1, 1)
            key = jnp.concatenate(
                [within + facts_ref[FAR_PLACE + i * blocks + k] * HALF for k in range(blocks)],
                axis=1,
            )
            seen = key <= position
            scores = jnp.where(seen, scores, MASKED)
            now = jnp.maximum(top, jnp.max(scores, axis=1, keepdims=True))
            weights = jnp.exp(scores - now)
            scale = jnp.exp(top - now)
            total = total * scale + jnp.sum(weights, axis=1, keepdims=True)
            out = out * scale + dot(weights.astype(jnp.bfloat16), far_ref[:, HEAD_DIM:])
            top = now
        attn_ref[rows, :] = unstacked(out / total).astype(jnp.bfloat16)
        lse_ref[half] = as_row(top + jnp.log(total))
    attn_ref[pl.ds(2 * HALF, short_ref.shape[0]), :] = short_ref[...]


def long_forward(line, q, far, facts, short, rows):
    return line(
        "long_forward",
        long_forward_kernel,
        (q, *far, facts, short),
        [VMEM] * 5 + [SMEM, VMEM],
        [shaped((rows, 256)), shaped((2, 8, 4 * HALF), jnp.float32)],
        [VMEM] * 2,
    )


def grad_terms(q, grad, k, v, seen, lse, delta):
    weights = jnp.where(seen, jnp.exp(dot(k, q, 1, 1) - lse), 0.0)
    grad_scores = (weights * (dot(v, grad, 1, 1) - delta)).astype(jnp.bfloat16)
    return (
        dot(grad_scores, k, 0, 0),
        dot(grad_scores, q),
        dot(weights.astype(jnp.bfloat16), grad),
    )


def row_product(left, right):
    return as_row(
        jnp.sum(left.astype(jnp.float32) * right.astype(jnp.float32), axis=1, keepdims=True)
    )[:1]


def short_backward_kernel(
    qkv_ref, facts_ref, attn_ref, grad_ref, lse_ref, cos_ref, sin_ref, out_ref, dk_ref, dv_ref
):
    packed = attn_ref.shape[0]
    scale = HEAD_DIM**-0.5
    dk_ref[...] = jnp.zeros_like(dk_ref)
    dv_ref[...] = jnp.zeros_like(dv_ref)
    for i, (at, count) in enumerate(blocks_of(packed)):
        rows = pl.ds(2 * HALF + at, count)
        keys = at + count
        q = stacked(qkv_ref[rows, :256]) * jnp.bfloat16(scale)
        k = qkv_ref[pl.ds(2 * HALF, keys), 256:320]
        v = qkv_ref[pl.ds(2 * HALF, keys), 320:384]
        grad = stacked(grad_ref[rows, :])
        delta = row_product(grad, stacked(attn_ref[pl.ds(at, count), :]))
        wide = count if count == HALF else 4 * count
        key = lax.broadcasted_iota(jnp.int32, (keys, wide), 0)
        query = lax.rem(lax.broadcasted_iota(jnp.int32, (1, wide), 1), count) + at
        seen = (key <= query) & (key >= start_of(query, facts_ref))
        seen = jnp.concatenate([seen] * (4 * count // wide), axis=1)
        dq, dk, dv = grad_terms(
            q,
            grad,
            k,
            v,
            seen,
            lse_ref[i, :1, : 4 * count],
            delta,
        )
        out_ref[pl.ds(at, count), :256] = turned(
            unstacked(dq * scale), cos_ref[rows, :], -sin_ref[rows, :]
        ).astype(jnp.bfloat16)
        dk_ref[pl.ds(0, keys), :] += dk
        dv_ref[pl.ds(0, keys), :] += dv
    rows = pl.ds(2 * HALF, packed)
    out_ref[:, 256:] = turned_key(
        jnp.concatenate([dk_ref[...], dv_ref[...]], axis=1), cos_ref[rows, :], -sin_ref[rows, :]
    ).astype(jnp.bfloat16)


def short_backward(line, qkv, facts, attn, grad, lse, cos_rows, sin_rows):
    rows = attn.shape[0]
    return line(
        "short_backward",
        short_backward_kernel,
        (qkv, facts, attn, grad, lse, cos_rows, sin_rows),
        [VMEM, SMEM] + [VMEM] * 5,
        [shaped((rows, 384))],
        [VMEM],
        [pltpu.VMEM((rows, HEAD_DIM), jnp.float32)] * 2,
    )[0]


def long_backward_kernel(q_ref, *refs):
    far_refs = refs[:4]
    facts_ref, attn_ref, grad_ref, lse_ref, cos_ref, sin_ref = refs[4:10]
    dq_ref, far_grad_ref, acc_ref = refs[10:]
    scale = HEAD_DIM**-0.5
    count = far_refs[0].shape[0]
    blocks = count // HALF
    queries = []
    for half in range(2):
        rows = pl.ds(half * HALF, HALF)
        grad = stacked(grad_ref[rows, :])
        column = lax.broadcasted_iota(jnp.int32, (1, HALF), 1)
        queries.append(
            (
                stacked(q_ref[rows, :256]) * jnp.bfloat16(scale),
                grad,
                lse_ref[half, :1],
                row_product(grad, stacked(attn_ref[rows, :])),
                jnp.concatenate([column + facts_ref[FIRST_PLACE + half] * HALF] * 4, axis=1),
            )
        )
    within = lax.broadcasted_iota(jnp.int32, (HALF, 1), 0)
    for i, far_ref in enumerate(far_refs):
        k, v = far_ref[:, :HEAD_DIM], far_ref[:, HEAD_DIM:]
        key = jnp.concatenate(
            [within + facts_ref[FAR_PLACE + i * blocks + n] * HALF for n in range(blocks)], axis=0
        )
        sums = []
        for half, (q, grad, lse, delta, position) in enumerate(queries):
            dq, dk, dv = grad_terms(q, grad, k, v, key <= position, lse, delta)
            acc_ref[half] = dq if i == 0 else acc_ref[half] + dq
            sums.append((dk, dv))
        total = jnp.concatenate(
            [sums[0][0] + sums[1][0], sums[0][1] + sums[1][1]], axis=1
        ).astype(jnp.bfloat16)
        rows = count // 4
        for n in range(4):
            far_grad_ref[n, pl.ds(i * rows, rows), :] = total[n * rows : (n + 1) * rows]
    for half in range(2):
        rows = pl.ds(half * HALF, HALF)
        dq_ref[rows, :] = turned(
            unstacked(acc_ref[half] * scale), cos_ref[rows, :], -sin_ref[rows, :]
        ).astype(jnp.bfloat16)


def long_backward(line, q, far, facts, attn, grad, lse, cos_rows, sin_rows):
    return line(
        "long_backward",
        long_backward_kernel,
        (q, *far, facts, attn, grad, lse, cos_rows, sin_rows),
        [VMEM] * 5 + [SMEM] + [VMEM] * 5,
        [shaped((2 * HALF, 256)), shaped((4, *far[0].shape))],
        [VMEM] * 2,
        [pltpu.VMEM((2, 4 * HALF, HEAD_DIM), jnp.float32)],
    )


def product_kernel(turned_right, left_ref, right_ref, out_ref):
    out_ref[...] = dot(left_ref[...], right_ref[...], 1, 1 if turned_right else 0).astype(
        out_ref.dtype
    )


def product(line, left, right, turned_right=False):
    rows, depth = left.shape
    width = right.shape[0] if turned_right else right.shape[1]
    block = rows // 2
    return line(
        "product",
        functools.partial(product_kernel, turned_right),
        (left, right),
        [rows_of(block, depth), once(right.shape)],
        [shaped((rows, width))],
        [rows_of(block, width)],
        grid=(2,),
    )[0]


def product_parts_kernel(terms, turned_right, *refs):
    outs = refs[2 * terms + 1 :]
    total = refs[2 * terms][...].astype(jnp.float32)
    for k in range(terms):
        total += dot(refs[2 * k][...], refs[2 * k + 1][...], 1, 1 if turned_right else 0)
    rows = outs[0].shape[0]
    for k, out_ref in enumerate(outs):
        out_ref[...] = total[k * rows : (k + 1) * rows].astype(jnp.bfloat16)


def product_parts(line, pairs, sent, turned_right=False):
    rows, width = sent.shape
    steps = 2 * len(pairs)
    block = width // steps
    specs = []
    for left, right in pairs:
        specs.append(once(left.shape))
        if turned_right:
            specs.append(rows_of(block, right.shape[1]))
        else:
            specs.append(columns_of(right.shape[0], block))
    return line(
        "product_parts",
        functools.partial(product_parts_kernel, len(pairs), turned_right),
        [array for pair in pairs for array in pair] + [sent],
        specs + [columns_of(rows, block)],
        [shaped((rows // 4, width))] * 4,
        [columns_of(rows // 4, block)] * 4,
        grid=(steps,),
    )


def merged(chunks):
    pieces = []
    for k in range(4):
        for (low, high), chunk in zip(CHUNKS, chunks):
            pieces.append(chunk[k * (high - low) : (k + 1) * (high - low)])
    return jnp.concatenate(pieces, axis=0)


def merged_product_kernel(count, with_sent, *refs):
    left = merged([ref[...] for ref in refs[:count]])
    total = dot(left, refs[count][...])
    outs = refs[count + 1 :]
    if with_sent:
        total += outs[0][...].astype(jnp.float32)
        outs = outs[1:]
    rows = outs[0].shape[0]
    for k, out_ref in enumerate(outs):
        out_ref[...] = total[k * rows : (k + 1) * rows].astype(jnp.bfloat16)


def merged_product(line, chunks, right, sent=None):
    rows = sum([chunk.shape[0] for chunk in chunks])
    depth, width = right.shape
    block = width // 2
    count = 1 if sent is None else 4
    extra = () if sent is None else (sent,)
    return line(
        "merged_product",
        functools.partial(merged_product_kernel, len(chunks), sent is not None),
        (*chunks, right, *extra),
        [once(chunk.shape) for chunk in chunks]
        + [columns_of(depth, block)]
        + [columns_of(rows, block)] * len(extra),
        [shaped((rows // count, width))] * count,
        [columns_of(rows // count, block)] * count,
        grid=(2,),
    )


def merged_back_kernel(count, *refs):
    left = merged([ref[...] for ref in refs[:count]])
    refs[-1][...] = dot(left, refs[count][...], 1, 1).astype(jnp.bfloat16)


def merged_back(line, chunks, right):
    rows = sum([chunk.shape[0] for chunk in chunks])
    return line(
        "merged_back",
        functools.partial(merged_back_kernel, len(chunks)),
        (*chunks, right),
        [VMEM] * (len(chunks) + 1),
        [shaped((rows, right.shape[0]))],
        [VMEM],
    )[0]


def arrange_kernel(facts_ref, rows_ref, *out_refs):
    del facts_ref
    for (low, high), out_ref in zip(CHUNKS, out_refs):
        out_ref[0] = rows_ref[0, low:high, :]


def arrange(line, rows, facts):
    _, count, d = rows.shape
    after = line.last

    def kernel(facts_ref, rows_ref, *refs):
        arrange_kernel(facts_ref, rows_ref, *refs[len(after) :])

    def source(i, facts_ref):
        core = jnp.where(i < 4, facts_ref[CORE_AT], 1 - facts_ref[CORE_AT])
        return core * 4 + (facts_ref[X_AT] + i) % 4, 0, 0

    results = pl.pallas_call(
        kernel,
        grid_spec=pltpu.PrefetchScalarGridSpec(
            num_scalar_prefetch=1,
            grid=(8,),
            in_specs=[pl.BlockSpec((1, count, d), source)] + [ANY] * len(after),
            out_specs=tuple(
                pl.BlockSpec((1, high - low, d), lambda i, facts_ref: (i, 0, 0))
                for low, high in CHUNKS
            ),
        ),
        out_shape=tuple(shaped((8, high - low, d)) for low, high in CHUNKS),
        compiler_params=PARAMS,
        cost_estimate=cost("arrange"),
        name="arrange",
    )(facts, rows, *after)
    return [array.reshape(-1, d) for array in results]


def weight_grad_kernel(count, beside, facts, *refs):
    facts_ref, *refs = refs if facts else (None, *refs)
    out_ref, width = refs[-1], refs[count].shape[1]
    total = dot(refs[0][...], refs[count][...], 0, 0)
    for k in range(1, count):
        total += dot(refs[k][...], refs[count + k][...], 0, 0)
    total = total.astype(jnp.bfloat16)
    if facts:
        rows = total.shape[0] // 2
        own_first = jnp.concatenate([total[rows:], total[:rows]])
        total = jnp.where(facts_ref[CORE_AT] == 0, total, own_first)
    out_ref[:, :width] = total
    if beside:
        out_ref[:, width:] = refs[2 * count][...]


def weight_grad(line, left, right, beside=(), facts=None):
    left = [piece if isinstance(piece, tuple) else (piece, 0) for piece in left]
    columns, width = left[0][0].shape[1], right[0].shape[1]
    whole = width + sum([array.shape[1] for array in beside])
    block = columns // 8

    def place(i, *facts_ref):
        if facts_ref:
            z = (i - facts_ref[0][Z_AT]) % 4
            yh = (i // 4 + facts_ref[0][YH_AT]) % 2
            return z * 2 + yh, 0
        return i % 4 * 2 + i // 4, 0

    def whole_block(i, *facts_ref):
        return 0, 0

    operands = (*[array for array, _ in left], *right, *beside)
    in_specs = (
        [
            pl.BlockSpec((part.shape[0], block), lambda i, *_, at=at: (at, i))
            for (_, at), part in zip(left, right)
        ]
        + [pl.BlockSpec(part.shape, whole_block, pipeline_mode=pl.Buffered(1)) for part in right]
        + [pl.BlockSpec((block, array.shape[1]), place) for array in beside]
    )
    out_spec = pl.BlockSpec((block, whole), place)
    kernel = functools.partial(weight_grad_kernel, len(left), len(beside), facts is not None)
    if facts is None:
        return line(
            "weight_grad",
            kernel,
            operands,
            in_specs,
            [shaped((columns, whole))],
            [out_spec],
            grid=(8,),
        )[0]
    after, count = line.last, len(operands) + 1

    def ordered(*refs):
        kernel(*refs[:count], *refs[count + len(after) :])

    result = pl.pallas_call(
        ordered,
        grid_spec=pltpu.PrefetchScalarGridSpec(
            num_scalar_prefetch=1,
            grid=(8,),
            in_specs=in_specs + [ANY] * len(after),
            out_specs=out_spec,
        ),
        out_shape=shaped((columns, whole)),
        compiler_params=PARAMS,
        cost_estimate=cost("weight_grad"),
        name="weight_grad",
    )(facts, *operands, *after)
    line.last = (result,)
    return result


def mix_kernel(low, high, tokens_ref, gain_ref, *refs):
    parts, (mixed_ref, hidden_ref) = refs[:4], refs[4:]
    mixed = tokens_ref[low:high, :].astype(jnp.float32) + total_of([ref[...] for ref in parts])
    inv = lax.rsqrt(jnp.mean(mixed * mixed, axis=-1, keepdims=True) + EPS)
    mixed_ref[...] = mixed
    hidden_ref[...] = (mixed * inv * gain_ref[...]).astype(jnp.bfloat16)


def mix(line, chunk, tokens, gain, parts):
    low, high = chunk
    d = tokens.shape[1]
    return line(
        "mix",
        functools.partial(mix_kernel, low, high),
        (tokens, gain, *parts),
        [VMEM] * 6,
        [shaped((high - low, d), jnp.float32), shaped((high - low, d))],
        [VMEM] * 2,
    )


def norm_back(grad_in, values, gain):
    inv = lax.rsqrt(jnp.mean(values * values, axis=-1, keepdims=True) + EPS)
    unit = values * inv
    scaled = grad_in * gain
    return inv * (scaled - unit * jnp.mean(scaled * unit, axis=-1, keepdims=True)), unit


def mix_back_kernel(low, high, grad_ref, mixed_ref, gain_ref, *refs):
    parts, (total_ref, low_ref, part_ref) = refs[:4], refs[4:]
    grad_in = total_of([ref[...] for ref in parts])
    back, unit = norm_back(grad_in, mixed_ref[...], gain_ref[...])
    total = grad_ref[low:high, :].astype(jnp.float32) + back
    total_ref[...] = total
    low_ref[...] = total.astype(jnp.bfloat16)
    part_ref[...] = jnp.sum(grad_in * unit, axis=0, keepdims=True)


def mix_back(line, chunk, grad, mixed, gain, parts):
    low, high = chunk
    rows, d = mixed.shape
    return line(
        "mix_back",
        functools.partial(mix_back_kernel, low, high),
        (grad, mixed, gain, *parts),
        [VMEM] * 7,
        [shaped((rows, d), jnp.float32), shaped((rows, d)), shaped((1, d), jnp.float32)],
        [VMEM] * 3,
    )


def mlp_kernel(hidden_ref, grad_act_ref, gate_ref, up_ref, act_ref, gate_out_ref, up_out_ref, *refs):
    hidden = hidden_ref[...]
    gate = dot(hidden, gate_ref[...])
    up = dot(hidden, up_ref[...])
    grad_act = grad_act_ref[...].astype(jnp.float32)
    sig = jax.nn.sigmoid(gate)
    silu = gate * sig
    act_ref[...] = (silu * up).astype(jnp.bfloat16)
    grad_gate = (grad_act * up * sig * (1.0 + gate * (1.0 - sig))).astype(jnp.bfloat16)
    grad_up = (grad_act * silu).astype(jnp.bfloat16)
    gate_out_ref[...] = grad_gate
    up_out_ref[...] = grad_up
    if refs:
        refs[0][...] = (
            dot(grad_gate, gate_ref[...], 1, 1) + dot(grad_up, up_ref[...], 1, 1)
        ).astype(jnp.bfloat16)


def mlp(line, hidden, grad_act, at, w_gate, w_up, with_back):
    rows, d = hidden.shape
    width = w_gate.shape[1]
    if with_back:
        block = rows // 2
        specs = [
            rows_of(block, d),
            pl.BlockSpec((block, width), lambda i: (2 * at + i, 0)),
            once((d, width)),
            once((d, width)),
        ]
        out_specs = [rows_of(block, width)] * 3 + [rows_of(block, d)]
    else:
        block = width // 4
        specs = [
            once((rows, d)),
            pl.BlockSpec((rows, block), lambda i: (at, i)),
            columns_of(d, block),
            columns_of(d, block),
        ]
        out_specs = [columns_of(rows, block)] * 3
    return line(
        "mlp",
        mlp_kernel,
        (hidden, grad_act, w_gate, w_up),
        specs,
        [shaped((rows, width))] * 3 + [shaped((rows, d))] * with_back,
        out_specs,
        grid=(2 if with_back else 4,),
    )


def hidden_grad_kernel(with_sent, low_ref, query_ref, kv_ref, hidden_ref, *refs):
    low = low_ref[...]
    grad = dot(low[:, :256], query_ref[...], 1, 1) + dot(low[:, 256:], kv_ref[...], 1, 1)
    gain = jnp.sum(grad * hidden_ref[...].astype(jnp.float32), axis=0, keepdims=True)
    if not with_sent:
        refs[0][...] = grad.astype(jnp.bfloat16)
        refs[1][...] = gain
        return
    sent_ref, gain_ref, mlp_gain_ref, *outs = refs
    grad += sent_ref[...].astype(jnp.float32)
    rows = outs[0].shape[0] - 8
    tail = []
    for values in (gain + gain_ref[...], mlp_gain_ref[...]):
        high = values.astype(jnp.bfloat16)
        tail += [high, (values - high.astype(jnp.float32)).astype(jnp.bfloat16)]
    tail = jnp.concatenate(tail + [jnp.zeros_like(tail[0])] * 4, axis=0)
    for k, out_ref in enumerate(outs):
        part = grad[k * rows : (k + 1) * rows].astype(jnp.bfloat16)
        out_ref[...] = jnp.concatenate([part, tail], axis=0)


def hidden_grad(line, low, w_query, w_key_value, hidden, sent=()):
    rows, d = hidden.shape
    block = d // 2
    if sent:
        outs = [shaped((rows // 4 + 8, d))] * 4
        out_specs = [columns_of(rows // 4 + 8, block)] * 4
    else:
        outs = [shaped((rows, d)), shaped((1, d), jnp.float32)]
        out_specs = [columns_of(rows, block), columns_of(1, block)]
    return line(
        "hidden_grad",
        functools.partial(hidden_grad_kernel, bool(sent)),
        (low, w_query, w_key_value, hidden, *sent),
        [once((rows, 384)), rows_of(block, 256), rows_of(block, 128), columns_of(rows, block)]
        + [columns_of(array.shape[0], block) for array in sent],
        outs,
        out_specs,
        grid=(2,),
    )


def gate_kernel(*refs):
    del refs


def gated(line, arrays):
    line.last = tuple([array for array in line.last if all([array is not one for one in arrays])])
    return line(
        "gated",
        gate_kernel,
        arrays,
        [ANY] * len(arrays),
        [shaped(array.shape, array.dtype) for array in arrays],
        [ANY] * len(arrays),
        input_output_aliases={k: k for k in range(len(arrays))},
    )


def out_mix_kernel(*refs):
    mixed = jnp.concatenate([ref[...] for ref in refs[:-5]], axis=0)
    refs[-1][...] = (mixed + total_of([ref[...] for ref in refs[-5:-1]])).astype(jnp.bfloat16)


def final_kernel(tokens_ref, gain_ref, *refs):
    out_ref, gains_ref = refs[-2:]
    total = total_of([ref[...] for ref in refs[-6:-2]])
    rows = out_ref.shape[0]
    back, _ = norm_back(total[:rows], tokens_ref[...].astype(jnp.float32), gain_ref[...])
    mixed = jnp.concatenate([ref[...] for ref in refs[:-6]], axis=0)
    out_ref[...] = (mixed + back).astype(jnp.bfloat16)
    sums = total[rows : rows + 8]
    gains_ref[...] = jnp.concatenate([sums[:1] + sums[1:2], sums[2:3] + sums[3:4]], axis=0)


def turn_far_kernel(grad_ref, cos_ref, sin_ref, long_ref, short_ref, out_ref):
    rows = pl.ds(0, 2 * HALF)
    out_ref[rows, :256] = long_ref[...]
    out_ref[rows, 256:] = turned_key(grad_ref[...], cos_ref[rows, :], -sin_ref[rows, :]).astype(
        jnp.bfloat16
    )
    out_ref[pl.ds(2 * HALF, short_ref.shape[0]), :] = short_ref[...]


def local(
    tokens,
    lengths,
    place,
    attn_gain,
    w_query,
    w_key,
    w_value,
    w_out,
    mlp_gain,
    w_gate,
    w_up,
    w_down,
    out_grad,
):
    rows, d = tokens.shape
    group_rows = rows * 8
    half_rows = rows * 4
    long_rows = 2 * HALF
    dp_index, mp_index = lax.axis_index("dp"), lax.axis_index("mp")
    yh, z, core = dp_index // 8, dp_index // 2 % 4, dp_index % 2
    yl, x = mp_index // 4, mp_index % 4
    native = core == yl
    line = Line()
    mlp_gain_row = mlp_gain.reshape(1, d)

    tokens = send(tokens, TURN)
    lengths = send(lengths, TURN)[0]
    w_key_value = send(jnp.concatenate([w_key, w_value], axis=1), WEIGHT_LOW)
    w_query = send(w_query, WEIGHT_LOW)
    w_out = send(w_out, WEIGHT_LOW)
    w_down = send(w_down, WEIGHT_HIGH)
    w_gate = send(w_gate, WEIGHT_LOW)
    w_up = send(w_up, WEIGHT_HIGH)
    out_grad = turn(out_grad, native)

    step = jnp.arange(16, dtype=jnp.int32)
    far_yh = jnp.where(step % 4 >= 2, 1 - yh, yh)
    far_yl = jnp.where((step % 4 == 1) | (step % 4 == 2), 1 - yl, yl)
    far_group = (far_yh * 4 + (z + step // 4) % 4) * 2 + far_yl
    far_index = (2 * far_group[:, None] + jnp.arange(2, dtype=jnp.int32)[None, :]).reshape(-1)
    half_ids = jnp.arange(place.shape[0], dtype=jnp.int32)
    far_place = jnp.sum(jnp.where(far_index[:, None] == half_ids[None, :], place, 0), axis=1)
    facts = jnp.concatenate(
        [
            far_place[:2],
            jnp.stack([lengths[0], lengths[0] + lengths[1], core, x, z, yh]),
            far_place,
        ]
    ).astype(jnp.int32)

    residual = tokens.astype(jnp.float32)
    inv_one = lax.rsqrt(jnp.mean(residual * residual, axis=-1, keepdims=True) + EPS)
    hidden_one = collect((residual * inv_one * attn_gain).astype(jnp.bfloat16))
    freq = jnp.tile(inverse_freq(HEAD_DIM), 4).reshape(1, 128)
    line.last += (w_query, w_key_value)
    cos_gathered, sin_gathered, cos_ordered, sin_ordered = line(
        "tables",
        functools.partial(tables_kernel, rows),
        (facts, freq),
        [SMEM, VMEM],
        [shaped((n, 128), jnp.float32) for n in (group_rows,) * 4],
        [VMEM] * 4,
    )
    hidden_own = join(line, hidden_one)
    hidden_one = (hidden_own, send(hidden_own, CORE))
    qkv = []
    for at, half in enumerate(hidden_one):
        line.last += (w_down,) * at
        qkv.append(
            project_qkv(line, half, w_query, w_key_value, cos_gathered, sin_gathered, at)
        )
    (out_grad,) = gated(line, (out_grad,))
    grad_rows = lax.all_gather(out_grad, BOTH, axis=0, axis_index_groups=CHIP_GROUPS)
    qkv = in_order(jnp.stack(qkv), core, x)
    near_rows = qkv[:long_rows, 256:]
    ring_rows = jnp.concatenate(
        [near_rows, send(near_rows, Y_LOW), send(near_rows, Y_HIGH), send(near_rows, Y_FAR)]
    )
    far_rows = (
        ring_rows, send(ring_rows, Z_DOWN), send(ring_rows, Z_FAR), send(ring_rows, Z_UP)
    )
    line.last += (ring_rows,)
    short_attn, short_lse = short_forward(line, qkv, facts)
    attn_ordered, long_lse = long_forward(line, qkv, far_rows, facts, short_attn, group_rows)
    attn_rows = from_order(attn_ordered, core, x)
    attn_rows = [chunks_of(attn_rows[half]) for half in range(2)]

    sent = [send(product(line, part, w_out), CORE) for part in attn_rows[1]]
    mixed_parts = [
        scatter(product_parts(line, [(part, w_out)], other))
        for part, other in zip(attn_rows[0], sent)
    ]
    grad_rows = arrange(line, grad_rows, facts)
    grad_act = [product(line, part, w_down, True) for part in grad_rows]
    mixed, hidden_two = [], []
    for chunk, parts in zip(CHUNKS, mixed_parts):
        mixed_rows, hidden_rows = mix(line, chunk, tokens, mlp_gain_row, parts)
        mixed.append(mixed_rows)
        hidden_two.append(collect(hidden_rows))

    count = len(CHUNKS)
    own, other, act, gate, up, back = ([None] * count for _ in range(6))

    def first_half(n):
        own[n] = join(line, hidden_two[n])
        other[n] = send(own[n], CORE)
        act[n], gate[n], up[n] = mlp(line, own[n], grad_act[n], 0, w_gate, w_up, False)

    def second_half(n):
        *terms, sum_back = mlp(line, other[n], grad_act[n], 1, w_gate, w_up, True)
        act[n], gate[n], up[n] = zip((act[n], gate[n], up[n]), terms)
        back[n] = send(sum_back, CORE)

    hidden_parts = []
    first_half(0)
    second_half(0)
    for n in range(count):
        if n + 1 < count:
            first_half(n + 1)
        if n + 1 == count:
            (down_rows,) = merged_product(line, [part[1] for part in act], w_down)
            down_rows = send(down_rows, CORE)
        terms = [(gate[n][0], w_gate), (up[n][0], w_up)]
        hidden_parts.append(scatter(product_parts(line, terms, back[n], True)))
        if n + 1 < count:
            second_half(n + 1)
    act, gate, up = [[pair[k] for pair in part for k in range(2)] for part in (act, gate, up)]
    hidden_two = [piece for pair in zip(own, other) for piece in pair]

    pieces = [(part, at) for part in grad_rows for at in range(2)]
    both_part = weight_grad(line, hidden_two, up, (weight_grad(line, hidden_two, gate),))
    grad_mixed, mixed_grad, gain_parts = [], [], []
    for n, (chunk, parts) in enumerate(zip(CHUNKS, hidden_parts)):
        total, low, gain_part = mix_back(line, chunk, out_grad, mixed[n], mlp_gain_row, parts)
        grad_mixed.append(total)
        mixed_grad.append(collect(low))
        gain_parts.append(gain_part)
    both_kept = reduce_near(gated(line, (both_part,))[0])
    down_part = weight_grad(line, pieces, act)
    out_parts = scatter(merged_product(line, act[0::2], w_down, down_rows))

    grad_own = [join(line, parts) for parts in mixed_grad]
    grad_other = [send(part, CORE) for part in grad_own]
    grad_attn = jnp.stack([merged_back(line, part, w_out) for part in (grad_own, grad_other)])
    grad_attn = in_order(grad_attn, core, x)
    long_dq, far_terms = long_backward(
        line,
        qkv,
        far_rows,
        facts,
        attn_ordered,
        grad_attn,
        long_lse,
        cos_ordered,
        sin_ordered,
    )
    ring_terms = total_of(
        (
            far_terms[0],
            send(far_terms[1], Y_LOW),
            send(far_terms[2], Y_HIGH),
            send(far_terms[3], Y_FAR),
        )
    ).astype(jnp.bfloat16)
    near = ring_terms.reshape(4, long_rows, -1)
    far_grads = total_of(
        (near[0], send(near[1], Z_UP), send(near[2], Z_FAR), send(near[3], Z_DOWN))
    )
    line.last += out_parts[1:]
    short_low = short_backward(
        line, qkv, facts, short_attn, grad_attn, short_lse, cos_ordered, sin_ordered
    )
    out_part = weight_grad(
        line,
        [piece for pair in zip(grad_own, grad_other) for piece in pair],
        [piece for pair in zip(*attn_rows) for piece in pair],
        (),
        facts,
    )
    (low_ordered,) = line(
        "turn_far",
        turn_far_kernel,
        (far_grads, cos_ordered, sin_ordered, long_dq, short_low),
        [VMEM] * 5,
        [shaped((group_rows, 384))],
        [VMEM],
    )
    low_rows = from_order(low_ordered, core, x)
    line.last += (both_kept,)
    down_kept = reduce_near(gated(line, (down_part,))[0])
    back, gain_other = hidden_grad(line, low_rows[1], w_query, w_key_value, hidden_one[1])
    back = send(back, CORE)
    last_part = weight_grad(line, hidden_one, (low_rows[0], low_rows[1]), (out_part,), facts)
    grad_parts = scatter(
        hidden_grad(
            line,
            low_rows[0],
            w_query,
            w_key_value,
            hidden_one[0],
            (back, gain_other, sum(gain_parts[1:], gain_parts[0])),
        )[:4]
    )
    last_kept, first_hop = reduce_ring(gated(line, (last_part,))[0])
    (output,) = line(
        "out_mix",
        out_mix_kernel,
        (*mixed, *out_parts),
        [VMEM] * (len(mixed) + 4),
        [shaped((rows, d))],
        [VMEM],
    )
    output = turn(output, native)
    line.last += first_hop
    grad_tokens, gains = line(
        "final",
        final_kernel,
        (tokens, attn_gain.reshape(1, d), *grad_mixed, *grad_parts),
        [VMEM] * (2 + len(grad_mixed) + 4),
        [shaped((rows, d)), shaped((2, d), jnp.float32)],
        [VMEM] * 2,
    )
    both_kept, down_kept = gated(line, (both_kept, down_kept))
    ff_sum = reduce_y(jnp.concatenate([both_kept, down_kept], axis=1), native)
    grad_tokens = turn(grad_tokens, native)
    gains = all_sum(gains)
    last_sum = sum_groups(last_kept, native)
    ff = w_gate.shape[1]
    return (
        output,
        grad_tokens,
        gains[0] / attn_gain,
        last_sum[:, :256],
        last_sum[:, 256:320],
        last_sum[:, 320:384],
        last_sum[:, 384:].T,
        gains[1],
        ff_sum[:, ff : 2 * ff],
        ff_sum[:, :ff],
        ff_sum[:, 2 * ff :].T,
    )


def solution(mesh):
    placed = (
        P(("dp", "mp"), None),
        P("dp", None),
        P(),
        P(),
        P(None, "mp"),
        P(None, "mp"),
        P(None, "mp"),
        P("mp", None),
        P(),
        P(None, "mp"),
        P(None, "mp"),
        P("mp", None),
        P(("dp", "mp"), None),
    )
    return jax.shard_map(
        local,
        mesh=mesh,
        in_specs=placed,
        out_specs=(
            P(("dp", "mp"), None),
            P(("dp", "mp"), None),
            P(),
            P("dp", "mp"),
            P("dp", "mp"),
            P("dp", "mp"),
            P("mp", "dp"),
            P(),
            P("dp", "mp"),
            P("dp", "mp"),
            P("mp", "dp"),
        ),
        check_vma=False,
    )
```
